32 devices in a mesh: ctx: 4 (over z), fsdp: 8 (over y, x, core).
Axes of the slice: x: 2, y: 2, z: 4, core: 2. Of those that a mesh axis runs over, the one named last changes fastest.
Arguments:
- tokens: bfloat16 [8, 512, 2048], P('fsdp', 'ctx'), may hold values from -6 to 6
- block_pairs: int32 [8, 4], P('fsdp'), may hold values from 0 to 3, each once within a row
- w_query: bfloat16 [2048, 2048], P('fsdp'), may hold values from -0.125 to 0.125
- w_key: bfloat16 [2048, 2048], P('fsdp'), may hold values from -0.125 to 0.125
- w_value: bfloat16 [2048, 2048], P('fsdp'), may hold values from -0.125 to 0.125
- w_out: bfloat16 [2048, 2048], P('fsdp'), may hold values from -0.125 to 0.125
- w_gate: bfloat16 [2048, 8192], P('fsdp'), may hold values from -0.125 to 0.125
- w_up: bfloat16 [2048, 8192], P('fsdp'), may hold values from -0.125 to 0.125
- w_down: bfloat16 [8192, 2048], P('fsdp'), may hold values from -0.0625 to 0.0625
- gain_query: float32 [2048], replicated, may hold values from 0.25 to 1.75
- gain_key: float32 [2048], replicated, may hold values from 0.25 to 1.75
- gain_attn: float32 [2048], replicated, may hold values from 0.25 to 1.75
- gain_mlp: float32 [2048], replicated, may hold values from 0.25 to 1.75
- cotangent: bfloat16 [8, 512, 2048], P('fsdp', 'ctx'), may hold values from -6 to 6
Outputs:
- output: bfloat16 [8, 512, 2048], P('fsdp', 'ctx')
- d_tokens: bfloat16 [8, 512, 2048], P('fsdp', 'ctx')
- grad_w_query: float32 [2048, 2048], P(('ctx', 'fsdp'))
- grad_w_key: float32 [2048, 2048], P(('ctx', 'fsdp'))
- grad_w_value: float32 [2048, 2048], P(('ctx', 'fsdp'))
- grad_w_out: float32 [2048, 2048], P(('ctx', 'fsdp'))
- grad_w_gate: float32 [2048, 8192], P(('ctx', 'fsdp'))
- grad_w_up: float32 [2048, 8192], P(('ctx', 'fsdp'))
- grad_w_down: float32 [8192, 2048], P(('ctx', 'fsdp'))
- grad_gain_query: float32 [2048], P(('ctx', 'fsdp'))
- grad_gain_key: float32 [2048], P(('ctx', 'fsdp'))
- grad_gain_attn: float32 [2048], P(('ctx', 'fsdp'))
- grad_gain_mlp: float32 [2048], P(('ctx', 'fsdp'))
The draws below stay inside these ranges and needn't reach their ends.
Inputs may be any that keep to these rules, and one draw needn't show every extreme that they name: Each row of block_pairs names every number from 0 to 3 once.
All inputs are finite; a program needn't handle non-finite values.
Results may differ from the reference program's by a relative error of at most 0.019.
Values may be sent and summed in bfloat16 or wider, within the bound.
A program may use at most 704 MiB of HBM per device.

```python
import jax
import jax.numpy as jnp
from jax import lax

D = 2048
HEADS = 16
HD = 128
FF = 8192
BLK = 64
SEQ = 512
SEQS = 8
N_CTX = 4


def strengthened(array, own_key, source, target, shards_of, factor):
    def block_of(position):
        return (jnp.arange(array.shape[position]) // (array.shape[position] // shards_of)).reshape((-1,) + (1,) * (array.ndim - 1 - position))

    one_side = jax.random.permutation(own_key, shards_of)[block_of(target)]
    other_side = (block_of(target) + shards_of // 2) % shards_of
    return jnp.where((block_of(source) == one_side) | (block_of(source) == other_side), factor * array, array)


def shard_levels(own_key, shape, cuts, smallest, top_value):
    def one(dim, parts):
        draws = jax.random.uniform(jax.random.fold_in(jax.random.fold_in(own_key, 6), dim), (parts,), jnp.float32, smallest / len(cuts), top_value / len(cuts))
        return jnp.repeat(jnp.exp(draws), shape[dim] // parts).reshape((-1,) + (1,) * (len(shape) - dim - 1))

    gain = one(*cuts[0])
    for cut in cuts[1:]:
        gain = gain * one(*cut)
    return gain


def centred(stream_key, extent, width, limit, shards=(), held_as=jnp.bfloat16):
    entries = jax.random.normal(stream_key, extent, jnp.float32) * width
    if len(shards) > 0:
        entries = shard_levels(stream_key, extent, shards, -0.22, 0.18) * entries
    return jnp.clip(entries, min=-limit, max=limit).astype(held_as)


def noise_with(key, dims, deviation, most, cuts, heavy, kind=jnp.bfloat16):
    drawn = deviation * jax.random.normal(key, dims, jnp.float32)
    if cuts:
        drawn = drawn * shard_levels(key, dims, cuts, -0.22, 0.18)
    return jnp.clip(strengthened(drawn, jax.random.fold_in(key, 3), *heavy), -most, most).astype(kind)


def setup_inputs(seed: int = 0) -> dict:
    streams_of = jax.random.split(jax.random.key(seed), 15)
    tokens = centred(streams_of[0], (SEQS, SEQ, D), 1.0, 6.0, ((0, 8), (1, 4)))
    block_pairs = jax.vmap(lambda own: jax.random.permutation(own, N_CTX))(jax.random.split(streams_of[1], SEQS)).reshape((SEQS, N_CTX)).astype(jnp.int32)
    w_query = centred(streams_of[2], (D, D), D ** -0.5, 0.125, ((0, 8),))
    w_key = centred(streams_of[3], (D, D), D ** -0.5, 0.125, ((0, 8),))
    w_value = centred(streams_of[4], (D, D), D ** -0.5, 0.125, ((0, 8),))
    w_out = centred(streams_of[5], (D, D), D ** -0.5, 0.125, ((0, 8),))
    w_gate = centred(streams_of[6], (D, FF), D ** -0.5, 0.125, ((0, 8),))
    w_up = centred(streams_of[7], (D, FF), D ** -0.5, 0.125, ((0, 8),))
    w_down = centred(streams_of[8], (FF, D), FF ** -0.5, 0.0625, ((0, 8),))
    gain_query = jnp.clip(1.0 + 0.15 * jax.random.normal(streams_of[9], (D,), jnp.float32), 0.25, 1.75)
    gain_key = jnp.clip(1.0 + 0.15 * jax.random.normal(streams_of[10], (D,), jnp.float32), 0.25, 1.75)
    gain_attn = jnp.clip(1.0 + 0.15 * jax.random.normal(streams_of[11], (D,), jnp.float32), 0.25, 1.75)
    gain_mlp = jnp.clip(1.0 + 0.15 * jax.random.normal(streams_of[12], (D,), jnp.float32), 0.25, 1.75)
    cotangent = noise_with(streams_of[13], (SEQS, SEQ, D), 1.0, 6.0, ((0, 8), (1, 4)), (1, 2, 4, 2.0))
    return {"tokens": tokens, "block_pairs": block_pairs, "w_query": w_query, "w_key": w_key, "w_value": w_value, "w_out": w_out, "w_gate": w_gate, "w_up": w_up, "w_down": w_down, "gain_query": gain_query, "gain_key": gain_key, "gain_attn": gain_attn, "gain_mlp": gain_mlp, "cotangent": cotangent}


EPSILON = 1e-06
ROPE_BASE = 500000.0
NEGATIVE = -1e+30

@jax.custom_vjp
def low(v):
    return lax.optimization_barrier(v.astype(jnp.bfloat16)).astype(jnp.float32)

@jax.custom_vjp
def low_back(v):
    return v

def low_keep(v):
    return (low(v), None)

def low_pass(kept, grad):
    return (grad,)

def back_keep(v):
    return (v, None)

def back_low(kept, grad):
    return (low(grad),)
low.defvjp(low_keep, low_pass)
low_back.defvjp(back_keep, back_low)

def norm_scale(values, gain_vec):
    return values * lax.rsqrt(lax.optimization_barrier(jnp.mean(values * values, axis=-1, keepdims=True)) + EPSILON) * gain_vec

def turn_half(values, cosine, sine):
    half_size = values.shape[-1] // 2
    turned = jnp.concatenate([-values[..., half_size:], values[..., :half_size]], axis=-1)
    return values * cosine + turned * sine

def angle_tables(positions, head_size):
    half_size = head_size // 2
    frequency = jnp.power(ROPE_BASE, -(jnp.arange(half_size).astype(jnp.float32) * 2.0 / head_size))
    angles = positions.astype(jnp.float32)[:, None] * frequency[None, :]
    angles = jnp.concatenate([angles, angles], axis=-1)
    return (jnp.cos(angles)[:, None, :], jnp.sin(angles)[:, None, :])

def row_positions(row_ids, pair_row, block_rows, ctx_count):
    rank_of = row_ids // (2 * block_rows)
    second = row_ids // block_rows % 2
    offset = row_ids % block_rows
    rank_match = (rank_of[:, None] == jnp.arange(ctx_count, dtype=jnp.int32)[None, :]).astype(jnp.int32)
    chosen = lax.optimization_barrier(jnp.sum(rank_match * pair_row[None, :], axis=1))
    block_index = jnp.where(second == 0, chosen, 2 * ctx_count - 1 - chosen)
    return (block_index * block_rows + offset).astype(jnp.int32)

def matmul_high(left, right):
    return jnp.dot(left, right, precision=lax.Precision.HIGHEST, preferred_element_type=jnp.float32)

def block_layer(token_rows, pair_row, q_weight, k_weight, v_weight, o_weight, g_weight, u_weight, d_weight, gain_q, gain_k, gain_a, gain_m):
    positions = row_positions(jnp.arange(SEQ, dtype=jnp.int32), pair_row, BLK, N_CTX)
    cosine, sine = angle_tables(positions, HD)
    q_raw = low_back(matmul_high(token_rows, q_weight))
    k_raw = low_back(matmul_high(token_rows, k_weight))
    v_raw = low_back(matmul_high(token_rows, v_weight))
    queries = low(turn_half(norm_scale(q_raw, gain_q).reshape(SEQ, HEADS, HD), cosine, sine))
    key_all = low(turn_half(norm_scale(k_raw, gain_k).reshape(SEQ, HEADS, HD), cosine, sine))
    value_all = low(v_raw).reshape(SEQ, HEADS, HD)
    q_width = min(512, SEQ)
    q_blocks = queries.reshape(SEQ // q_width, q_width, HEADS, HD)
    pos_blocks = positions.reshape(SEQ // q_width, q_width)

    def attend(pieces):
        block_q, block_pos = pieces
        scores = jnp.einsum('qhd,khd->hqk', block_q, key_all, precision=lax.Precision.HIGHEST) * HD ** (-0.5)
        scores = low_back(scores)
        scores = jnp.where(positions[None, None, :] <= block_pos[None, :, None], scores, NEGATIVE)
        prob_low = low(jax.nn.softmax(scores, axis=-1))
        return jnp.einsum('hqk,khd->qhd', prob_low, value_all, precision=lax.Precision.HIGHEST)
    attended = lax.map(jax.checkpoint(attend), (q_blocks, pos_blocks)).reshape(SEQ, D)
    attended = low(low_back(attended))
    branch = low_back(matmul_high(attended, o_weight))
    mid_stream = token_rows + norm_scale(branch, gain_a)
    mid_low = low(mid_stream)
    gate_act = low_back(matmul_high(mid_low, g_weight))
    up_act = low_back(matmul_high(mid_low, u_weight))
    hidden = low(jax.nn.silu(gate_act) * up_act)
    mlp_out = low_back(matmul_high(hidden, d_weight))
    return mid_stream + norm_scale(mlp_out, gain_m)

def reference(tokens, block_pairs, w_query, w_key, w_value, w_out, w_gate, w_up, w_down, gain_query, gain_key, gain_attn, gain_mlp, cotangent):
    floats = [a.astype(jnp.float32) for a in (tokens, w_query, w_key, w_value, w_out, w_gate, w_up, w_down, gain_query, gain_key, gain_attn, gain_mlp)]

    def forward(x_all, q_weight, k_weight, v_weight, o_weight, g_weight, u_weight, d_weight, gain_q, gain_k, gain_a, gain_m):

        def seq_step(scan_state, pieces):
            result = block_layer(pieces[0], pieces[1], q_weight, k_weight, v_weight, o_weight, g_weight, u_weight, d_weight, gain_q, gain_k, gain_a, gain_m)
            return (scan_state, result)
        return lax.scan(seq_step, jnp.zeros((), jnp.float32), (x_all, block_pairs))[1]
    result, pull_back = jax.vjp(forward, *floats)
    gradients = pull_back(cotangent.astype(jnp.float32))
    return (result.astype(jnp.bfloat16), gradients[0].astype(jnp.bfloat16), gradients[1], gradients[2], gradients[3], gradients[4], gradients[5], gradients[6], gradients[7], gradients[8], gradients[9], gradients[10], gradients[11])
```

```python
import jax
import jax.numpy as jnp
from jax import lax
from jax.sharding import PartitionSpec as P

HD = 128


EPSILON = 1e-06
ROPE_BASE = 500000.0
NEGATIVE = -1e30


def norm_scale(values, gain_vec):
    return (
        values * lax.rsqrt(jnp.mean(values * values, axis=-1, keepdims=True) + EPSILON) * gain_vec
    )


def turn_half(values, cosine, sine):
    half_size = values.shape[-1] // 2
    turned = jnp.concatenate([-values[..., half_size:], values[..., :half_size]], axis=-1)
    return values * cosine + turned * sine


def angle_tables(positions, head_size):
    half_size = head_size // 2
    frequency = jnp.power(ROPE_BASE, -(jnp.arange(half_size).astype(jnp.float32) * 2.0 / head_size))
    angles = positions.astype(jnp.float32)[:, None] * frequency[None, :]
    angles = jnp.concatenate([angles, angles], axis=-1)
    return (jnp.cos(angles)[:, None, :], jnp.sin(angles)[:, None, :])


def row_positions(row_ids, pair_row, block_rows, ctx_count):
    rank_of = row_ids // (2 * block_rows)
    second = row_ids // block_rows % 2
    offset = row_ids % block_rows
    rank_match = (rank_of[:, None] == jnp.arange(ctx_count, dtype=jnp.int32)[None, :]).astype(
        jnp.int32
    )
    chosen = jnp.sum(rank_match * pair_row[None, :], axis=1)
    block_index = jnp.where(second == 0, chosen, 2 * ctx_count - 1 - chosen)
    return block_index * block_rows + offset


def times_transpose(left, right):
    return lax.dot_general(
        left, right, (((1,), (1,)), ((), ())), preferred_element_type=jnp.float32
    )


def transpose_times(left, right):
    return lax.dot_general(
        left, right, (((0,), (0,)), ((), ())), preferred_element_type=jnp.float32
    )


def activate(gate_in, up_in):
    return jax.nn.silu(gate_in) * up_in


def spread_rows(values, outer, inner):
    rows, width = values.shape
    return (
        values.reshape(outer, inner, rows // (outer * inner), width)
        .transpose(1, 0, 2, 3)
        .reshape(rows, width)
    )


def shards(
    tokens,
    block_pairs,
    w_query,
    w_key,
    w_value,
    w_out,
    w_gate,
    w_up,
    w_down,
    gain_query,
    gain_key,
    gain_attn,
    gain_mlp,
    cotangent,
):
    bf16 = jnp.bfloat16
    f32 = jnp.float32
    local_rows = tokens.shape[1]
    block_rows = local_rows // 2
    width = w_query.shape[1]
    hidden_width = w_gate.shape[1]
    ctx_count = lax.axis_size("ctx")
    fsdp_count = lax.axis_size("fsdp")
    ctx_index = lax.axis_index("ctx")
    seq = local_rows * ctx_count
    cols = width // ctx_count
    heads = cols // HD
    strip = hidden_width // (ctx_count * fsdp_count)
    hid = strip * fsdp_count
    scale = HD ** (-0.5)

    def ctx_cols(w):
        return lax.dynamic_slice_in_dim(w, ctx_index * cols, cols, 1)

    def ctx_strips(w):
        parts = w.reshape(w.shape[0], fsdp_count, ctx_count, strip)
        return lax.dynamic_index_in_dim(parts, ctx_index, 2, keepdims=False).reshape(w.shape[0], hid)

    token_rows = tokens[0]
    x_all = lax.all_gather(token_rows, "ctx", axis=0, tiled=True)
    qkv_w = lax.all_gather(
        jnp.concatenate([ctx_cols(w_query), ctx_cols(w_key), ctx_cols(w_value)], axis=1),
        "fsdp", axis=0, tiled=True,
    )
    out_w = lax.dynamic_slice_in_dim(
        lax.all_gather(w_out, "fsdp", axis=0, tiled=True), ctx_index * cols, cols, 0
    )
    gate_w = lax.all_gather(ctx_strips(w_gate), "fsdp", axis=0, tiled=True)
    up_w = lax.all_gather(ctx_strips(w_up), "fsdp", axis=0, tiled=True)
    down_w = lax.all_gather(
        lax.dynamic_slice_in_dim(w_down, ctx_index * strip, strip, 0), "fsdp", axis=0, tiled=True
    )

    pos = row_positions(jnp.arange(seq, dtype=jnp.int32), block_pairs[0], block_rows, ctx_count)
    cosine, sine = angle_tables(pos, HD)
    mask = pos[None, :] <= pos[:, None]
    gain_q = lax.dynamic_slice_in_dim(gain_query, ctx_index * cols, cols)
    gain_k = lax.dynamic_slice_in_dim(gain_key, ctx_index * cols, cols)

    qkv = jnp.dot(x_all, qkv_w, preferred_element_type=f32)
    q_raw, k_raw, v_raw = qkv[:, :cols], qkv[:, cols : 2 * cols], qkv[:, 2 * cols :]
    squares = jnp.stack([jnp.sum(q_raw * q_raw, axis=1), jnp.sum(k_raw * k_raw, axis=1)])
    squares = lax.psum(squares, "ctx")
    scales = lax.rsqrt(squares / width + EPSILON)
    c_q, c_k = scales[0][:, None], scales[1][:, None]

    def rope(v):
        return turn_half(v.reshape(seq, heads, HD), cosine, sine)

    def rope_back(w):
        w = w.reshape(seq, heads, HD)
        u = w * sine
        half = HD // 2
        turned = jnp.concatenate([u[..., half:], -u[..., :half]], axis=-1)
        return (w * cosine + turned).reshape(seq, cols)

    queries = rope(q_raw * c_q * gain_q).astype(bf16)
    keys = rope(k_raw * c_k * gain_k).astype(bf16)
    values = v_raw.astype(bf16).reshape(seq, heads, HD)
    scores = jnp.einsum("qhd,khd->hqk", queries, keys, preferred_element_type=f32) * scale
    scores = jnp.where(mask[None], scores, NEGATIVE)
    exponent = jnp.exp(scores - jnp.max(scores, axis=-1, keepdims=True))
    probs = exponent / jnp.sum(exponent, axis=-1, keepdims=True)
    prob_low = probs.astype(bf16)
    attended = (
        jnp.einsum("hqk,khd->qhd", prob_low, values, preferred_element_type=f32)
        .reshape(seq, cols)
        .astype(bf16)
    )
    branch = lax.psum_scatter(
        jnp.dot(attended, out_w, preferred_element_type=f32).astype(bf16),
        "ctx", scatter_dimension=0, tiled=True,
    ).astype(f32)
    mid = token_rows.astype(f32) + norm_scale(branch, gain_attn)
    mid_all = lax.all_gather(mid.astype(bf16), "ctx", axis=0, tiled=True)
    gate_act = jnp.dot(mid_all, gate_w, preferred_element_type=f32)
    up_act = jnp.dot(mid_all, up_w, preferred_element_type=f32)
    hidden = activate(gate_act, up_act).astype(bf16)
    mlp_out = lax.psum_scatter(
        jnp.dot(hidden, down_w, preferred_element_type=f32).astype(bf16),
        "ctx", scatter_dimension=0, tiled=True,
    ).astype(f32)
    output = (mid + norm_scale(mlp_out, gain_mlp)).astype(bf16)

    d_output = cotangent[0].astype(f32)
    unused_mlp, pull_mlp = jax.vjp(norm_scale, mlp_out, gain_mlp)
    d_mlp, grad_gm = pull_mlp(d_output)
    d_mlp_all = lax.all_gather(d_mlp.astype(bf16), "ctx", axis=0, tiled=True)
    d_hidden = times_transpose(d_mlp_all, down_w)
    unused_act, pull_act = jax.vjp(activate, gate_act, up_act)
    d_gate, d_up = pull_act(d_hidden)
    d_gate = d_gate.astype(bf16)
    d_up = d_up.astype(bf16)
    d_mid_part = times_transpose(d_gate, gate_w) + times_transpose(d_up, up_w)
    d_mid = d_output + lax.psum_scatter(
        d_mid_part.astype(bf16), "ctx", scatter_dimension=0, tiled=True
    ).astype(f32)

    down_sum = lax.psum_scatter(
        transpose_times(hidden, d_mlp_all).astype(bf16), "fsdp", scatter_dimension=0, tiled=True
    )
    moves = [
        (z * fsdp_count + f, f * ctx_count + z)
        for z in range(ctx_count)
        for f in range(fsdp_count)
    ]
    grad_down = lax.ppermute(down_sum, ("ctx", "fsdp"), moves).astype(f32)

    def column_grad(left, right):
        part = transpose_times(left, right).astype(bf16)
        mine = lax.psum_scatter(
            spread_rows(part, ctx_count, fsdp_count), "fsdp", scatter_dimension=0, tiled=True
        )
        mine = mine.reshape(ctx_count, mine.shape[0] // ctx_count, mine.shape[1])
        return lax.all_to_all(mine, "ctx", 0, 0, tiled=True)

    gate_up = column_grad(mid_all, jnp.concatenate([d_gate, d_up], axis=1))
    rows = gate_up.shape[1]

    def from_strips(part):
        return (
            part.reshape(ctx_count, rows, fsdp_count, strip)
            .transpose(1, 2, 0, 3)
            .reshape(rows, hidden_width)
            .astype(f32)
        )

    unused_branch, pull_branch = jax.vjp(norm_scale, branch, gain_attn)
    d_branch, grad_ga = pull_branch(d_mid)
    d_branch_all = lax.all_gather(d_branch.astype(bf16), "ctx", axis=0, tiled=True)
    d_attended = times_transpose(d_branch_all, out_w).astype(bf16).reshape(seq, heads, HD)
    grad_out = lax.psum_scatter(
        transpose_times(attended, d_branch_all).astype(bf16),
        "fsdp", scatter_dimension=0, tiled=True,
    ).astype(f32)

    d_values = jnp.einsum("hqk,qhd->khd", prob_low, d_attended, preferred_element_type=f32)
    d_values = d_values.astype(bf16).reshape(seq, cols)
    d_probs = jnp.einsum("qhd,khd->hqk", d_attended, values, preferred_element_type=f32)
    delta = jnp.sum(probs * d_probs, axis=-1, keepdims=True)
    d_scores = (probs * (d_probs - delta)).astype(bf16)
    d_queries = jnp.einsum("hqk,khd->qhd", d_scores, keys, preferred_element_type=f32) * scale
    d_keys = jnp.einsum("hqk,qhd->khd", d_scores, queries, preferred_element_type=f32) * scale
    dy_q = rope_back(d_queries)
    dy_k = rope_back(d_keys)
    dots = jnp.stack([
        jnp.sum(q_raw * gain_q * dy_q, axis=1), jnp.sum(k_raw * gain_k * dy_k, axis=1)
    ])
    dots = lax.psum(dots, "ctx") / width
    d_q = c_q * gain_q * dy_q - q_raw * (c_q * c_q * c_q * dots[0][:, None])
    d_k = c_k * gain_k * dy_k - k_raw * (c_k * c_k * c_k * dots[1][:, None])
    d_qkv = jnp.concatenate([d_q.astype(bf16), d_k.astype(bf16), d_values], axis=1)
    d_tokens = d_mid + lax.psum_scatter(
        times_transpose(d_qkv, qkv_w).astype(bf16), "ctx", scatter_dimension=0, tiled=True
    ).astype(f32)
    qkv_grad = column_grad(x_all, d_qkv).transpose(1, 0, 2)
    sum_gqk = lax.psum_scatter(
        jnp.stack([jnp.sum(dy_q * q_raw * c_q, axis=0), jnp.sum(dy_k * k_raw * c_k, axis=0)]),
        "fsdp", scatter_dimension=1, tiled=True,
    )
    sum_gam = lax.psum_scatter(
        jnp.stack([grad_ga, grad_gm]), ("ctx", "fsdp"), scatter_dimension=1, tiled=True
    )

    def whole(part):
        return part.reshape(part.shape[0], width).astype(f32)

    return (
        output[None],
        d_tokens.astype(bf16)[None],
        whole(qkv_grad[:, :, :cols]),
        whole(qkv_grad[:, :, cols : 2 * cols]),
        whole(qkv_grad[:, :, 2 * cols :]),
        grad_out,
        from_strips(gate_up[:, :, :hid]),
        from_strips(gate_up[:, :, hid:]),
        grad_down,
        sum_gqk[0],
        sum_gqk[1],
        sum_gam[0],
        sum_gam[1],
    )


def solution(mesh):
    in_specs = (
        P("fsdp", "ctx", None),
        P("fsdp", None),
        P("fsdp", None),
        P("fsdp", None),
        P("fsdp", None),
        P("fsdp", None),
        P("fsdp", None),
        P("fsdp", None),
        P("fsdp", None),
        P(),
        P(),
        P(),
        P(),
        P("fsdp", "ctx", None),
    )
    out_specs = (
        P("fsdp", "ctx", None),
        P("fsdp", "ctx", None),
        P(("ctx", "fsdp"), None),
        P(("ctx", "fsdp"), None),
        P(("ctx", "fsdp"), None),
        P(("ctx", "fsdp"), None),
        P(("ctx", "fsdp"), None),
        P(("ctx", "fsdp"), None),
        P(("ctx", "fsdp"), None),
        P(("ctx", "fsdp")),
        P(("ctx", "fsdp")),
        P(("ctx", "fsdp")),
        P(("ctx", "fsdp")),
    )
    return jax.shard_map(shards, mesh=mesh, in_specs=in_specs, out_specs=out_specs, check_vma=False)
```

```python
import math

import jax
import jax.numpy as jnp
from jax import lax
from jax.experimental import pallas as pl
from jax.experimental.pallas import tpu as pltpu
from jax.sharding import PartitionSpec as P

HD = 128


EPSILON = 1e-06
ROPE_BASE = 500000.0
NEGATIVE = -1e30


def norm_scale(values, gain_vec):
    return (
        values * lax.rsqrt(jnp.mean(values * values, axis=-1, keepdims=True) + EPSILON) * gain_vec
    )


def turn_half(values, cosine, sine):
    half_size = values.shape[-1] // 2
    turned = jnp.concatenate([-values[..., half_size:], values[..., :half_size]], axis=-1)
    return values * cosine + turned * sine


def angle_tables(positions, head_size):
    half_size = head_size // 2
    frequency = jnp.power(ROPE_BASE, -(jnp.arange(half_size).astype(jnp.float32) * 2.0 / head_size))
    angles = positions.astype(jnp.float32)[:, None] * frequency[None, :]
    angles = jnp.concatenate([angles, angles], axis=-1)
    return (jnp.cos(angles)[:, None, :], jnp.sin(angles)[:, None, :])


def row_positions(row_ids, pair_row, block_rows, ctx_count):
    rank_of = row_ids // (2 * block_rows)
    second = row_ids // block_rows % 2
    offset = row_ids % block_rows
    rank_match = (rank_of[:, None] == jnp.arange(ctx_count, dtype=jnp.int32)[None, :]).astype(
        jnp.int32
    )
    chosen = jnp.sum(rank_match * pair_row[None, :], axis=1)
    block_index = jnp.where(second == 0, chosen, 2 * ctx_count - 1 - chosen)
    return block_index * block_rows + offset


def times_transpose(left, right):
    return lax.dot_general(
        left, right, (((1,), (1,)), ((), ())), preferred_element_type=jnp.float32
    )


def transpose_times(left, right):
    return lax.dot_general(
        left, right, (((0,), (0,)), ((), ())), preferred_element_type=jnp.float32
    )


def activate(gate_in, up_in):
    return jax.nn.silu(gate_in) * up_in


def spread_rows(values, outer, inner):
    rows, width = values.shape
    return (
        values.reshape(outer, inner, rows // (outer * inner), width)
        .transpose(1, 0, 2, 3)
        .reshape(rows, width)
    )


def shards_general(
    tokens,
    block_pairs,
    w_query,
    w_key,
    w_value,
    w_out,
    w_gate,
    w_up,
    w_down,
    gain_query,
    gain_key,
    gain_attn,
    gain_mlp,
    cotangent,
):
    bf16 = jnp.bfloat16
    f32 = jnp.float32
    local_rows = tokens.shape[1]
    block_rows = local_rows // 2
    width = w_query.shape[1]
    hidden_width = w_gate.shape[1]
    ctx_count = lax.axis_size("ctx")
    fsdp_count = lax.axis_size("fsdp")
    ctx_index = lax.axis_index("ctx")
    seq = local_rows * ctx_count
    cols = width // ctx_count
    heads = cols // HD
    strip = hidden_width // (ctx_count * fsdp_count)
    hid = strip * fsdp_count
    scale = HD ** (-0.5)

    def ctx_cols(w):
        return lax.dynamic_slice_in_dim(w, ctx_index * cols, cols, 1)

    def ctx_strips(w):
        parts = w.reshape(w.shape[0], fsdp_count, ctx_count, strip)
        return lax.dynamic_index_in_dim(parts, ctx_index, 2, keepdims=False).reshape(w.shape[0], hid)

    token_rows = tokens[0]
    x_all = lax.all_gather(token_rows, "ctx", axis=0, tiled=True)
    qkv_w = lax.all_gather(
        jnp.concatenate([ctx_cols(w_query), ctx_cols(w_key), ctx_cols(w_value)], axis=1),
        "fsdp", axis=0, tiled=True,
    )
    out_w = lax.dynamic_slice_in_dim(
        lax.all_gather(w_out, "fsdp", axis=0, tiled=True), ctx_index * cols, cols, 0
    )
    gate_w = lax.all_gather(ctx_strips(w_gate), "fsdp", axis=0, tiled=True)
    up_w = lax.all_gather(ctx_strips(w_up), "fsdp", axis=0, tiled=True)
    down_w = lax.all_gather(
        lax.dynamic_slice_in_dim(w_down, ctx_index * strip, strip, 0), "fsdp", axis=0, tiled=True
    )

    pos = row_positions(jnp.arange(seq, dtype=jnp.int32), block_pairs[0], block_rows, ctx_count)
    cosine, sine = angle_tables(pos, HD)
    mask = pos[None, :] <= pos[:, None]
    gain_q = lax.dynamic_slice_in_dim(gain_query, ctx_index * cols, cols)
    gain_k = lax.dynamic_slice_in_dim(gain_key, ctx_index * cols, cols)

    qkv = jnp.dot(x_all, qkv_w, preferred_element_type=f32)
    q_raw, k_raw, v_raw = qkv[:, :cols], qkv[:, cols : 2 * cols], qkv[:, 2 * cols :]
    squares = jnp.stack([jnp.sum(q_raw * q_raw, axis=1), jnp.sum(k_raw * k_raw, axis=1)])
    squares = lax.psum(squares, "ctx")
    scales = lax.rsqrt(squares / width + EPSILON)
    c_q, c_k = scales[0][:, None], scales[1][:, None]

    def rope(v):
        return turn_half(v.reshape(seq, heads, HD), cosine, sine)

    def rope_back(w):
        w = w.reshape(seq, heads, HD)
        u = w * sine
        half = HD // 2
        turned = jnp.concatenate([u[..., half:], -u[..., :half]], axis=-1)
        return (w * cosine + turned).reshape(seq, cols)

    queries = rope(q_raw * c_q * gain_q).astype(bf16)
    keys = rope(k_raw * c_k * gain_k).astype(bf16)
    values = v_raw.astype(bf16).reshape(seq, heads, HD)
    scores = jnp.einsum("qhd,khd->hqk", queries, keys, preferred_element_type=f32) * scale
    scores = jnp.where(mask[None], scores, NEGATIVE)
    exponent = jnp.exp(scores - jnp.max(scores, axis=-1, keepdims=True))
    probs = exponent / jnp.sum(exponent, axis=-1, keepdims=True)
    prob_low = probs.astype(bf16)
    attended = (
        jnp.einsum("hqk,khd->qhd", prob_low, values, preferred_element_type=f32)
        .reshape(seq, cols)
        .astype(bf16)
    )
    branch = lax.psum_scatter(
        jnp.dot(attended, out_w, preferred_element_type=f32).astype(bf16),
        "ctx", scatter_dimension=0, tiled=True,
    ).astype(f32)
    mid = token_rows.astype(f32) + norm_scale(branch, gain_attn)
    mid_all = lax.all_gather(mid.astype(bf16), "ctx", axis=0, tiled=True)
    gate_act = jnp.dot(mid_all, gate_w, preferred_element_type=f32)
    up_act = jnp.dot(mid_all, up_w, preferred_element_type=f32)
    hidden = activate(gate_act, up_act).astype(bf16)
    mlp_out = lax.psum_scatter(
        jnp.dot(hidden, down_w, preferred_element_type=f32).astype(bf16),
        "ctx", scatter_dimension=0, tiled=True,
    ).astype(f32)
    output = (mid + norm_scale(mlp_out, gain_mlp)).astype(bf16)

    d_output = cotangent[0].astype(f32)
    unused_mlp, pull_mlp = jax.vjp(norm_scale, mlp_out, gain_mlp)
    d_mlp, grad_gm = pull_mlp(d_output)
    d_mlp_all = lax.all_gather(d_mlp.astype(bf16), "ctx", axis=0, tiled=True)
    d_hidden = times_transpose(d_mlp_all, down_w)
    unused_act, pull_act = jax.vjp(activate, gate_act, up_act)
    d_gate, d_up = pull_act(d_hidden)
    d_gate = d_gate.astype(bf16)
    d_up = d_up.astype(bf16)
    d_mid_part = times_transpose(d_gate, gate_w) + times_transpose(d_up, up_w)
    d_mid = d_output + lax.psum_scatter(
        d_mid_part.astype(bf16), "ctx", scatter_dimension=0, tiled=True
    ).astype(f32)

    down_sum = lax.psum_scatter(
        transpose_times(hidden, d_mlp_all).astype(bf16), "fsdp", scatter_dimension=0, tiled=True
    )
    moves = [
        (z * fsdp_count + f, f * ctx_count + z)
        for z in range(ctx_count)
        for f in range(fsdp_count)
    ]
    grad_down = lax.ppermute(down_sum, ("ctx", "fsdp"), moves).astype(f32)

    def column_grad(left, right):
        part = transpose_times(left, right).astype(bf16)
        mine = lax.psum_scatter(
            spread_rows(part, ctx_count, fsdp_count), "fsdp", scatter_dimension=0, tiled=True
        )
        mine = mine.reshape(ctx_count, mine.shape[0] // ctx_count, mine.shape[1])
        return lax.all_to_all(mine, "ctx", 0, 0, tiled=True)

    gate_up = column_grad(mid_all, jnp.concatenate([d_gate, d_up], axis=1))
    rows = gate_up.shape[1]

    def from_strips(part):
        return (
            part.reshape(ctx_count, rows, fsdp_count, strip)
            .transpose(1, 2, 0, 3)
            .reshape(rows, hidden_width)
            .astype(f32)
        )

    unused_branch, pull_branch = jax.vjp(norm_scale, branch, gain_attn)
    d_branch, grad_ga = pull_branch(d_mid)
    d_branch_all = lax.all_gather(d_branch.astype(bf16), "ctx", axis=0, tiled=True)
    d_attended = times_transpose(d_branch_all, out_w).astype(bf16).reshape(seq, heads, HD)
    grad_out = lax.psum_scatter(
        transpose_times(attended, d_branch_all).astype(bf16),
        "fsdp", scatter_dimension=0, tiled=True,
    ).astype(f32)

    d_values = jnp.einsum("hqk,qhd->khd", prob_low, d_attended, preferred_element_type=f32)
    d_values = d_values.astype(bf16).reshape(seq, cols)
    d_probs = jnp.einsum("qhd,khd->hqk", d_attended, values, preferred_element_type=f32)
    delta = jnp.sum(probs * d_probs, axis=-1, keepdims=True)
    d_scores = (probs * (d_probs - delta)).astype(bf16)
    d_queries = jnp.einsum("hqk,khd->qhd", d_scores, keys, preferred_element_type=f32) * scale
    d_keys = jnp.einsum("hqk,qhd->khd", d_scores, queries, preferred_element_type=f32) * scale
    dy_q = rope_back(d_queries)
    dy_k = rope_back(d_keys)
    dots = jnp.stack([
        jnp.sum(q_raw * gain_q * dy_q, axis=1), jnp.sum(k_raw * gain_k * dy_k, axis=1)
    ])
    dots = lax.psum(dots, "ctx") / width
    d_q = c_q * gain_q * dy_q - q_raw * (c_q * c_q * c_q * dots[0][:, None])
    d_k = c_k * gain_k * dy_k - k_raw * (c_k * c_k * c_k * dots[1][:, None])
    d_qkv = jnp.concatenate([d_q.astype(bf16), d_k.astype(bf16), d_values], axis=1)
    d_tokens = d_mid + lax.psum_scatter(
        times_transpose(d_qkv, qkv_w).astype(bf16), "ctx", scatter_dimension=0, tiled=True
    ).astype(f32)
    qkv_grad = column_grad(x_all, d_qkv).transpose(1, 0, 2)
    sum_gqk = lax.psum_scatter(
        jnp.stack([jnp.sum(dy_q * q_raw * c_q, axis=0), jnp.sum(dy_k * k_raw * c_k, axis=0)]),
        "fsdp", scatter_dimension=1, tiled=True,
    )
    sum_gam = lax.psum_scatter(
        jnp.stack([grad_ga, grad_gm]), ("ctx", "fsdp"), scatter_dimension=1, tiled=True
    )

    def whole(part):
        return part.reshape(part.shape[0], width).astype(f32)

    return (
        output[None],
        d_tokens.astype(bf16)[None],
        whole(qkv_grad[:, :, :cols]),
        whole(qkv_grad[:, :, cols : 2 * cols]),
        whole(qkv_grad[:, :, 2 * cols :]),
        grad_out,
        from_strips(gate_up[:, :, :hid]),
        from_strips(gate_up[:, :, hid:]),
        grad_down,
        sum_gqk[0],
        sum_gqk[1],
        sum_gam[0],
        sum_gam[1],
    )


MESH = pl.DeviceIdType.MESH
BF16 = jnp.bfloat16
F32 = jnp.float32
LINE = 4
PLANE = 4


def dot(left, right):
    return lax.dot_general(left, right, (((1,), (0,)), ((), ())), preferred_element_type=F32)


def dot_rt(left, right):
    return lax.dot_general(left, right, (((1,), (1,)), ((), ())), preferred_element_type=F32)


def dot_lt(left, right):
    return lax.dot_general(left, right, (((0,), (0,)), ((), ())), preferred_element_type=F32)


def exact(left, right, dims):
    return lax.dot_general(
        left, right, (dims, ((), ())), precision=lax.Precision.HIGHEST, preferred_element_type=F32
    )


def remote(src, dst, send, recv, device):
    return pltpu.make_async_remote_copy(
        src_ref=src, dst_ref=dst, send_sem=send, recv_sem=recv, device_id=device, device_id_type=MESH
    )


def at128(i, step=128):
    return pl.ds(i if isinstance(i, int) else pl.multiple_of(i, step), step)


class Place:
    def __init__(self):
        z = lax.axis_index("ctx")
        f = lax.axis_index("fsdp")
        self.z, self.f = z, f
        self.p, self.k = f // 2, f % 2
        self.p_x = self.p + 1 - 2 * (self.p % 2)
        self.p_y = (self.p + 2) % PLANE
        self.p_d = PLANE - 1 - self.p
        self.partner = (z, 2 * self.p + 1 - self.k)
        self.x = (z, 2 * self.p_x + self.k)
        self.y = (z, 2 * self.p_y + self.k)
        self.d = (z, 2 * self.p_d + self.k)
        self.ends = z // 3 + (3 - z) // 3

    def line(self, c):
        return (c, self.f)

    def order(self, s):
        z, e, t = self.z, self.ends, s // 3
        end = z + s * (1 - 2 * (z // 3))
        mid = (1 - t) * (z + (3 * s * s - 5 * s) // 2) + t * 3 * (2 - z)
        return e * end + (1 - e) * mid

    def cross(self, c):
        return (c, 2 * self.p + 1 - self.k)

    def barrier(self, more=(), senders=()):
        sem = pltpu.get_barrier_semaphore()

        def greet(peer):
            pl.semaphore_signal(sem, inc=1, device_id=peer, device_id_type=MESH)

        peers = [self.partner, self.x, self.y] + list(more)
        peers += [self.line((self.z + step) % LINE) for step in range(1, LINE)]
        for peer in peers:
            greet(peer)
        count = len(peers)
        for here, peer in senders:
            pl.when(here)(lambda peer=peer: greet(peer))
            count = count + here.astype(jnp.int32)
        pl.semaphore_wait(sem, count)


class Gather:
    def __init__(self, place, buf, z_send, z_recv, c_send, c_recv):
        self.pl, self.buf = place, buf
        self.sems = z_send, z_recv, c_send, c_recv

    def to_line(self, c, target, way):
        z_send, z_recv, _, _ = self.sems
        part = self.buf.at[c, self.pl.k]
        return remote(part, part, z_send.at[way, c], z_recv.at[c], self.pl.line(target))

    def to_core(self, c):
        _, _, c_send, c_recv = self.sems
        part = self.buf.at[c, self.pl.k]
        return remote(part, part, c_send.at[c], c_recv.at[c], self.pl.partner)

    def from_core(self, c):
        _, _, c_send, c_recv = self.sems
        part = self.buf.at[c, 1 - self.pl.k]
        return remote(part, part, c_send.at[c], c_recv.at[c], self.pl.partner)

    def start(self):
        z = self.pl.z
        pl.when(z < LINE - 1)(lambda: self.to_line(z, z + 1, 0).start())
        pl.when(z > 0)(lambda: self.to_line(z, z - 1, 1).start())
        self.to_core(z).start()

    def arrive(self, c):
        z = self.pl.z
        self.to_line(c, z, 0).wait_recv()
        pl.when(jnp.logical_and(c < z, z < LINE - 1))(lambda: self.to_line(c, z + 1, 0).start())
        pl.when(jnp.logical_and(c > z, z > 0))(lambda: self.to_line(c, z - 1, 1).start())
        self.to_core(c).start()

    def arrive_first(self):
        self.arrive(self.pl.order(1))
        pl.when(self.pl.ends == 0)(lambda: self.arrive(self.pl.order(2)))

    def arrive_second(self):
        pl.when(self.pl.ends == 1)(lambda: self.arrive(self.pl.order(2)))

    def arrive_third(self):
        self.arrive(self.pl.order(3))

    def ready(self, c):
        self.from_core(c).wait_recv()

    def finish(self):
        z = self.pl.z

        def body(c, carry):
            pl.when(jnp.logical_and(c <= z, z < LINE - 1))(
                lambda: self.to_line(c, z, 0).wait_send()
            )
            pl.when(jnp.logical_and(c >= z, z > 0))(lambda: self.to_line(c, z, 1).wait_send())
            self.to_core(c).wait_send()
            return carry

        lax.fori_loop(0, LINE, body, 0)


class RowSum:
    def __init__(self, place, term, pair_out, pair_in, keep, mine, line_out, line_in, sems):
        self.pl, self.term = place, term
        self.pair_out, self.pair_in, self.keep, self.mine = pair_out, pair_in, keep, mine
        self.line_out, self.line_in = line_out, line_in
        self.p_send, self.p_recv, self.l_send, self.l_recv = sems

    def pair(self, c):
        return remote(
            self.pair_out.at[c], self.pair_in.at[c], self.p_send.at[c], self.p_recv.at[c], self.pl.partner
        )

    def line(self, c, source):
        return remote(
            self.line_out.at[c], self.line_in.at[source], self.l_send.at[c], self.l_recv.at[source],
            self.pl.line(c),
        )

    def give(self, c, s):
        k = self.pl.k
        self.pair_out[c] = self.term[1 - k].astype(BF16)
        self.pair(c).start()
        self.keep[s % 2] = self.term[k]

    def pass_on(self, c, s):
        z = self.pl.z
        self.pair(c).wait_recv()

        @pl.when(c != z)
        def _():
            self.line_out[c] = (self.keep[s % 2] + self.pair_in[c].astype(F32)).astype(BF16)
            self.line(c, z).start()

        @pl.when(c == z)
        def _():
            self.mine[...] = self.keep[s % 2] + self.pair_in[c].astype(F32)

    def total(self):
        z = self.pl.z
        for step in range(1, LINE):
            self.line((z + step) % LINE, (z + step) % LINE).wait_recv()
        result = self.mine[...]
        for step in range(1, LINE):
            result = result + self.line_in[(z + step) % LINE].astype(F32)
        return result

    def finish(self):
        z = self.pl.z

        def body(c, carry):
            self.pair(c).wait_send()
            pl.when(c != z)(lambda: self.line(c, z).wait_send())
            return carry

        lax.fori_loop(0, LINE, body, 0)


class Ring:
    def __init__(self, place, buf, rows, send, recv):
        self.pl, self.buf, self.rows = place, buf, rows
        self.send, self.recv = send, recv

    def block(self, p):
        return self.buf.at[at128(p * self.rows, self.rows)]

    def half(self, p, i):
        size = self.rows // 2
        return self.buf.at[at128(p * self.rows + i * size, size)]

    def own(self, way):
        part = self.block(self.pl.p)
        return remote(part, part, self.send.at[way], self.recv.at[way], (self.pl.x, self.pl.y)[way])

    def far(self, i):
        part = self.half((self.pl.p_x, self.pl.p_y)[i], i)
        return remote(part, part, self.send.at[2 + i], self.recv.at[2 + i], (self.pl.y, self.pl.x)[i])

    def start(self):
        self.own(0).start()
        self.own(1).start()

    def forward(self):
        for i in range(2):
            part = self.block((self.pl.p_x, self.pl.p_y)[i])
            remote(part, part, self.send.at[i], self.recv.at[i], (self.pl.x, self.pl.y)[i]).wait_recv()
            self.far(i).start()

    def ready(self):
        for i in range(2):
            part = self.half(self.pl.p_d, i)
            remote(part, part, self.send.at[2 + i], self.recv.at[2 + i], self.pl.x).wait_recv()

    def finish(self):
        for i in range(2):
            self.own(i).wait_send()
            self.far(i).wait_send()


def scale_columns(totals, rows, which):
    pick = (lax.broadcasted_iota(jnp.int32, (8, 128), 0) == which).astype(F32)
    return exact(totals[:, rows], pick, ((0,), (0,)))


def forward_kernel(
    pairs, gains_qk, gain_attn, gain_mlp, tokens, cotangent,
    w_query, w_key, w_value, w_out, w_gate, w_up, w_down,
    o_out, o_dmlp, o_gm, o_branch, o_tot,
    o_qkv, o_wo, o_g, o_u, o_dn, o_x, o_m, o_ga, o_ua, o_hid, o_raw, o_heads, o_probs, o_att, o_tab,
    qkv, wo, wg, wu, wd, xs, ms, ga, ua, hid, raw, heads, probs, att, tab, posr, posc,
    term, pair_out, pair_in, keep, mine, line_out, line_in,
    sq_own, sq_pair, sq_both, sq_line, mid,
    loc_sem, swap_send, swap_recv, ring_send, ring_recv, wo_send, wo_recv,
    zs, zr, cs, cr, ps, pr, ls, lr, ts, tr, as_, ar, out_sem,
):
    place = Place()
    z, f, p, k = place.z, place.f, place.p, place.k
    rows = 128
    width = 2048
    cols = 256
    seq = 512
    place.barrier()

    def own_rows(n):
        return at128(n * (2 * p + k), n)

    def strips(core):
        return [1024 * (2 * q + core) + 256 * z for q in range(PLANE)]

    local, swap = {}, {}

    def split(name, w, buf, sources, first):
        local[name], swap[name] = [], []
        for i, (mine, theirs) in enumerate(sources):
            dst = buf.at[own_rows(256), pl.ds(256 * i + first[1], 256)]
            local[name].append(
                pltpu.make_async_copy(w.at[:, at128(mine, 256)], dst, loc_sem.at[first[0] + i])
            )
            swap[name].append(
                remote(
                    w.at[:, at128(theirs, 256)], dst, swap_send.at[first[0] + i],
                    swap_recv.at[first[0] + i], place.partner,
                )
            )

    head_cols = [(256 * (2 * z + k), 256 * (2 * z + 1 - k))]
    hid_cols = list(zip(strips(k), strips(1 - k)))
    split("q", w_query, qkv, head_cols, (0, 0))
    split("k", w_key, qkv, head_cols, (1, 256))
    split("v", w_value, qkv, head_cols, (2, 512))
    split("g", w_gate, wg, hid_cols, (3, 0))
    split("u", w_up, wu, hid_cols, (7, 0))

    def begin(*names):
        for name in names:
            for a, b in zip(local[name], swap[name]):
                b.start()
                a.start()

    def settle(*names):
        for name in names:
            for a, b in zip(local[name], swap[name]):
                a.wait()
                b.wait_recv()

    begin("q", "k", "v")
    xs[z, k] = tokens[...]
    gather_x = Gather(place, xs, zs.at[0], zr.at[0], cs.at[0], cr.at[0])
    gather_x.start()
    down_copy = pltpu.make_async_copy(
        w_down.at[at128(256 * z, 256)], wd.at[at128(256 * p, 256)], loc_sem.at[11]
    )
    down_copy.start()
    begin("g", "u")
    ring_qkv = Ring(place, qkv, 512, ring_send.at[0], ring_recv.at[0])
    ring_g = Ring(place, wg, 512, ring_send.at[1], ring_recv.at[1])
    ring_u = Ring(place, wu, 512, ring_send.at[2], ring_recv.at[2])
    ring_d = Ring(place, wd, 256, ring_send.at[3], ring_recv.at[3])
    settle("q", "k", "v")
    ring_qkv.start()

    dx, dy = (p % 2 + z % 2) % 2, (p // 2 + z // 2) % 2
    top, low = wo.at[pl.ds(0, 128)], wo.at[pl.ds(128, 128)]
    wo_copy = pltpu.make_async_copy(w_out, wo, loc_sem.at[12])

    def wo_send_to(i, part, device):
        return remote(part, part, wo_send.at[i], wo_recv.at[i], device)

    is_source = jnp.logical_and(dx == 0, dy == 0)
    is_x = jnp.logical_and(dx == 1, dy == 0)
    is_y = jnp.logical_and(dx == 0, dy == 1)
    is_d = jnp.logical_and(dx == 1, dy == 1)

    @pl.when(is_source)
    def _():
        wo_copy.start()

    def positions(shape, axis):
        i = lax.broadcasted_iota(jnp.int32, shape, axis)
        block = i // 64
        pos = jnp.zeros(shape, jnp.int32)
        for r in range(LINE):
            b = pairs[0, r]
            pos = pos + jnp.where(block == 2 * r, b * 64, 0)
            pos = pos + jnp.where(block == 2 * r + 1, (2 * LINE - 1 - b) * 64, 0)
        return (pos + i % 64).astype(F32)

    posr[k] = positions((8, seq), 1)
    col = positions((seq, 128), 0)
    posc[k] = col
    lane = lax.broadcasted_iota(jnp.int32, (seq, 128), 1)
    freq = jnp.exp((lane % 64).astype(F32) * (-2.0 / HD * math.log(ROPE_BASE)))
    angle = col * freq
    tab[0, k] = jnp.cos(angle)
    sine = jnp.sin(angle)
    tab[1, k] = jnp.where(lane < 64, -sine, sine)
    tables = [
        remote(r, r, ts.at[i], tr.at[i], place.partner)
        for i, r in enumerate([posr.at[k], posc.at[k], tab.at[0, k], tab.at[1, k]])
    ]
    for t in tables:
        t.start()

    gather_x.arrive_first()
    ring_qkv.forward()
    settle("g")
    ring_g.start()

    @pl.when(is_source)
    def _():
        wo_copy.wait()
        wo_send_to(0, top, place.x).start()
        wo_send_to(1, low, place.y).start()

    gather_x.arrive_second()
    ring_qkv.ready()

    def project(c):
        gather_x.ready(c)
        chunk = xs[c].reshape(2 * rows, width)
        there = at128(c * rows)
        sums = jnp.zeros((8, 2 * rows), F32)
        pick = lax.broadcasted_iota(jnp.int32, (8, cols), 0)
        for i in range(2):
            part = dot(chunk, qkv[:, i * cols : (i + 1) * cols])
            raw[i, :, there] = part.reshape(2, rows, cols)
            sums = sums + exact((pick == i).astype(F32), part * part, ((1,), (1,)))
        part = dot(chunk, qkv[:, 2 * cols :])
        heads[2, :, there] = part.astype(BF16).reshape(2, rows, cols)
        sq_own[c] = sums

    def project_step(s, carry):
        project(place.order(s))
        return carry

    lax.fori_loop(0, 2, project_step, 0)
    pl.when(is_x)(lambda: wo_send_to(0, top, place.x).wait_recv())
    pl.when(is_x)(lambda: wo_send_to(0, top, place.y).start())
    pl.when(is_y)(lambda: wo_send_to(1, low, place.x).wait_recv())
    pl.when(is_y)(lambda: wo_send_to(1, low, place.x).start())
    gather_x.arrive_third()
    lax.fori_loop(2, 4, project_step, 0)

    pair_sq = remote(sq_own, sq_pair, as_.at[0], ar.at[0], place.partner)
    pair_sq.start()
    settle("u")
    pair_sq.wait_recv()
    sq_both[...] = sq_own[...] + sq_pair[...]

    def line_sq(step, source):
        return remote(
            sq_both, sq_line.at[source], as_.at[step], ar.at[1 + source],
            place.line((z + step) % LINE),
        )

    for step in range(1, LINE):
        line_sq(step, z).start()
    for t in tables:
        t.wait_recv()
    for step in range(1, LINE):
        line_sq(step, (z + step) % LINE).wait_recv()
    sq_line[z] = sq_both[...]
    total = (sq_line[0] + sq_line[1]) + (sq_line[2] + sq_line[3])
    scales = lax.rsqrt(total / width + EPSILON)
    o_tot[...] = scales

    def rotate(c, carry):
        there = at128(c * rows)
        now = o_tot[c]
        for i in range(2):
            pick = (lax.broadcasted_iota(jnp.int32, (8, 128), 0) == i).astype(F32)
            column = exact(now, pick, ((0,), (0,)))
            for s in range(2):
                for h in range(2):
                    lanes = slice(128 * h, 128 * h + 128)
                    v = raw[i, s, there, lanes] * column[128 * s : 128 * s + 128]
                    v = v * gains_qk[i : i + 1, lanes]
                    v = v * tab[0, s, there] + pltpu.roll(v, 64, 1) * tab[1, s, there]
                    heads[i, s, there, lanes] = v.astype(BF16)
        return carry

    lax.fori_loop(0, LINE, rotate, 0)

    def attend(s, carry):
        mask = posr[s, 0:1, :] <= posc[s][:, 0:1]
        for h in range(2):
            lanes = slice(128 * h, 128 * h + 128)
            scores = dot_rt(heads[0, s, :, lanes], heads[1, s, :, lanes]) * (HD ** -0.5)
            scores = jnp.where(mask, scores, NEGATIVE)
            e = jnp.exp(scores - jnp.max(scores, axis=1, keepdims=True))
            low_p = (e / jnp.sum(e, axis=1, keepdims=True)).astype(BF16)
            probs[s, h] = low_p
            att[s, :, lanes] = dot(low_p, heads[2, s, :, lanes]).astype(BF16)
        return carry

    lax.fori_loop(0, 2, attend, 0)

    ring_g.forward()
    ring_u.start()

    @pl.when(is_d)
    def _():
        wo_send_to(0, top, place.x).wait_recv()
        wo_send_to(0, top, place.x).start()
        wo_send_to(1, low, place.x).wait_recv()
        wo_send_to(1, low, place.y).start()

    pl.when(is_x)(lambda: wo_send_to(1, low, place.x).wait_recv())
    pl.when(is_y)(lambda: wo_send_to(0, top, place.x).wait_recv())

    sums = RowSum(place, term, pair_out, pair_in, keep, mine, line_out, line_in, (ps, pr, ls, lr))

    def tiles(c, left, weight):
        def body(t, carry):
            lanes = at128(t * 512, 512)
            term[:, :, lanes] = dot(left, weight[:, lanes]).reshape(2, rows, 512)
            return carry

        lax.fori_loop(0, 4, body, 0)

    def branch_step(s, carry):
        c = place.order(3 - s)
        there = at128(c * rows)
        tiles(c, att[:, there].reshape(2 * rows, cols), wo)
        sums.give(c, s)
        pl.when(s > 0)(lambda: sums.pass_on(place.order(4 - s), s + 1))
        return carry

    lax.fori_loop(0, 4, branch_step, 0)
    sums.pass_on(z, 3)
    ring_u.forward()
    down_copy.wait()
    ring_d.start()
    branch = sums.total()
    sums.finish()
    o_branch[...] = branch

    def mean_sq(v):
        return jnp.sum(v * v, axis=1, keepdims=True) / width

    mid[...] = tokens[...].astype(F32) + branch * lax.rsqrt(mean_sq(branch) + EPSILON) * gain_attn[...]
    ms[z, k] = mid[...].astype(BF16)
    gather_m = Gather(place, ms, zs.at[1], zr.at[1], cs.at[1], cr.at[1])
    gather_m.start()

    ring_g.ready()
    ring_u.ready()

    def expand(s, carry):
        c = place.order(s)
        gather_m.ready(c)
        chunk = ms[c].reshape(2 * rows, width)

        def body(t, inner):
            lanes = at128(t * 256, 256)
            g = dot(chunk, wg[:, lanes])
            u = dot(chunk, wu[:, lanes])
            ga[c, :, lanes] = g.astype(BF16)
            ua[c, :, lanes] = u.astype(BF16)
            hid[c, :, lanes] = (g / (1.0 + jnp.exp(-g)) * u).astype(BF16)
            return inner

        lax.fori_loop(0, 4, body, 0)
        return carry

    def contract(s, carry):
        c = place.order(s)
        tiles(c, hid[c], wd)
        sums.give(c, s)
        pl.when(s > 0)(lambda: sums.pass_on(place.order(s - 1), s + 1))
        return carry

    lax.fori_loop(0, 1, expand, 0)
    gather_m.arrive_first()
    lax.fori_loop(1, 2, expand, 0)
    ring_d.forward()
    gather_m.arrive_second()
    lax.fori_loop(2, 3, expand, 0)
    ring_d.ready()
    lax.fori_loop(0, 3, contract, 0)
    gather_m.arrive_third()
    lax.fori_loop(3, 4, expand, 0)
    lax.fori_loop(3, 4, contract, 0)
    sums.pass_on(place.order(3), 3)

    saves = [
        (qkv, o_qkv), (wo, o_wo), (wg, o_g), (wu, o_u), (wd, o_dn), (xs, o_x), (ms, o_m), (ga, o_ga),
        (ua, o_ua), (hid, o_hid), (raw, o_raw), (heads, o_heads), (probs, o_probs), (att, o_att),
        (tab, o_tab),
    ]
    copies = [pltpu.make_async_copy(a, b, out_sem.at[i]) for i, (a, b) in enumerate(saves)]
    for copy in copies:
        copy.start()

    mlp = sums.total()
    sums.finish()
    c_m = lax.rsqrt(mean_sq(mlp) + EPSILON)
    gain = gain_mlp[...]
    o_out[...] = (mid[...] + mlp * c_m * gain).astype(BF16)
    dy = cotangent[...].astype(F32)
    gdy = gain * dy
    inner = jnp.sum(mlp * gdy, axis=1, keepdims=True) / width
    o_dmlp[...] = (c_m * gdy - mlp * (c_m * c_m * c_m * inner)).astype(BF16)
    o_gm[...] = jnp.sum(dy * mlp * c_m, axis=0, keepdims=True)

    gather_x.finish()
    gather_m.finish()
    for ring in (ring_qkv, ring_g, ring_u, ring_d):
        ring.finish()
    for group in swap.values():
        for copy in group:
            copy.wait_send()
    for t in tables:
        t.wait_send()
    pair_sq.wait_send()
    for step in range(1, LINE):
        line_sq(step, z).wait_send()

    @pl.when(is_source)
    def _():
        wo_send_to(0, top, place.x).wait_send()
        wo_send_to(1, low, place.y).wait_send()

    pl.when(is_x)(lambda: wo_send_to(0, top, place.y).wait_send())
    pl.when(is_y)(lambda: wo_send_to(1, low, place.x).wait_send())

    @pl.when(is_d)
    def _():
        wo_send_to(0, top, place.x).wait_send()
        wo_send_to(1, low, place.y).wait_send()

    for copy in copies:
        copy.wait()


def any_spec():
    return pl.BlockSpec(memory_space=pl.ANY)


def vmem_spec():
    return pl.BlockSpec(memory_space=pltpu.VMEM)


def run_forward(pairs, gains_qk, gain_attn, gain_mlp, tokens, cotangent, weights):
    shape = jax.ShapeDtypeStruct
    dma = pltpu.SemaphoreType.DMA
    kept = [
        shape((2048, 768), BF16),
        shape((256, 2048), BF16),
        shape((2048, 1024), BF16),
        shape((2048, 1024), BF16),
        shape((1024, 2048), BF16),
        shape((4, 2, 128, 2048), BF16),
        shape((4, 2, 128, 2048), BF16),
        shape((4, 256, 1024), BF16),
        shape((4, 256, 1024), BF16),
        shape((4, 256, 1024), BF16),
        shape((2, 2, 512, 256), F32),
        shape((3, 2, 512, 256), BF16),
        shape((2, 2, 512, 512), BF16),
        shape((2, 512, 256), BF16),
        shape((2, 2, 512, 128), F32),
    ]
    return pl.pallas_call(
        forward_kernel,
        name="forward",
        out_shape=[
            shape((128, 2048), BF16),
            shape((128, 2048), BF16),
            shape((1, 2048), F32),
            shape((128, 2048), F32),
            shape((4, 8, 256), F32),
        ]
        + kept,
        in_specs=[pl.BlockSpec(memory_space=pltpu.SMEM)] + [vmem_spec()] * 5 + [any_spec()] * 7,
        out_specs=[vmem_spec()] * 5 + [any_spec()] * len(kept),
        scratch_shapes=[pltpu.VMEM(k.shape, k.dtype) for k in kept]
        + [
            pltpu.VMEM((2, 8, 512), F32),
            pltpu.VMEM((2, 512, 128), F32),
            pltpu.VMEM((2, 128, 2048), F32),
            pltpu.VMEM((4, 128, 2048), BF16),
            pltpu.VMEM((4, 128, 2048), BF16),
            pltpu.VMEM((2, 128, 2048), F32),
            pltpu.VMEM((128, 2048), F32),
            pltpu.VMEM((4, 128, 2048), BF16),
            pltpu.VMEM((4, 128, 2048), BF16),
            pltpu.VMEM((4, 8, 256), F32),
            pltpu.VMEM((4, 8, 256), F32),
            pltpu.VMEM((4, 8, 256), F32),
            pltpu.VMEM((4, 4, 8, 256), F32),
            pltpu.VMEM((128, 2048), F32),
            dma((13,)),
            dma((11,)),
            dma((11,)),
            dma((4, 4)),
            dma((4, 4)),
            dma((2,)),
            dma((2,)),
            dma((2, 2, 4)),
            dma((2, 4)),
            dma((2, 4)),
            dma((2, 4)),
            dma((4,)),
            dma((4,)),
            dma((4,)),
            dma((4,)),
            dma((4,)),
            dma((4,)),
            dma((4,)),
            dma((5,)),
            dma((len(kept),)),
        ],
        compiler_params=pltpu.CompilerParams(
            collective_id=0, has_side_effects=True, vmem_limit_bytes=64 * 1024 * 1024
        ),
    )(pairs, gains_qk, gain_attn, gain_mlp, tokens, cotangent, *weights)


def backward_kernel(
    gains_qk, gain_attn, d_mlp, cotangent, branch, scales, gm_part,
    h_qkv, h_wo, h_g, h_u, h_dn, h_x, h_m, h_ga, h_ua, h_hid, h_raw, h_heads, h_probs, h_att, h_tab,
    o_tok, o_gains, o_down, o_out, o_gu, o_qkv,
    st_dn, rc_dn, st_gu, rc_gu, st_qkv, rc_qkv, st_out, rc_out,
    wd, wg, wu, ga, ua, hid, dm, dg, du, ms, db, raw, tab, datt, dy,
    term, pair_out, pair_in, keep, mine, line_out, line_in,
    sq_own, sq_pair, sq_both, sq_line, gn_own, gn_in, d_mid, stage, stage_d,
    ld, zs, zr, cs, cr, ps, pr, ls, lr, as_, ar, gs, gr, in_send, in_recv, st_sem, sum_sem,
    fin_send, fin_recv, fin_loc, al_send, al_recv, al_loc,
):
    place = Place()
    z, f, p, k = place.z, place.f, place.p, place.k
    rows, width, cols = 128, 2048, 256

    down_to = ((p - z + LINE) % LINE, 4 * k + z)
    down_from = (f % 4, 2 * ((z + f % 4) % LINE) + f // 4)
    down_moves = jnp.logical_or(down_to[0] != z, down_to[1] != f)
    out_to = (z, 4 * k + p)
    out_from = (z, 2 * (f % 4) + f // 4)
    out_moves = out_to[1] != f
    place.barrier(
        [place.d] + [place.cross((z + step) % LINE) for step in range(1, LINE)],
        [(down_moves, down_from), (out_moves, out_from)],
    )

    loads = {}

    def load(name, src, dst):
        loads[name] = pltpu.make_async_copy(src, dst, ld.at[len(loads)])
        loads[name].start()

    dm[at128(z * 256 + k * rows)] = d_mlp[...]

    class Rows:
        def __init__(self, ref):
            self.ref = ref

        @property
        def at(self):
            ref = self.ref

            class At:
                def __getitem__(self, key):
                    c, core = key
                    return ref.at[at128(c * 256 + core * rows)]

            return At()

    gather_d = Gather(place, Rows(dm), zs.at[0], zr.at[0], cs.at[0], cr.at[0])
    gather_d.start()
    load("wd", h_dn, wd)
    load("ga", h_ga, ga)
    load("ua", h_ua, ua)
    load("wg", h_g, wg)
    load("wu", h_u, wu)
    load("hid", h_hid, hid)
    load("ms", h_m, ms)
    load("raw", h_raw, raw)
    load("tab", h_tab, tab)

    sums = RowSum(place, term, pair_out, pair_in, keep, mine, line_out, line_in, (ps, pr, ls, lr))

    def chunk_rows(c):
        return at128(c * 256, 256)

    def ffn(s, carry):
        c = place.order(s)
        gather_d.ready(c)
        here = chunk_rows(c)
        grad = dm[here]

        def act(t, inner):
            lanes = at128(t * 256, 256)
            dh = dot_rt(grad, wd[lanes])
            g = ga[here, lanes].astype(F32)
            u = ua[here, lanes].astype(F32)
            sig = 1.0 / (1.0 + jnp.exp(-g))
            dg[here, lanes] = (dh * u * sig * (1.0 + g * (1.0 - sig))).astype(BF16)
            du[here, lanes] = (dh * g * sig).astype(BF16)
            return inner

        lax.fori_loop(0, 4, act, 0)
        left_g, left_u = dg[here], du[here]

        def back(t, inner):
            lanes = at128(t * 512, 512)
            part = dot_rt(left_g, wg[lanes]) + dot_rt(left_u, wu[lanes])
            term[:, :, lanes] = part.reshape(2, rows, 512)
            return inner

        lax.fori_loop(0, 4, back, 0)
        sums.give(c, s)
        pl.when(s > 0)(lambda: sums.pass_on(place.order(s - 1), s + 1))
        return carry

    for name in ("wd", "ga", "ua", "wg", "wu"):
        loads[name].wait()
    lax.fori_loop(0, 1, ffn, 0)
    gather_d.arrive_first()
    lax.fori_loop(1, 2, ffn, 0)
    gather_d.arrive_second()
    lax.fori_loop(2, 3, ffn, 0)
    gather_d.arrive_third()
    lax.fori_loop(3, 4, ffn, 0)
    sums.pass_on(place.order(3), 3)
    load("x", h_x, wd)
    load("qkv", h_qkv, wg.at[:, pl.ds(0, 768)])
    load("probs", h_probs, wu.at[:, pl.ds(0, 512)])
    load("qk", h_heads.at[pl.ds(0, 2048)], wu.at[:, pl.ds(512, 256)])
    load("v", h_heads.at[pl.ds(2048, 1024)], wu.at[pl.ds(0, 1024), pl.ds(768, 256)])
    load("att", h_att, wu.at[pl.ds(1024, 1024), pl.ds(768, 256)])

    chips = [place.p_x, place.p_y, place.p_d, p]
    near = [place.x, place.y, place.d]

    def send_part(kind, i, src, dst):
        return remote(src.at[i], dst.at[i], in_send.at[kind, i], in_recv.at[kind, i], near[i])

    loads["hid"].wait()
    order = (2, 0, 1, 3)
    for n, i in enumerate(order):
        strip = hid[:, at128(((chips[i] - z + LINE) % LINE) * 256, 256)]

        def down(t, carry, strip=strip):
            lanes = at128(t * 512, 512)
            stage_d[:, lanes] = dot_lt(strip, dm[:, lanes]).astype(BF16)
            return carry

        lax.fori_loop(0, 4, down, 0)
        copy = pltpu.make_async_copy(stage_d, st_dn.at[i], st_sem.at[0])
        copy.start()
        copy.wait()
        if i < 3:
            send_part(0, i, st_dn, rc_dn).start()

    load("wo", h_wo, stage_d)
    loads["ms"].wait()

    def feature_rows(ref, chip):
        return jnp.concatenate([ref[:, at128(512 * c + 128 * chip)] for c in range(LINE)], axis=1)

    for n, i in enumerate(order):
        left = feature_rows(ms, chips[i])
        for m, right in enumerate((dg, du)):

            def both(t, carry, left=left, right=right, m=m):
                lanes = at128(t * 256, 256)
                stage[m, :, lanes] = dot_lt(left, right[:, lanes]).astype(BF16)
                return carry

            lax.fori_loop(0, 4, both, 0)
            copy = pltpu.make_async_copy(stage.at[m], st_gu.at[i, m], st_sem.at[1 + m])
            copy.start()
        for m in range(2):
            pltpu.make_async_copy(stage.at[m], st_gu.at[i, m], st_sem.at[1 + m]).wait()
        if i < 3:
            send_part(1, i, st_gu, rc_gu).start()

    gather_d.finish()

    def mean_of(v):
        return jnp.sum(v, axis=1, keepdims=True) / width

    d_mid[...] = cotangent[...].astype(F32) + sums.total()
    sums.finish()
    b = branch[...]
    c_b = lax.rsqrt(mean_of(b * b) + EPSILON)
    gdy = gain_attn[...] * d_mid[...]
    db[at128(z * 256 + k * rows)] = (
        c_b * gdy - b * (c_b * c_b * c_b * mean_of(b * gdy))
    ).astype(BF16)
    gather_b = Gather(place, Rows(db), zs.at[1], zr.at[1], cs.at[1], cr.at[1])
    gather_b.start()
    gn_own[...] = jnp.zeros((8, width), F32)
    gn_own[2:3, :] = jnp.sum(d_mid[...] * b * c_b, axis=0, keepdims=True)
    gn_own[3:4, :] = gm_part[...]

    for name in ("wo", "raw", "tab", "x", "qkv", "probs", "qk", "v", "att"):
        loads[name].wait()

    def attended_step(s, carry):
        c = place.order(s)
        gather_b.ready(c)
        part = dot_rt(db[chunk_rows(c)], stage_d[...]).astype(BF16)
        datt[:, at128(c * rows)] = part.reshape(2, rows, cols)
        return carry

    gather_b.arrive_first()
    lax.fori_loop(0, 2, attended_step, 0)

    for i in range(3):
        send_part(0, i, st_dn, rc_dn).wait_recv()
    parts = [rc_dn.at[0], rc_dn.at[1], rc_dn.at[2], st_dn.at[3]]
    gather_b.arrive_second()
    copies = [
        pltpu.make_async_copy(src, ms.at[pl.ds(256 * i, 256)], sum_sem.at[i])
        for i, src in enumerate(parts)
    ]
    for copy in copies:
        copy.start()
    for copy in copies:
        copy.wait()

    def add_down(t, carry):
        lanes = at128(t * 512, 512)
        acc = ms[0:256, lanes].astype(F32)
        for i in range(1, 4):
            acc = acc + ms[256 * i : 256 * i + 256, lanes].astype(F32)
        dm[0:256, lanes] = acc.astype(BF16)
        return carry

    lax.fori_loop(0, 4, add_down, 0)
    down_done = dm.at[pl.ds(0, 256)]
    fin_down = remote(down_done, o_down, fin_send.at[0], fin_recv.at[0], down_to)
    keep_down = pltpu.make_async_copy(down_done, o_down, fin_loc.at[0])
    pl.when(down_moves)(lambda: fin_down.start())
    pl.when(jnp.logical_not(down_moves))(lambda: keep_down.start())

    lax.fori_loop(2, 3, attended_step, 0)
    gather_b.arrive_third()
    lax.fori_loop(3, 4, attended_step, 0)

    def attend(s, carry):
        there = at128(s * 512, 512)
        for h in range(2):
            lanes = slice(128 * h, 128 * h + 128)
            more = slice(512 + 128 * h, 640 + 128 * h)
            vals = slice(768 + 128 * h, 896 + 128 * h)
            low_p = wu[at128((2 * s + h) * 512, 512), 0:512]
            grad = datt[s, :, lanes]
            q = wu[there, more]
            key = wu[at128(1024 + s * 512, 512), more]
            value = wu[there, vals]
            d_value = dot_lt(low_p, grad).astype(BF16)
            d_probs = dot_rt(grad, value)
            pr32 = low_p.astype(F32)
            delta = jnp.sum(pr32 * d_probs, axis=1, keepdims=True)
            d_scores = (pr32 * (d_probs - delta)).astype(BF16)
            d_q = dot(d_scores, key) * (HD ** -0.5)
            d_k = dot_lt(d_scores, q) * (HD ** -0.5)
            for i, d in enumerate((d_q, d_k)):
                dy[i, s, :, lanes] = d * tab[0, s] - pltpu.roll(d, 64, 1) * tab[1, s]
            for c in range(LINE):
                ga[c * 256 + s * rows : c * 256 + s * rows + rows, vals.start - 256 : vals.stop - 256] = (
                    d_value[c * rows : c * rows + rows]
                )
        return carry

    for s in range(2):
        attend(s, 0)

    def dots_step(c, carry):
        there = at128(c * rows)
        pick = lax.broadcasted_iota(jnp.int32, (8, cols), 0)
        acc = jnp.zeros((8, 2 * rows), F32)
        for i in range(2):
            part = (raw[i, :, there] * dy[i, :, there]).reshape(2 * rows, cols) * gains_qk[i : i + 1]
            acc = acc + exact((pick == i).astype(F32), part, ((1,), (1,)))
        sq_own[c] = acc
        return carry

    lax.fori_loop(0, LINE, dots_step, 0)
    pair_sq = remote(sq_own, sq_pair, as_.at[0], ar.at[0], place.partner)
    pair_sq.start()
    pair_sq.wait_recv()
    sq_both[...] = sq_own[...] + sq_pair[...]

    def line_sq(step, source):
        return remote(
            sq_both, sq_line.at[source], as_.at[step], ar.at[1 + source], place.line((z + step) % LINE)
        )

    for step in range(1, LINE):
        line_sq(step, z).start()
    for step in range(1, LINE):
        line_sq(step, (z + step) % LINE).wait_recv()
    sq_line[z] = sq_both[...]

    def normalise(c, gains):
        there = at128(c * rows)
        means = ((sq_line[0, c] + sq_line[1, c]) + (sq_line[2, c] + sq_line[3, c])) / width
        now = scales[c]
        result = []
        for i in range(2):
            pick = (lax.broadcasted_iota(jnp.int32, (8, 128), 0) == i).astype(F32)
            scale = exact(now, pick, ((0,), (0,)))
            mean = exact(means, pick, ((0,), (0,)))
            gain_sum = []
            for h in range(2):
                lanes = slice(128 * h, 128 * h + 128)
                v = raw[i, :, there, lanes].reshape(2 * rows, 128)
                d = dy[i, :, there, lanes].reshape(2 * rows, 128)
                gain_sum.append(jnp.sum(d * v * scale, axis=0, keepdims=True))
                d = scale * gains_qk[i : i + 1, lanes] * d - v * (scale * scale * scale * mean)
                ga[chunk_rows(c), 256 * i + 128 * h : 256 * i + 128 * h + 128] = d.astype(BF16)
            result.append(gains[i] + jnp.concatenate(gain_sum, axis=1))
        return tuple(result)

    start = (jnp.zeros((1, cols), F32), jnp.zeros((1, cols), F32))
    gain_q, gain_k = lax.fori_loop(0, LINE, normalise, start)
    own_cols = at128(cols * (2 * z + k), cols)
    gn_own[0:1, own_cols] = gain_q
    gn_own[1:2, own_cols] = gain_k

    def token_step(s, carry):
        c = place.order(3 - s)
        left = ga[chunk_rows(c), 0:768]

        def body(t, inner):
            lanes = at128(t * 512, 512)
            term[:, :, lanes] = dot_rt(left, wg[lanes, 0:768]).reshape(2, rows, 512)
            return inner

        lax.fori_loop(0, 4, body, 0)
        sums.give(c, s)
        pl.when(s > 0)(lambda: sums.pass_on(place.order(4 - s), s + 1))
        return carry

    lax.fori_loop(0, 4, token_step, 0)
    sums.pass_on(z, 3)

    for n, i in enumerate(order):
        left = feature_rows(wd, chips[i])

        def three(t, carry, left=left):
            lanes = at128(t * 256, 256)
            stage[0, :, lanes] = dot_lt(left, ga[:, lanes]).astype(BF16)
            return carry

        lax.fori_loop(0, 3, three, 0)
        part = stage.at[0, :, pl.ds(0, 768)]
        copy = pltpu.make_async_copy(part, st_qkv.at[i], st_sem.at[3])
        copy.start()
        copy.wait()
        if i < 3:
            send_part(2, i, st_qkv, rc_qkv).start()

    for s in range(2):
        for c in range(LINE):
            dg[c * 256 + s * rows : c * 256 + s * rows + rows, 0:256] = (
                wu[1024 + s * 512 + c * rows : 1024 + s * 512 + c * rows + rows, 768:1024]
            )

    def outer(t, carry):
        lanes = at128(t * 512, 512)
        stage_d[:, lanes] = dot_lt(dg[:, 0:256], db[:, lanes]).astype(BF16)
        return carry

    lax.fori_loop(0, 4, outer, 0)
    copy = pltpu.make_async_copy(stage_d, st_out, st_sem.at[0])
    copy.start()
    copy.wait()

    def out_part(i):
        return remote(
            st_out.at[at128(64 * chips[i], 64)], rc_out.at[i], in_send.at[3, i], in_recv.at[3, i], near[i]
        )

    for i in range(3):
        out_part(i).start()

    def share(step, peer):
        return remote(gn_own, gn_in.at[step], gs.at[step], gr.at[step], peer)

    for step, peer in enumerate((place.partner, place.x, place.y)):
        copy = share(step, peer)
        copy.start()
        copy.wait()
        gn_own[...] = gn_own[...] + gn_in[step]

    def line_gain(step, source):
        return remote(
            gn_own, gn_in.at[3 + source], gs.at[2 + step], gr.at[3 + source],
            place.line((z + step) % LINE),
        )

    for step in range(1, LINE):
        line_gain(step, z).start()

    def to_owner(kind, src, dst):
        def go(c, core, device, there):
            return remote(
                src(c, core), there, al_send.at[kind, c, core], al_recv.at[kind, z, k], device
            )

        def each(action):
            for step in range(1, LINE):
                c = (z + step) % LINE
                action(go(c, k, place.line(c), dst.at[z, k]))
                action(go(c, 1 - k, place.cross(c), dst.at[z, k]))
            action(go(z, 1 - k, place.partner, dst.at[z, k]))

        here = pltpu.make_async_copy(src(z, k), dst.at[z, k], al_loc.at[kind])
        each(lambda copy: copy.start())
        here.start()

        def wait():
            here.wait()
            each(lambda copy: copy.wait_send())
            for step in range(LINE):
                c = (z + step) % LINE
                for core in (0, 1):
                    got = remote(
                        src(c, k), dst.at[c, core], al_send.at[kind, c, core], al_recv.at[kind, c, core],
                        place.partner,
                    )
                    if step == 0:
                        pl.when(k != core)(lambda got=got: got.wait_recv())
                    else:
                        got.wait_recv()

        return wait

    for i in range(3):
        send_part(1, i, st_gu, rc_gu).wait_recv()
    waits = []
    for m, (a, b2) in enumerate(((hid, ua), (dg, du))):
        slots = [a.at[pl.ds(0, 512)], a.at[pl.ds(512, 512)], b2.at[pl.ds(0, 512)], b2.at[pl.ds(512, 512)]]
        sources = [rc_gu.at[0, m], rc_gu.at[1, m], rc_gu.at[2, m], st_gu.at[3, m]]
        copies = [
            pltpu.make_async_copy(src, dst, sum_sem.at[4 + 4 * m + i])
            for i, (src, dst) in enumerate(zip(sources, slots))
        ]
        for copy in copies:
            copy.start()
        for copy in copies:
            copy.wait()

        def add_up(t, carry, a=a, b2=b2):
            there = at128(t * 128)
            acc = a[there].astype(F32) + a[at128(512 + t * 128)].astype(F32)
            acc = acc + b2[there].astype(F32) + b2[at128(512 + t * 128)].astype(F32)
            a[there] = acc.astype(BF16)
            return carry

        lax.fori_loop(0, 4, add_up, 0)
        waits.append(
            to_owner(
                m, lambda c, core, a=a: a.at[at128(c * 128 + core * 64, 64)], o_gu.at[m]
            )
        )

    o_tok[...] = (d_mid[...] + sums.total()).astype(BF16)
    sums.finish()

    for i in range(3):
        send_part(2, i, st_qkv, rc_qkv).wait_recv()
    lanes = pl.ds(0, 768)
    slots = [ua.at[pl.ds(0, 512), lanes], ua.at[pl.ds(512, 512), lanes],
             du.at[pl.ds(0, 512), lanes], du.at[pl.ds(512, 512), lanes]]
    sources = [rc_qkv.at[0], rc_qkv.at[1], rc_qkv.at[2], st_qkv.at[3]]
    copies = [
        pltpu.make_async_copy(src, dst, sum_sem.at[12 + i])
        for i, (src, dst) in enumerate(zip(sources, slots))
    ]
    for copy in copies:
        copy.start()
    for copy in copies:
        copy.wait()

    def add_qkv(t, carry):
        there, then = at128(t * 128), at128(512 + t * 128)
        acc = ua[there, 0:768].astype(F32) + ua[then, 0:768].astype(F32)
        acc = acc + du[there, 0:768].astype(F32) + du[then, 0:768].astype(F32)
        ua[there, 0:768] = acc.astype(BF16)
        return carry

    lax.fori_loop(0, 4, add_qkv, 0)
    waits.append(
        to_owner(2, lambda c, core: ua.at[at128(c * 128 + core * 64, 64), lanes], o_qkv)
    )

    for i in range(3):
        out_part(i).wait_recv()
    sources = [rc_out.at[0], rc_out.at[1], rc_out.at[2], st_out.at[at128(64 * p, 64)]]
    copies = [
        pltpu.make_async_copy(src, ms.at[pl.ds(64 * i, 64)], sum_sem.at[16 + i])
        for i, src in enumerate(sources)
    ]
    for copy in copies:
        copy.start()
    for copy in copies:
        copy.wait()
    acc = ms[0:64].astype(F32) + ms[64:128].astype(F32)
    acc = acc + ms[128:192].astype(F32) + ms[192:256].astype(F32)
    ms[256:320] = acc.astype(BF16)
    out_done = ms.at[pl.ds(256, 64)]
    fin_out = remote(out_done, o_out, fin_send.at[1], fin_recv.at[1], out_to)
    keep_out = pltpu.make_async_copy(out_done, o_out, fin_loc.at[1])
    pl.when(out_moves)(lambda: fin_out.start())
    pl.when(jnp.logical_not(out_moves))(lambda: keep_out.start())

    for step in range(1, LINE):
        line_gain(step, (z + step) % LINE).wait_recv()
    for step in range(1, LINE):
        line_gain(step, z).wait_send()
    total = gn_own[...]
    for step in range(1, LINE):
        total = total + gn_in[3 + (z + step) % LINE]
    o_gains[...] = total

    gather_b.finish()
    pair_sq.wait_send()
    for step in range(1, LINE):
        line_sq(step, z).wait_send()
    for i in range(3):
        send_part(0, i, st_dn, rc_dn).wait_send()
        send_part(1, i, st_gu, rc_gu).wait_send()
        send_part(2, i, st_qkv, rc_qkv).wait_send()
        out_part(i).wait_send()
    for wait in waits:
        wait()
    pl.when(down_moves)(lambda: fin_down.wait())
    pl.when(jnp.logical_not(down_moves))(lambda: keep_down.wait())
    pl.when(out_moves)(lambda: fin_out.wait())
    pl.when(jnp.logical_not(out_moves))(lambda: keep_out.wait())


def run_backward(gains_qk, gain_attn, d_mlp, cotangent, branch, scales, gm_part, kept):
    shape = jax.ShapeDtypeStruct
    dma = pltpu.SemaphoreType.DMA
    flat = [(2048, 768), (256, 2048), (2048, 1024), (2048, 1024), (1024, 2048), (1024, 2048), (1024, 2048),
            (1024, 1024), (1024, 1024), (1024, 1024), None, (3072, 256), (2048, 512), (1024, 256), None]
    kept = [a if s is None else a.reshape(s) for a, s in zip(kept, flat)]
    results = [
        shape((256, 2048), BF16),
        shape((64, 2048), BF16),
        shape((2, 4, 2, 64, 1024), BF16),
        shape((4, 2, 64, 768), BF16),
    ]
    transit = [
        shape((4, 256, 2048), BF16),
        shape((3, 256, 2048), BF16),
        shape((4, 2, 512, 1024), BF16),
        shape((3, 2, 512, 1024), BF16),
        shape((4, 512, 768), BF16),
        shape((3, 512, 768), BF16),
        shape((256, 2048), BF16),
        shape((3, 64, 2048), BF16),
    ]
    wide, square = pltpu.VMEM((1024, 2048), BF16), pltpu.VMEM((1024, 1024), BF16)
    tall = pltpu.VMEM((2048, 1024), BF16)
    rows = pltpu.VMEM((4, 128, 2048), BF16)
    small = pltpu.VMEM((4, 8, 256), F32)
    return pl.pallas_call(
        backward_kernel,
        name="backward",
        out_shape=[shape((128, 2048), BF16), shape((8, 2048), F32)] + results + transit,
        in_specs=[vmem_spec()] * 7 + [any_spec()] * len(kept),
        out_specs=[vmem_spec()] * 2 + [any_spec()] * (len(results) + len(transit)),
        scratch_shapes=[
            wide, tall, tall, square, square, square, wide, square, square, wide, wide,
            pltpu.VMEM((2, 2, 512, 256), F32),
            pltpu.VMEM((2, 2, 512, 128), F32),
            pltpu.VMEM((2, 512, 256), BF16),
            pltpu.VMEM((2, 2, 512, 256), F32),
            pltpu.VMEM((2, 128, 2048), F32),
            rows,
            rows,
            pltpu.VMEM((2, 128, 2048), F32),
            pltpu.VMEM((128, 2048), F32),
            rows,
            rows,
            small,
            small,
            small,
            pltpu.VMEM((4, 4, 8, 256), F32),
            pltpu.VMEM((8, 2048), F32),
            pltpu.VMEM((7, 8, 2048), F32),
            pltpu.VMEM((128, 2048), F32),
            pltpu.VMEM((2, 512, 1024), BF16),
            pltpu.VMEM((256, 2048), BF16),
            dma((16,)),
            dma((2, 2, 4)), dma((2, 4)), dma((2, 4)), dma((2, 4)),
            dma((4,)), dma((4,)), dma((4,)), dma((4,)),
            dma((4,)), dma((5,)),
            dma((6,)), dma((7,)),
            dma((4, 3)), dma((4, 3)),
            dma((4,)), dma((20,)),
            dma((2,)), dma((2,)), dma((2,)),
            dma((3, 4, 2)), dma((3, 4, 2)), dma((3,)),
        ],
        compiler_params=pltpu.CompilerParams(
            collective_id=1, has_side_effects=True, vmem_limit_bytes=64 * 1024 * 1024
        ),
    )(gains_qk, gain_attn, d_mlp, cotangent, branch, scales, gm_part, *kept)[:6]


def shards_kernels(tokens, block_pairs, w_query, w_key, w_value, w_out, w_gate, w_up, w_down,
                   gain_query, gain_key, gain_attn, gain_mlp, cotangent):
    z = lax.axis_index("ctx")
    f = lax.axis_index("fsdp")
    start = 256 * (2 * z + f % 2)
    gains_qk = jnp.stack([
        lax.dynamic_slice_in_dim(gain_query, start, 256), lax.dynamic_slice_in_dim(gain_key, start, 256)
    ])
    out, d_mlp, gm_part, branch, scales, *kept = run_forward(
        block_pairs, gains_qk, gain_attn[None], gain_mlp[None], tokens[0], cotangent[0],
        (w_query, w_key, w_value, w_out, w_gate, w_up, w_down),
    )
    d_tokens, gains, down, out_rows, gate_up, qkv = run_backward(
        gains_qk, gain_attn[None], d_mlp, cotangent[0], branch, scales, gm_part, kept
    )
    gate_up = gate_up.reshape(2, 4, 2, 64, 4, 256).transpose(0, 3, 4, 2, 1, 5).reshape(2, 64, 8192)
    qkv = qkv.reshape(4, 2, 64, 3, 256).transpose(3, 2, 0, 1, 4).reshape(3, 64, 2048)
    gains = lax.dynamic_slice_in_dim(gains, 64 * (8 * z + f), 64, 1)
    return (
        out[None],
        d_tokens[None],
        qkv[0].astype(F32),
        qkv[1].astype(F32),
        qkv[2].astype(F32),
        out_rows.astype(F32),
        gate_up[0].astype(F32),
        gate_up[1].astype(F32),
        down.astype(F32),
        gains[0],
        gains[1],
        gains[2],
        gains[3],
    )


def shards(*arrays):
    tokens, w_query, w_down = arrays[0], arrays[2], arrays[8]
    here = (lax.axis_size("ctx"), lax.axis_size("fsdp"), tokens.shape, w_query.shape, w_down.shape)
    if here == (LINE, 2 * PLANE, (1, 128, 2048), (256, 2048), (1024, 2048)):
        return shards_kernels(*arrays)
    return shards_general(*arrays)


def solution(mesh):
    in_specs = (
        P("fsdp", "ctx", None),
        P("fsdp", None),
        P("fsdp", None),
        P("fsdp", None),
        P("fsdp", None),
        P("fsdp", None),
        P("fsdp", None),
        P("fsdp", None),
        P("fsdp", None),
        P(),
        P(),
        P(),
        P(),
        P("fsdp", "ctx", None),
    )
    out_specs = (
        P("fsdp", "ctx", None),
        P("fsdp", "ctx", None),
        P(("ctx", "fsdp"), None),
        P(("ctx", "fsdp"), None),
        P(("ctx", "fsdp"), None),
        P(("ctx", "fsdp"), None),
        P(("ctx", "fsdp"), None),
        P(("ctx", "fsdp"), None),
        P(("ctx", "fsdp"), None),
        P(("ctx", "fsdp")),
        P(("ctx", "fsdp")),
        P(("ctx", "fsdp")),
        P(("ctx", "fsdp")),
    )
    return jax.shard_map(shards, mesh=mesh, in_specs=in_specs, out_specs=out_specs, check_vma=False)
```

```python
import math

import jax
import jax.numpy as jnp
from jax import lax
from jax.experimental import pallas as pl
from jax.experimental.pallas import tpu as pltpu
from jax.sharding import PartitionSpec as P

HD = 128


EPSILON = 1e-06
ROPE_BASE = 500000.0
NEGATIVE = -1e30


def norm_scale(values, gain_vec):
    return (
        values * lax.rsqrt(jnp.mean(values * values, axis=-1, keepdims=True) + EPSILON) * gain_vec
    )


def turn_half(values, cosine, sine):
    half_size = values.shape[-1] // 2
    turned = jnp.concatenate([-values[..., half_size:], values[..., :half_size]], axis=-1)
    return values * cosine + turned * sine


def angle_tables(positions, head_size):
    half_size = head_size // 2
    frequency = jnp.power(ROPE_BASE, -(jnp.arange(half_size).astype(jnp.float32) * 2.0 / head_size))
    angles = positions.astype(jnp.float32)[:, None] * frequency[None, :]
    angles = jnp.concatenate([angles, angles], axis=-1)
    return (jnp.cos(angles)[:, None, :], jnp.sin(angles)[:, None, :])


def row_positions(row_ids, pair_row, block_rows, ctx_count):
    rank_of = row_ids // (2 * block_rows)
    second = row_ids // block_rows % 2
    offset = row_ids % block_rows
    rank_match = (rank_of[:, None] == jnp.arange(ctx_count, dtype=jnp.int32)[None, :]).astype(
        jnp.int32
    )
    chosen = jnp.sum(rank_match * pair_row[None, :], axis=1)
    block_index = jnp.where(second == 0, chosen, 2 * ctx_count - 1 - chosen)
    return block_index * block_rows + offset


def times_transpose(left, right):
    return lax.dot_general(
        left, right, (((1,), (1,)), ((), ())), preferred_element_type=jnp.float32
    )


def transpose_times(left, right):
    return lax.dot_general(
        left, right, (((0,), (0,)), ((), ())), preferred_element_type=jnp.float32
    )


def activate(gate_in, up_in):
    return jax.nn.silu(gate_in) * up_in


def spread_rows(values, outer, inner):
    rows, width = values.shape
    return (
        values.reshape(outer, inner, rows // (outer * inner), width)
        .transpose(1, 0, 2, 3)
        .reshape(rows, width)
    )


def shards_general(
    tokens,
    block_pairs,
    w_query,
    w_key,
    w_value,
    w_out,
    w_gate,
    w_up,
    w_down,
    gain_query,
    gain_key,
    gain_attn,
    gain_mlp,
    cotangent,
):
    bf16 = jnp.bfloat16
    f32 = jnp.float32
    local_rows = tokens.shape[1]
    block_rows = local_rows // 2
    width = w_query.shape[1]
    hidden_width = w_gate.shape[1]
    ctx_count = lax.axis_size("ctx")
    fsdp_count = lax.axis_size("fsdp")
    ctx_index = lax.axis_index("ctx")
    seq = local_rows * ctx_count
    cols = width // ctx_count
    heads = cols // HD
    strip = hidden_width // (ctx_count * fsdp_count)
    hid = strip * fsdp_count
    scale = HD ** (-0.5)

    def ctx_cols(w):
        return lax.dynamic_slice_in_dim(w, ctx_index * cols, cols, 1)

    def ctx_strips(w):
        parts = w.reshape(w.shape[0], fsdp_count, ctx_count, strip)
        return lax.dynamic_index_in_dim(parts, ctx_index, 2, keepdims=False).reshape(w.shape[0], hid)

    token_rows = tokens[0]
    x_all = lax.all_gather(token_rows, "ctx", axis=0, tiled=True)
    qkv_w = lax.all_gather(
        jnp.concatenate([ctx_cols(w_query), ctx_cols(w_key), ctx_cols(w_value)], axis=1),
        "fsdp", axis=0, tiled=True,
    )
    out_w = lax.dynamic_slice_in_dim(
        lax.all_gather(w_out, "fsdp", axis=0, tiled=True), ctx_index * cols, cols, 0
    )
    gate_w = lax.all_gather(ctx_strips(w_gate), "fsdp", axis=0, tiled=True)
    up_w = lax.all_gather(ctx_strips(w_up), "fsdp", axis=0, tiled=True)
    down_w = lax.all_gather(
        lax.dynamic_slice_in_dim(w_down, ctx_index * strip, strip, 0), "fsdp", axis=0, tiled=True
    )

    pos = row_positions(jnp.arange(seq, dtype=jnp.int32), block_pairs[0], block_rows, ctx_count)
    cosine, sine = angle_tables(pos, HD)
    mask = pos[None, :] <= pos[:, None]
    gain_q = lax.dynamic_slice_in_dim(gain_query, ctx_index * cols, cols)
    gain_k = lax.dynamic_slice_in_dim(gain_key, ctx_index * cols, cols)

    qkv = jnp.dot(x_all, qkv_w, preferred_element_type=f32)
    q_raw, k_raw, v_raw = qkv[:, :cols], qkv[:, cols : 2 * cols], qkv[:, 2 * cols :]
    squares = jnp.stack([jnp.sum(q_raw * q_raw, axis=1), jnp.sum(k_raw * k_raw, axis=1)])
    squares = lax.psum(squares, "ctx")
    scales = lax.rsqrt(squares / width + EPSILON)
    c_q, c_k = scales[0][:, None], scales[1][:, None]

    def rope(v):
        return turn_half(v.reshape(seq, heads, HD), cosine, sine)

    def rope_back(w):
        w = w.reshape(seq, heads, HD)
        u = w * sine
        half = HD // 2
        turned = jnp.concatenate([u[..., half:], -u[..., :half]], axis=-1)
        return (w * cosine + turned).reshape(seq, cols)

    queries = rope(q_raw * c_q * gain_q).astype(bf16)
    keys = rope(k_raw * c_k * gain_k).astype(bf16)
    values = v_raw.astype(bf16).reshape(seq, heads, HD)
    scores = jnp.einsum("qhd,khd->hqk", queries, keys, preferred_element_type=f32) * scale
    scores = jnp.where(mask[None], scores, NEGATIVE)
    exponent = jnp.exp(scores - jnp.max(scores, axis=-1, keepdims=True))
    probs = exponent / jnp.sum(exponent, axis=-1, keepdims=True)
    prob_low = probs.astype(bf16)
    attended = (
        jnp.einsum("hqk,khd->qhd", prob_low, values, preferred_element_type=f32)
        .reshape(seq, cols)
        .astype(bf16)
    )
    branch = lax.psum_scatter(
        jnp.dot(attended, out_w, preferred_element_type=f32).astype(bf16),
        "ctx", scatter_dimension=0, tiled=True,
    ).astype(f32)
    mid = token_rows.astype(f32) + norm_scale(branch, gain_attn)
    mid_all = lax.all_gather(mid.astype(bf16), "ctx", axis=0, tiled=True)
    gate_act = jnp.dot(mid_all, gate_w, preferred_element_type=f32)
    up_act = jnp.dot(mid_all, up_w, preferred_element_type=f32)
    hidden = activate(gate_act, up_act).astype(bf16)
    mlp_out = lax.psum_scatter(
        jnp.dot(hidden, down_w, preferred_element_type=f32).astype(bf16),
        "ctx", scatter_dimension=0, tiled=True,
    ).astype(f32)
    output = (mid + norm_scale(mlp_out, gain_mlp)).astype(bf16)

    d_output = cotangent[0].astype(f32)
    unused_mlp, pull_mlp = jax.vjp(norm_scale, mlp_out, gain_mlp)
    d_mlp, grad_gm = pull_mlp(d_output)
    d_mlp_all = lax.all_gather(d_mlp.astype(bf16), "ctx", axis=0, tiled=True)
    d_hidden = times_transpose(d_mlp_all, down_w)
    unused_act, pull_act = jax.vjp(activate, gate_act, up_act)
    d_gate, d_up = pull_act(d_hidden)
    d_gate = d_gate.astype(bf16)
    d_up = d_up.astype(bf16)
    d_mid_part = times_transpose(d_gate, gate_w) + times_transpose(d_up, up_w)
    d_mid = d_output + lax.psum_scatter(
        d_mid_part.astype(bf16), "ctx", scatter_dimension=0, tiled=True
    ).astype(f32)

    down_sum = lax.psum_scatter(
        transpose_times(hidden, d_mlp_all).astype(bf16), "fsdp", scatter_dimension=0, tiled=True
    )
    moves = [
        (z * fsdp_count + f, f * ctx_count + z)
        for z in range(ctx_count)
        for f in range(fsdp_count)
    ]
    grad_down = lax.ppermute(down_sum, ("ctx", "fsdp"), moves).astype(f32)

    def column_grad(left, right):
        part = transpose_times(left, right).astype(bf16)
        mine = lax.psum_scatter(
            spread_rows(part, ctx_count, fsdp_count), "fsdp", scatter_dimension=0, tiled=True
        )
        mine = mine.reshape(ctx_count, mine.shape[0] // ctx_count, mine.shape[1])
        return lax.all_to_all(mine, "ctx", 0, 0, tiled=True)

    gate_up = column_grad(mid_all, jnp.concatenate([d_gate, d_up], axis=1))
    rows = gate_up.shape[1]

    def from_strips(part):
        return (
            part.reshape(ctx_count, rows, fsdp_count, strip)
            .transpose(1, 2, 0, 3)
            .reshape(rows, hidden_width)
            .astype(f32)
        )

    unused_branch, pull_branch = jax.vjp(norm_scale, branch, gain_attn)
    d_branch, grad_ga = pull_branch(d_mid)
    d_branch_all = lax.all_gather(d_branch.astype(bf16), "ctx", axis=0, tiled=True)
    d_attended = times_transpose(d_branch_all, out_w).astype(bf16).reshape(seq, heads, HD)
    grad_out = lax.psum_scatter(
        transpose_times(attended, d_branch_all).astype(bf16),
        "fsdp", scatter_dimension=0, tiled=True,
    ).astype(f32)

    d_values = jnp.einsum("hqk,qhd->khd", prob_low, d_attended, preferred_element_type=f32)
    d_values = d_values.astype(bf16).reshape(seq, cols)
    d_probs = jnp.einsum("qhd,khd->hqk", d_attended, values, preferred_element_type=f32)
    delta = jnp.sum(probs * d_probs, axis=-1, keepdims=True)
    d_scores = (probs * (d_probs - delta)).astype(bf16)
    d_queries = jnp.einsum("hqk,khd->qhd", d_scores, keys, preferred_element_type=f32) * scale
    d_keys = jnp.einsum("hqk,qhd->khd", d_scores, queries, preferred_element_type=f32) * scale
    dy_q = rope_back(d_queries)
    dy_k = rope_back(d_keys)
    dots = jnp.stack([
        jnp.sum(q_raw * gain_q * dy_q, axis=1), jnp.sum(k_raw * gain_k * dy_k, axis=1)
    ])
    dots = lax.psum(dots, "ctx") / width
    d_q = c_q * gain_q * dy_q - q_raw * (c_q * c_q * c_q * dots[0][:, None])
    d_k = c_k * gain_k * dy_k - k_raw * (c_k * c_k * c_k * dots[1][:, None])
    d_qkv = jnp.concatenate([d_q.astype(bf16), d_k.astype(bf16), d_values], axis=1)
    d_tokens = d_mid + lax.psum_scatter(
        times_transpose(d_qkv, qkv_w).astype(bf16), "ctx", scatter_dimension=0, tiled=True
    ).astype(f32)
    qkv_grad = column_grad(x_all, d_qkv).transpose(1, 0, 2)
    sum_gqk = lax.psum_scatter(
        jnp.stack([jnp.sum(dy_q * q_raw * c_q, axis=0), jnp.sum(dy_k * k_raw * c_k, axis=0)]),
        "fsdp", scatter_dimension=1, tiled=True,
    )
    sum_gam = lax.psum_scatter(
        jnp.stack([grad_ga, grad_gm]), ("ctx", "fsdp"), scatter_dimension=1, tiled=True
    )

    def whole(part):
        return part.reshape(part.shape[0], width).astype(f32)

    return (
        output[None],
        d_tokens.astype(bf16)[None],
        whole(qkv_grad[:, :, :cols]),
        whole(qkv_grad[:, :, cols : 2 * cols]),
        whole(qkv_grad[:, :, 2 * cols :]),
        grad_out,
        from_strips(gate_up[:, :, :hid]),
        from_strips(gate_up[:, :, hid:]),
        grad_down,
        sum_gqk[0],
        sum_gqk[1],
        sum_gam[0],
        sum_gam[1],
    )


MESH = pl.DeviceIdType.MESH
BF16 = jnp.bfloat16
F32 = jnp.float32
LINE = 4
PLANE = 4


def dot(left, right):
    return lax.dot_general(left, right, (((1,), (0,)), ((), ())), preferred_element_type=F32)


def dot_rt(left, right):
    return lax.dot_general(left, right, (((1,), (1,)), ((), ())), preferred_element_type=F32)


def dot_lt(left, right):
    return lax.dot_general(left, right, (((0,), (0,)), ((), ())), preferred_element_type=F32)


def exact(left, right, dims):
    return lax.dot_general(
        left, right, (dims, ((), ())), precision=lax.Precision.HIGHEST, preferred_element_type=F32
    )


def remote(src, dst, send, recv, device):
    return pltpu.make_async_remote_copy(
        src_ref=src, dst_ref=dst, send_sem=send, recv_sem=recv, device_id=device, device_id_type=MESH
    )


def at128(i, step=128):
    return pl.ds(i if isinstance(i, int) else pl.multiple_of(i, step), step)


class Place:
    def __init__(self):
        z = lax.axis_index("ctx")
        f = lax.axis_index("fsdp")
        self.z, self.f = z, f
        self.p, self.k = f // 2, f % 2
        self.p_x = self.p + 1 - 2 * (self.p % 2)
        self.p_y = (self.p + 2) % PLANE
        self.p_d = PLANE - 1 - self.p
        self.partner = (z, 2 * self.p + 1 - self.k)
        self.x = (z, 2 * self.p_x + self.k)
        self.y = (z, 2 * self.p_y + self.k)
        self.d = (z, 2 * self.p_d + self.k)
        self.ends = z // 3 + (3 - z) // 3

    def line(self, c):
        return (c, self.f)

    def order(self, s):
        z, e, t = self.z, self.ends, s // 3
        end = z + s * (1 - 2 * (z // 3))
        mid = (1 - t) * (z + (3 * s * s - 5 * s) // 2) + t * 3 * (2 - z)
        return e * end + (1 - e) * mid

    def cross(self, c):
        return (c, 2 * self.p + 1 - self.k)

    def barrier(self, more=(), senders=()):
        sem = pltpu.get_barrier_semaphore()

        def greet(peer):
            pl.semaphore_signal(sem, inc=1, device_id=peer, device_id_type=MESH)

        peers = [self.partner, self.x, self.y] + list(more)
        peers += [self.line((self.z + step) % LINE) for step in range(1, LINE)]
        for peer in peers:
            greet(peer)
        count = len(peers)
        for here, peer in senders:
            pl.when(here)(lambda peer=peer: greet(peer))
            count = count + here.astype(jnp.int32)
        pl.semaphore_wait(sem, count)


class Gather:
    def __init__(self, place, buf, z_send, z_recv, c_send, c_recv):
        self.pl, self.buf = place, buf
        self.sems = z_send, z_recv, c_send, c_recv

    def to_line(self, c, target, way):
        z_send, z_recv, _, _ = self.sems
        part = self.buf.at[c, self.pl.k]
        return remote(part, part, z_send.at[way, c], z_recv.at[c], self.pl.line(target))

    def to_core(self, c):
        _, _, c_send, c_recv = self.sems
        part = self.buf.at[c, self.pl.k]
        return remote(part, part, c_send.at[c], c_recv.at[c], self.pl.partner)

    def from_core(self, c):
        _, _, c_send, c_recv = self.sems
        part = self.buf.at[c, 1 - self.pl.k]
        return remote(part, part, c_send.at[c], c_recv.at[c], self.pl.partner)

    def start(self):
        z = self.pl.z
        pl.when(z < LINE - 1)(lambda: self.to_line(z, z + 1, 0).start())
        pl.when(z > 0)(lambda: self.to_line(z, z - 1, 1).start())
        self.to_core(z).start()

    def arrive(self, c):
        z = self.pl.z
        self.to_line(c, z, 0).wait_recv()
        pl.when(jnp.logical_and(c < z, z < LINE - 1))(lambda: self.to_line(c, z + 1, 0).start())
        pl.when(jnp.logical_and(c > z, z > 0))(lambda: self.to_line(c, z - 1, 1).start())
        self.to_core(c).start()

    def arrive_first(self):
        self.arrive(self.pl.order(1))
        pl.when(self.pl.ends == 0)(lambda: self.arrive(self.pl.order(2)))

    def arrive_second(self):
        self.arrive(self.pl.order(3 - self.pl.ends))

    def arrive_third(self):
        pl.when(self.pl.ends == 1)(lambda: self.arrive(self.pl.order(3)))

    def ready(self, c):
        self.from_core(c).wait_recv()

    def finish(self):
        z = self.pl.z

        def body(c, carry):
            pl.when(jnp.logical_and(c <= z, z < LINE - 1))(
                lambda: self.to_line(c, z, 0).wait_send()
            )
            pl.when(jnp.logical_and(c >= z, z > 0))(lambda: self.to_line(c, z, 1).wait_send())
            self.to_core(c).wait_send()
            return carry

        lax.fori_loop(0, LINE, body, 0)


class RowSum:
    def __init__(self, place, h, buffers, sems):
        self.pl, self.h = place, h
        self.term, self.pair_out, self.pair_in, self.keep, self.mine, self.line_out, self.line_in = buffers
        self.p_send, self.p_recv, self.l_send, self.l_recv = sems

    def pair(self, c):
        h = self.h
        return remote(
            self.pair_out.at[h, c], self.pair_in.at[h, c], self.p_send.at[h, c], self.p_recv.at[h, c],
            self.pl.partner,
        )

    def line(self, c, slot, target):
        h = self.h
        return remote(
            self.line_out.at[h, c], self.line_in.at[h, slot], self.l_send.at[h, c],
            self.l_recv.at[h, slot], self.pl.line(target),
        )

    def mate(self):
        return self.pl.z + 1 - 2 * (self.pl.z % 2)

    def give(self, c, s):
        h, k = self.h, self.pl.k
        self.pair_out[h, c] = self.term[1 - k].astype(BF16)
        self.pair(c).start()
        self.keep[h, s % 2] = self.term[k]

    def pass_on(self, c, s):
        h, z = self.h, self.pl.z
        near = c // 2 == z // 2
        end = self.pl.ends == 1
        self.pair(c).wait_recv()

        @pl.when(c == z)
        def _():
            self.mine[h] = self.keep[h, s % 2] + self.pair_in[h, c].astype(F32)

        @pl.when(c != z)
        def _():
            self.line_out[h, c] = (self.keep[h, s % 2] + self.pair_in[h, c].astype(F32)).astype(BF16)

        pl.when(jnp.logical_and(c != z, near))(lambda: self.line(c, z, c).start())
        pl.when(jnp.logical_and(jnp.logical_not(near), end))(
            lambda: self.line(c, 2 * c - 3 * (1 - z // 2), self.mate()).start()
        )

    def relay(self, far):
        h, z = self.h, self.pl.z

        @pl.when(self.pl.ends == 0)
        def _():
            c = 3 * (2 - z) if far else 3 - z
            slot = 2 * c - 3 * (2 - z)
            self.line(c, slot, z).wait_recv()
            self.line_out[h, c] = (
                self.line_out[h, c].astype(F32) + self.line_in[h, slot].astype(F32)
            ).astype(BF16)
            self.line(c, z, c).start()

    def total(self):
        h, z = self.h, self.pl.z
        result = self.mine[h]
        for source in (self.mate(), 2 - z // 2):
            self.line(source, source, source).wait_recv()
            result = result + self.line_in[h, source].astype(F32)
        return result

    def finish(self):
        z = self.pl.z

        def body(c, carry):
            self.pair(c).wait_send()
            pl.when(c != z)(lambda: self.line(c, z, c).wait_send())
            return carry

        lax.fori_loop(0, LINE, body, 0)


class Ring:
    def __init__(self, place, buf, rows, send, recv):
        self.pl, self.buf, self.rows = place, buf, rows
        self.send, self.recv = send, recv

    def block(self, p):
        return self.buf.at[at128(p * self.rows, self.rows)]

    def half(self, p, i):
        size = self.rows // 2
        return self.buf.at[at128(p * self.rows + i * size, size)]

    def own(self, way):
        part = self.block(self.pl.p)
        return remote(part, part, self.send.at[way], self.recv.at[way], (self.pl.x, self.pl.y)[way])

    def far(self, i):
        part = self.half((self.pl.p_x, self.pl.p_y)[i], i)
        return remote(part, part, self.send.at[2 + i], self.recv.at[2 + i], (self.pl.y, self.pl.x)[i])

    def start(self):
        self.own(0).start()
        self.own(1).start()

    def forward(self):
        for i in range(2):
            part = self.block((self.pl.p_x, self.pl.p_y)[i])
            remote(part, part, self.send.at[i], self.recv.at[i], (self.pl.x, self.pl.y)[i]).wait_recv()
            self.far(i).start()

    def ready(self):
        for i in range(2):
            part = self.half(self.pl.p_d, i)
            remote(part, part, self.send.at[2 + i], self.recv.at[2 + i], self.pl.x).wait_recv()

    def finish(self):
        for i in range(2):
            self.own(i).wait_send()
            self.far(i).wait_send()


def scale_columns(totals, rows, which):
    pick = (lax.broadcasted_iota(jnp.int32, (8, 128), 0) == which).astype(F32)
    return exact(totals[:, rows], pick, ((0,), (0,)))


def forward_kernel(
    pairs, gains_qk, gain_attn, gain_mlp, tokens, cotangent,
    w_query, w_key, w_value, w_out, w_gate, w_up, w_down,
    o_out, o_dmlp, o_gm, o_branch, o_tot,
    o_qkv, o_wo, o_g, o_u, o_dn, o_x, o_m, o_ga, o_ua, o_hid, o_raw, o_heads, o_probs, o_att, o_tab,
    qkv, wo, wg, wu, wd, xs, ms, ga, ua, hid, raw, heads, probs, att, tab, posr, posc,
    term, pair_out, pair_in, keep, mine, line_out, line_in,
    sq_own, sq_pair, sq_both, sq_line, mid,
    loc_sem, swap_send, swap_recv, ring_send, ring_recv, wo_send, wo_recv,
    zs, zr, cs, cr, ps, pr, ls, lr, ts, tr, as_, ar, out_sem,
):
    place = Place()
    z, f, p, k = place.z, place.f, place.p, place.k
    rows = 128
    width = 2048
    cols = 256
    seq = 512
    place.barrier()

    def own_rows(n):
        return at128(n * (2 * p + k), n)

    def strips(core):
        return [1024 * (2 * q + core) + 256 * z for q in range(PLANE)]

    local, swap = {}, {}

    def split(name, w, buf, sources, first):
        local[name], swap[name] = [], []
        for i, (mine, theirs) in enumerate(sources):
            dst = buf.at[own_rows(256), pl.ds(256 * i + first[1], 256)]
            local[name].append(
                pltpu.make_async_copy(w.at[:, at128(mine, 256)], dst, loc_sem.at[first[0] + i])
            )
            swap[name].append(
                remote(
                    w.at[:, at128(theirs, 256)], dst, swap_send.at[first[0] + i],
                    swap_recv.at[first[0] + i], place.partner,
                )
            )

    head_cols = [(256 * (2 * z + k), 256 * (2 * z + 1 - k))]
    hid_cols = list(zip(strips(k), strips(1 - k)))
    split("q", w_query, qkv, head_cols, (0, 0))
    split("k", w_key, qkv, head_cols, (1, 256))
    split("v", w_value, qkv, head_cols, (2, 512))
    split("g", w_gate, wg, hid_cols, (3, 0))
    split("u", w_up, wu, hid_cols, (7, 0))

    def begin(*names):
        for name in names:
            for a, b in zip(local[name], swap[name]):
                b.start()
                a.start()

    def settle(*names):
        for name in names:
            for a, b in zip(local[name], swap[name]):
                a.wait()
                b.wait_recv()

    dx, dy = (p % 2 + z % 2) % 2, (p // 2 + z // 2) % 2
    top, low = wo.at[pl.ds(0, 128)], wo.at[pl.ds(128, 128)]
    wo_copy = pltpu.make_async_copy(w_out, wo, loc_sem.at[12])

    def wo_first(i, device):
        rows_i = pl.ds(128 * i, 128)
        return remote(w_out.at[rows_i], wo.at[rows_i], wo_send.at[i], wo_recv.at[i], device)

    def wo_send_to(i, part, device):
        return remote(part, part, wo_send.at[i], wo_recv.at[i], device)

    is_source = jnp.logical_and(dx == 0, dy == 0)
    is_x = jnp.logical_and(dx == 1, dy == 0)
    is_y = jnp.logical_and(dx == 0, dy == 1)
    is_d = jnp.logical_and(dx == 1, dy == 1)

    @pl.when(is_source)
    def _():
        wo_copy.start()
        wo_first(0, place.x).start()
        wo_first(1, place.y).start()

    begin("q", "k", "v")
    xs[z, k] = tokens[...]
    gather_x = Gather(place, xs, zs.at[0], zr.at[0], cs.at[0], cr.at[0])
    gather_x.start()
    down_copies = [
        pltpu.make_async_copy(
            w_down.at[at128(256 * z, 256), pl.ds(1024 * h, 1024)], wd.at[h, at128(256 * p, 256)],
            loc_sem.at[(11, 13)[h]],
        )
        for h in range(2)
    ]
    for copy in down_copies:
        copy.start()
    begin("g", "u")
    ring_qkv = Ring(place, qkv, 512, ring_send.at[0], ring_recv.at[0])
    ring_g = Ring(place, wg, 512, ring_send.at[1], ring_recv.at[1])
    ring_u = Ring(place, wu, 512, ring_send.at[2], ring_recv.at[2])
    ring_d = [Ring(place, wd.at[h], 256, ring_send.at[3 + h], ring_recv.at[3 + h]) for h in range(2)]
    settle("q", "k", "v")
    ring_qkv.start()

    def positions(shape, axis):
        i = lax.broadcasted_iota(jnp.int32, shape, axis)
        block = i // 64
        pos = jnp.zeros(shape, jnp.int32)
        for r in range(LINE):
            b = pairs[0, r]
            pos = pos + jnp.where(block == 2 * r, b * 64, 0)
            pos = pos + jnp.where(block == 2 * r + 1, (2 * LINE - 1 - b) * 64, 0)
        return (pos + i % 64).astype(F32)

    posr[k] = positions((8, seq), 1)
    col = positions((seq, 128), 0)
    posc[k] = col
    lane = lax.broadcasted_iota(jnp.int32, (seq, 128), 1)
    freq = jnp.exp((lane % 64).astype(F32) * (-2.0 / HD * math.log(ROPE_BASE)))
    angle = col * freq
    tab[0, k] = jnp.cos(angle)
    sine = jnp.sin(angle)
    tab[1, k] = jnp.where(lane < 64, -sine, sine)
    tables = [
        remote(r, r, ts.at[i], tr.at[i], place.partner)
        for i, r in enumerate([posr.at[k], posc.at[k], tab.at[0, k], tab.at[1, k]])
    ]
    for t in tables:
        t.start()

    gather_x.arrive_first()
    pl.when(is_x)(lambda: wo_send_to(0, top, place.x).wait_recv())
    pl.when(is_x)(lambda: wo_send_to(0, top, place.y).start())
    pl.when(is_y)(lambda: wo_send_to(1, low, place.x).wait_recv())
    pl.when(is_y)(lambda: wo_send_to(1, low, place.x).start())
    ring_qkv.forward()
    settle("g", "u")
    gather_x.arrive_second()

    @pl.when(is_d)
    def _():
        wo_send_to(0, top, place.x).wait_recv()
        wo_send_to(0, top, place.x).start()
        wo_send_to(1, low, place.x).wait_recv()
        wo_send_to(1, low, place.y).start()

    ring_g.start()
    ring_qkv.ready()

    def project(c):
        gather_x.ready(c)
        chunk = xs[c].reshape(2 * rows, width)
        there = at128(c * rows)
        sums = jnp.zeros((8, 2 * rows), F32)
        pick = lax.broadcasted_iota(jnp.int32, (8, cols), 0)
        for i in range(2):
            part = dot(chunk, qkv[:, i * cols : (i + 1) * cols])
            raw[i, :, there] = part.reshape(2, rows, cols)
            sums = sums + exact((pick == i).astype(F32), part * part, ((1,), (1,)))
        part = dot(chunk, qkv[:, 2 * cols :])
        heads[2, :, there] = part.astype(BF16).reshape(2, rows, cols)
        sq_own[c] = sums

    def project_step(s, carry):
        project(place.order(s))
        return carry

    lax.fori_loop(0, 3, project_step, 0)
    gather_x.arrive_third()
    lax.fori_loop(3, 4, project_step, 0)

    pair_sq = remote(sq_own, sq_pair, as_.at[0], ar.at[0], place.partner)
    pair_sq.start()
    ring_u.start()
    pair_sq.wait_recv()
    sq_both[...] = sq_own[...] + sq_pair[...]

    def line_sq(step, source):
        return remote(
            sq_both, sq_line.at[source], as_.at[step], ar.at[1 + source],
            place.line((z + step) % LINE),
        )

    for step in range(1, LINE):
        line_sq(step, z).start()
    for t in tables:
        t.wait_recv()
    for step in range(1, LINE):
        line_sq(step, (z + step) % LINE).wait_recv()
    sq_line[z] = sq_both[...]
    total = (sq_line[0] + sq_line[1]) + (sq_line[2] + sq_line[3])
    scales = lax.rsqrt(total / width + EPSILON)
    o_tot[...] = scales

    def rotate(c, carry):
        there = at128(c * rows)
        now = o_tot[c]
        for i in range(2):
            pick = (lax.broadcasted_iota(jnp.int32, (8, 128), 0) == i).astype(F32)
            column = exact(now, pick, ((0,), (0,)))
            for s in range(2):
                for h in range(2):
                    lanes = slice(128 * h, 128 * h + 128)
                    v = raw[i, s, there, lanes] * column[128 * s : 128 * s + 128]
                    v = v * gains_qk[i : i + 1, lanes]
                    v = v * tab[0, s, there] + pltpu.roll(v, 64, 1) * tab[1, s, there]
                    heads[i, s, there, lanes] = v.astype(BF16)
        return carry

    lax.fori_loop(0, LINE, rotate, 0)

    def attend(s, carry):
        mask = posr[s, 0:1, :] <= posc[s][:, 0:1]
        for h in range(2):
            lanes = slice(128 * h, 128 * h + 128)
            scores = dot_rt(heads[0, s, :, lanes], heads[1, s, :, lanes]) * (HD ** -0.5)
            scores = jnp.where(mask, scores, NEGATIVE)
            e = jnp.exp(scores - jnp.max(scores, axis=1, keepdims=True))
            low_p = (e / jnp.sum(e, axis=1, keepdims=True)).astype(BF16)
            probs[s, h] = low_p
            att[s, :, lanes] = dot(low_p, heads[2, s, :, lanes]).astype(BF16)
        return carry

    lax.fori_loop(0, 2, attend, 0)

    pl.when(is_source)(lambda: wo_copy.wait())
    pl.when(is_x)(lambda: wo_send_to(1, low, place.x).wait_recv())
    pl.when(is_y)(lambda: wo_send_to(0, top, place.x).wait_recv())

    ring_g.forward()
    buffers = (term, pair_out, pair_in, keep, mine, line_out, line_in)
    sums = [RowSum(place, h, buffers, (ps, pr, ls, lr)) for h in range(2)]

    def branch_step(s, carry):
        c = place.order(3 - s)
        left = att[:, at128(c * rows)].reshape(2 * rows, cols)
        for h in range(2):
            term[...] = dot(left, wo[:, 1024 * h : 1024 * h + 1024]).reshape(2, rows, 1024)
            sums[h].give(c, s)
        for h in range(2):
            pl.when(s > 0)(lambda h=h: sums[h].pass_on(place.order(4 - s), s + 1))
        return carry

    lax.fori_loop(0, 4, branch_step, 0)
    for h in range(2):
        sums[h].pass_on(z, 3)
    for h in range(2):
        sums[h].relay(True)
    ring_u.forward()
    for h in range(2):
        sums[h].relay(False)
    for copy in down_copies:
        copy.wait()
    ring_d[0].start()
    branch = jnp.concatenate([sums[h].total() for h in range(2)], axis=1)
    for h in range(2):
        sums[h].finish()
    o_branch[...] = branch

    def mean_sq(v):
        return jnp.sum(v * v, axis=1, keepdims=True) / width

    mid[...] = tokens[...].astype(F32) + branch * lax.rsqrt(mean_sq(branch) + EPSILON) * gain_attn[...]
    ms[z, k] = mid[...].astype(BF16)
    gather_m = Gather(place, ms, zs.at[1], zr.at[1], cs.at[1], cr.at[1])
    gather_m.start()

    ring_d[0].forward()
    ring_d[1].start()
    ring_g.ready()
    ring_u.ready()

    def expand(s, carry):
        c = place.order(s)
        gather_m.ready(c)
        chunk = ms[c].reshape(2 * rows, width)

        def body(t, inner):
            lanes = at128(t * 256, 256)
            g = dot(chunk, wg[:, lanes])
            u = dot(chunk, wu[:, lanes])
            ga[c, :, lanes] = g.astype(BF16)
            ua[c, :, lanes] = u.astype(BF16)
            hid[c, :, lanes] = (g / (1.0 + jnp.exp(-g)) * u).astype(BF16)
            return inner

        lax.fori_loop(0, 4, body, 0)
        return carry

    def contract(h):
        def step(s, carry):
            c = place.order(s)
            term[...] = dot(hid[c], wd[h]).reshape(2, rows, 1024)
            sums[h].give(c, s)
            pl.when(s > 0)(lambda: sums[h].pass_on(place.order(s - 1), s + 1))
            return carry

        return step

    lax.fori_loop(0, 1, expand, 0)
    gather_m.arrive_first()
    lax.fori_loop(1, 2, expand, 0)
    ring_d[0].ready()
    lax.fori_loop(0, 2, contract(0), 0)
    gather_m.arrive_second()
    ring_d[1].forward()
    lax.fori_loop(2, 3, expand, 0)
    lax.fori_loop(2, 3, contract(0), 0)
    ring_d[1].ready()
    lax.fori_loop(0, 3, contract(1), 0)
    gather_m.arrive_third()
    lax.fori_loop(3, 4, expand, 0)
    for h in range(2):
        lax.fori_loop(3, 4, contract(h), 0)
    for h in range(2):
        sums[h].relay(False)
    for h in range(2):
        sums[h].pass_on(place.order(3), 3)
    for h in range(2):
        sums[h].relay(True)

    saves = [
        (qkv, o_qkv), (wo, o_wo), (wg, o_g), (wu, o_u), (wd.at[0], o_dn.at[:, pl.ds(0, 1024)]),
        (wd.at[1], o_dn.at[:, pl.ds(1024, 1024)]), (xs, o_x), (ms, o_m), (ga, o_ga),
        (ua, o_ua), (hid, o_hid), (raw, o_raw), (heads, o_heads), (probs, o_probs), (att, o_att),
        (tab, o_tab),
    ]
    copies = [pltpu.make_async_copy(a, b, out_sem.at[i]) for i, (a, b) in enumerate(saves)]
    for copy in copies:
        copy.start()

    mlp = jnp.concatenate([sums[h].total() for h in range(2)], axis=1)
    for h in range(2):
        sums[h].finish()
    c_m = lax.rsqrt(mean_sq(mlp) + EPSILON)
    gain = gain_mlp[...]
    o_out[...] = (mid[...] + mlp * c_m * gain).astype(BF16)
    dy = cotangent[...].astype(F32)
    gdy = gain * dy
    inner = jnp.sum(mlp * gdy, axis=1, keepdims=True) / width
    o_dmlp[...] = (c_m * gdy - mlp * (c_m * c_m * c_m * inner)).astype(BF16)
    o_gm[...] = jnp.sum(dy * mlp * c_m, axis=0, keepdims=True)

    gather_x.finish()
    gather_m.finish()
    for ring in (ring_qkv, ring_g, ring_u, *ring_d):
        ring.finish()
    for group in swap.values():
        for copy in group:
            copy.wait_send()
    for t in tables:
        t.wait_send()
    pair_sq.wait_send()
    for step in range(1, LINE):
        line_sq(step, z).wait_send()

    @pl.when(is_source)
    def _():
        wo_first(0, place.x).wait_send()
        wo_first(1, place.y).wait_send()

    pl.when(is_x)(lambda: wo_send_to(0, top, place.y).wait_send())
    pl.when(is_y)(lambda: wo_send_to(1, low, place.x).wait_send())

    @pl.when(is_d)
    def _():
        wo_send_to(0, top, place.x).wait_send()
        wo_send_to(1, low, place.y).wait_send()

    for copy in copies:
        copy.wait()


def any_spec():
    return pl.BlockSpec(memory_space=pl.ANY)


def vmem_spec():
    return pl.BlockSpec(memory_space=pltpu.VMEM)


def run_forward(pairs, gains_qk, gain_attn, gain_mlp, tokens, cotangent, weights):
    shape = jax.ShapeDtypeStruct
    dma = pltpu.SemaphoreType.DMA
    kept = [
        shape((2048, 768), BF16),
        shape((256, 2048), BF16),
        shape((2048, 1024), BF16),
        shape((2048, 1024), BF16),
        shape((1024, 2048), BF16),
        shape((4, 2, 128, 2048), BF16),
        shape((4, 2, 128, 2048), BF16),
        shape((4, 256, 1024), BF16),
        shape((4, 256, 1024), BF16),
        shape((4, 256, 1024), BF16),
        shape((2, 2, 512, 256), F32),
        shape((3, 2, 512, 256), BF16),
        shape((2, 2, 512, 512), BF16),
        shape((2, 512, 256), BF16),
        shape((2, 2, 512, 128), F32),
    ]
    return pl.pallas_call(
        forward_kernel,
        name="forward",
        out_shape=[
            shape((128, 2048), BF16),
            shape((128, 2048), BF16),
            shape((1, 2048), F32),
            shape((128, 2048), F32),
            shape((4, 8, 256), F32),
        ]
        + kept,
        in_specs=[pl.BlockSpec(memory_space=pltpu.SMEM)] + [vmem_spec()] * 5 + [any_spec()] * 7,
        out_specs=[vmem_spec()] * 5 + [any_spec()] * len(kept),
        scratch_shapes=[pltpu.VMEM((2, 1024, 1024) if i == 4 else k.shape, k.dtype) for i, k in enumerate(kept)]
        + [
            pltpu.VMEM((2, 8, 512), F32),
            pltpu.VMEM((2, 512, 128), F32),
            pltpu.VMEM((2, 128, 1024), F32),
            pltpu.VMEM((2, 4, 128, 1024), BF16),
            pltpu.VMEM((2, 4, 128, 1024), BF16),
            pltpu.VMEM((2, 2, 128, 1024), F32),
            pltpu.VMEM((2, 128, 1024), F32),
            pltpu.VMEM((2, 4, 128, 1024), BF16),
            pltpu.VMEM((2, 4, 128, 1024), BF16),
            pltpu.VMEM((4, 8, 256), F32),
            pltpu.VMEM((4, 8, 256), F32),
            pltpu.VMEM((4, 8, 256), F32),
            pltpu.VMEM((4, 4, 8, 256), F32),
            pltpu.VMEM((128, 2048), F32),
            dma((14,)),
            dma((11,)),
            dma((11,)),
            dma((5, 4)),
            dma((5, 4)),
            dma((2,)),
            dma((2,)),
            dma((2, 2, 4)),
            dma((2, 4)),
            dma((2, 4)),
            dma((2, 4)),
            dma((2, 4)),
            dma((2, 4)),
            dma((2, 4)),
            dma((2, 4)),
            dma((4,)),
            dma((4,)),
            dma((4,)),
            dma((5,)),
            dma((len(kept) + 1,)),
        ],
        compiler_params=pltpu.CompilerParams(
            collective_id=0, has_side_effects=True, vmem_limit_bytes=64 * 1024 * 1024
        ),
    )(pairs, gains_qk, gain_attn, gain_mlp, tokens, cotangent, *weights)


def backward_kernel(
    gains_qk, gain_attn, d_mlp, cotangent, branch, scales, gm_part,
    h_qkv, h_wo, h_g, h_u, h_dn, h_x, h_m, h_ga, h_ua, h_hid, h_raw, h_heads, h_probs, h_att, h_tab,
    o_tok, o_down, o_out, o_gu, o_qkv,
    st_g, rc_g, st_u, rc_u, st_dn, rc_dn, st_qkv, rc_qkv, st_out, rc_out,
    wd, wg, wu, ga, ua, hid, dm, dg, du, ms, db, raw, tab, datt, dy,
    term, pair_out, pair_in, keep, mine, line_out, line_in,
    sq_own, sq_pair, sq_both, sq_line, gn_own, d_mid, stage, stage_d, far_in,
    ld, far_sem, zs, zr, cs, cr, ps, pr, ls, lr, as_, ar, in_send, in_recv, st_sem, sum_sem,
    fin_send, fin_recv, fin_loc, al_send, al_recv, al_loc,
):
    place = Place()
    z, f, p, k = place.z, place.f, place.p, place.k
    rows, width, cols = 128, 2048, 256

    def strip_of(chip, plane):
        return (chip % 2 + plane // 2) % 2 + 2 * ((chip // 2 + plane % 2) % 2)

    down_to = (strip_of(p, z), 4 * k + z)
    down_from = (f % 4, 2 * strip_of(z, f % 4) + f // 4)
    down_moves = jnp.logical_or(down_to[0] != z, down_to[1] != f)
    out_to = (z, 4 * k + p)
    out_from = (z, 2 * (f % 4) + f // 4)
    out_moves = out_to[1] != f
    place.barrier(
        [place.d] + [place.cross((z + step) % LINE) for step in range(1, LINE)],
        [(down_moves, down_from), (out_moves, out_from)],
    )

    loads = {}

    def load(name, src, dst):
        loads[name] = pltpu.make_async_copy(src, dst, ld.at[len(loads)])
        loads[name].start()

    dm[at128(z * 256 + k * rows)] = d_mlp[...]

    class Rows:
        def __init__(self, ref):
            self.ref = ref

        @property
        def at(self):
            ref = self.ref

            class At:
                def __getitem__(self, key):
                    c, core = key
                    return ref.at[at128(c * 256 + core * rows)]

            return At()

    gather_d = Gather(place, Rows(dm), zs.at[0], zr.at[0], cs.at[0], cr.at[0])
    gather_d.start()
    load("wd", h_dn, wd)
    load("ga", h_ga, ga)
    load("ua", h_ua, ua)
    load("wg", h_g, wg)
    load("wu", h_u, wu)
    load("hid", h_hid, hid)
    load("ms", h_m, ms)
    load("raw", h_raw, raw)
    load("tab", h_tab, tab)

    buffers = (term, pair_out, pair_in, keep, mine, line_out, line_in)
    sums = [RowSum(place, h, buffers, (ps, pr, ls, lr)) for h in range(2)]

    def chunk_rows(c):
        return at128(c * 256, 256)

    def expand(s, carry):
        c = place.order(s)
        gather_d.ready(c)
        here = chunk_rows(c)
        grad = dm[here]

        def act(t, inner):
            lanes = at128(t * 256, 256)
            dh = dot_rt(grad, wd[lanes])
            g = ga[here, lanes].astype(F32)
            u = ua[here, lanes].astype(F32)
            sig = 1.0 / (1.0 + jnp.exp(-g))
            dg[here, lanes] = (dh * u * sig * (1.0 + g * (1.0 - sig))).astype(BF16)
            du[here, lanes] = (dh * g * sig).astype(BF16)
            return inner

        lax.fori_loop(0, 4, act, 0)
        return carry

    def contract(s, carry):
        c = place.order(s)
        here = chunk_rows(c)
        left_g, left_u = dg[here], du[here]
        for h in range(2):
            out = slice(1024 * h, 1024 * h + 1024)
            term[...] = (dot_rt(left_g, wg[out]) + dot_rt(left_u, wu[out])).reshape(2, rows, 1024)
            sums[h].give(c, s)
        for h in range(2):
            pl.when(s > 0)(lambda h=h: sums[h].pass_on(place.order(s - 1), s + 1))
        return carry

    for name in ("wd", "ga", "ua"):
        loads[name].wait()
    lax.fori_loop(0, 1, expand, 0)
    for name in ("wg", "wu"):
        loads[name].wait()
    gather_d.arrive_first()
    lax.fori_loop(0, 1, contract, 0)
    for s in (1, 2):
        if s == 2:
            gather_d.arrive_second()
        lax.fori_loop(s, s + 1, expand, 0)
        lax.fori_loop(s, s + 1, contract, 0)
    gather_d.arrive_third()
    lax.fori_loop(3, 4, expand, 0)
    lax.fori_loop(3, 4, contract, 0)
    for h in range(2):
        sums[h].pass_on(place.order(3), 3)
    load("x", h_x, wd)
    load("qkv", h_qkv, wg.at[:, pl.ds(0, 768)])
    load("probs", h_probs, wu.at[:, pl.ds(0, 512)])
    load("qk", h_heads.at[pl.ds(0, 2048)], wu.at[:, pl.ds(512, 256)])
    load("v", h_heads.at[pl.ds(2048, 1024)], wu.at[pl.ds(0, 1024), pl.ds(768, 256)])
    load("att", h_att, wu.at[pl.ds(1024, 1024), pl.ds(768, 256)])

    chips = [place.p_x, place.p_y, place.p_d, p]
    near = [place.x, place.y, place.d]
    GATE, UP, DOWN, QKV, OUT = range(5)
    kinds = {GATE: (st_g, rc_g), UP: (st_u, rc_u), DOWN: (st_dn, rc_dn), QKV: (st_qkv, rc_qkv)}

    def half_of(kind, ref, i, half):
        if kind == DOWN:
            return ref.at[i, :, pl.ds(1024 * half, 1024)]
        return ref.at[i, pl.ds(256 * half, 256)]

    def far_part(kind, half):
        st, rc = kinds[kind]
        return remote(
            half_of(kind, st, 2, half), half_of(kind, rc, 2, half), in_send.at[kind, 2 + half],
            in_recv.at[kind, 2 + half], near[half],
        )

    def near_part(kind, i):
        st, rc = kinds[kind]
        return remote(st.at[i], rc.at[i], in_send.at[kind, i], in_recv.at[kind, i], near[i])

    def put(kind, i, buf, sem):
        wide = 896 if kind == QKV else 1024
        if i < 2:
            half = 1 - i
            far_part(kind, half).wait_recv()
            got = far_in.at[:, pl.ds(0, wide)]
            copy = pltpu.make_async_copy(half_of(kind, kinds[kind][1], 2, half), got, far_sem)
            copy.start()
            copy.wait()
            if kind == DOWN:
                now = (slice(None), slice(1024 * half, 1024 * half + 1024))
            else:
                now = (slice(256 * half, 256 * half + 256), slice(0, wide))
            buf[now] = (buf[now].astype(F32) + far_in[:, 0:wide].astype(F32)).astype(BF16)
        src = buf.at[:, pl.ds(0, 896)] if kind == QKV else buf
        copy = pltpu.make_async_copy(src, kinds[kind][0].at[i], st_sem.at[sem])
        copy.start()
        copy.wait()
        if i == 2:
            far_part(kind, 0).start()
            far_part(kind, 1).start()
        elif i < 2:
            near_part(kind, i).start()

    def feature_rows(ref, chip):
        return jnp.concatenate([ref[:, at128(512 * c + 128 * chip)] for c in range(LINE)], axis=1).T

    def gate_up_part(i):
        left = feature_rows(ms, chips[i])
        for m, right in enumerate((dg, du)):
            for t in range(2):
                lanes = slice(512 * t, 512 * t + 512)
                stage[m, :, lanes] = dot(left, right[:, lanes]).astype(BF16)
            put(m, i, stage.at[m], m)

    def down_part(i):
        left = hid[:, at128(strip_of(chips[i], z) * 256, 256)].T
        for t in range(4):
            lanes = slice(512 * t, 512 * t + 512)
            stage_d[:, lanes] = dot(left, dm[:, lanes]).astype(BF16)
        put(DOWN, i, stage_d, 2)

    loads["ms"].wait()
    loads["hid"].wait()
    gate_up_part(2)
    for h in range(2):
        sums[h].relay(False)
    down_part(2)
    gate_up_part(3)
    for h in range(2):
        sums[h].relay(True)
    gate_up_part(0)
    gate_up_part(1)
    gather_d.finish()

    def mean_of(v):
        return jnp.sum(v, axis=1, keepdims=True) / width

    d_mid[...] = cotangent[...].astype(F32) + jnp.concatenate([sums[h].total() for h in range(2)], axis=1)
    for h in range(2):
        sums[h].finish()
    b = branch[...]
    c_b = lax.rsqrt(mean_of(b * b) + EPSILON)
    gdy = gain_attn[...] * d_mid[...]
    db[at128(z * 256 + k * rows)] = (
        c_b * gdy - b * (c_b * c_b * c_b * mean_of(b * gdy))
    ).astype(BF16)
    gather_b = Gather(place, Rows(db), zs.at[1], zr.at[1], cs.at[1], cr.at[1])
    gather_b.start()
    gn_own[...] = jnp.zeros((8, width), F32)
    gn_own[2:3, :] = jnp.sum(d_mid[...] * b * c_b, axis=0, keepdims=True)
    gn_own[3:4, :] = gm_part[...]

    down_part(3)
    down_part(0)
    down_part(1)
    load("wo", h_wo, stage_d)

    for name in ("wo", "raw", "tab", "x", "qkv", "probs", "qk", "v", "att"):
        loads[name].wait()

    def attended_step(s, carry):
        c = place.order(s)
        gather_b.ready(c)
        part = dot_rt(db[chunk_rows(c)], stage_d[...]).astype(BF16)
        datt[:, at128(c * rows)] = part.reshape(2, rows, cols)
        return carry

    gather_b.arrive_first()
    lax.fori_loop(0, 2, attended_step, 0)
    gather_b.arrive_second()
    lax.fori_loop(2, 3, attended_step, 0)

    def fetch(kind, parts, first):
        copies = [
            pltpu.make_async_copy(src, dst, sum_sem.at[first + n]) for n, (src, dst) in enumerate(parts)
        ]
        for copy in copies:
            copy.start()
        for copy in copies:
            copy.wait()

    def to_owner(kind, src, dst):
        def go(c, core, device):
            return remote(
                src(c, core), dst.at[z, k], al_send.at[kind, c, core], al_recv.at[kind, z, k], device
            )

        def each(action):
            for step in range(1, LINE):
                c = (z + step) % LINE
                action(go(c, k, place.line(c)))
                action(go(c, 1 - k, place.cross(c)))
            action(go(z, 1 - k, place.partner))

        here = pltpu.make_async_copy(src(z, k), dst.at[z, k], al_loc.at[kind])
        each(lambda copy: copy.start())
        here.start()

        def wait():
            here.wait()
            each(lambda copy: copy.wait_send())
            for step in range(LINE):
                c = (z + step) % LINE
                for core in (0, 1):
                    got = remote(
                        src(c, k), dst.at[c, core], al_send.at[kind, c, core], al_recv.at[kind, c, core],
                        place.partner,
                    )
                    if step == 0:
                        pl.when(k != core)(lambda got=got: got.wait_recv())
                    else:
                        got.wait_recv()

        return wait

    waits = []

    def square_sum(kind, buf, other, lanes, dst):
        st, rc = kinds[kind]
        cut = pl.ds(0, lanes)
        near_part(kind, 0).wait_recv()
        near_part(kind, 1).wait_recv()
        fetch(
            kind,
            [
                (st.at[3], buf.at[pl.ds(0, 512), cut]),
                (rc.at[0], buf.at[pl.ds(512, 512), cut]),
                (rc.at[1], other.at[pl.ds(0, 512), cut]),
            ],
            3 * kind,
        )

        def add_up(t, carry):
            there = at128(t * 128)
            acc = buf[there, 0:lanes].astype(F32) + buf[at128(512 + t * 128), 0:lanes].astype(F32)
            buf[there, 0:lanes] = (acc + other[there, 0:lanes].astype(F32)).astype(BF16)
            return carry

        lax.fori_loop(0, 4, add_up, 0)
        waits.append(
            to_owner(
                min(kind, 2), lambda c, core: buf.at[at128(c * 128 + core * 64, 64), cut], dst
            )
        )

    square_sum(GATE, hid, ua, 1024, o_gu.at[0])
    gather_b.arrive_third()
    lax.fori_loop(3, 4, attended_step, 0)

    def attend(s, carry):
        there = at128(s * 512, 512)
        for h in range(2):
            lanes = slice(128 * h, 128 * h + 128)
            more = slice(512 + 128 * h, 640 + 128 * h)
            vals = slice(768 + 128 * h, 896 + 128 * h)
            low_p = wu[at128((2 * s + h) * 512, 512), 0:512]
            grad = datt[s, :, lanes]
            q = wu[there, more]
            key = wu[at128(1024 + s * 512, 512), more]
            value = wu[there, vals]
            d_value = dot_lt(low_p, grad).astype(BF16)
            d_probs = dot_rt(grad, value)
            pr32 = low_p.astype(F32)
            delta = jnp.sum(pr32 * d_probs, axis=1, keepdims=True)
            d_scores = (pr32 * (d_probs - delta)).astype(BF16)
            d_q = dot(d_scores, key) * (HD ** -0.5)
            d_k = dot_lt(d_scores, q) * (HD ** -0.5)
            for i, d in enumerate((d_q, d_k)):
                dy[i, s, :, lanes] = d * tab[0, s] - pltpu.roll(d, 64, 1) * tab[1, s]
            for c in range(LINE):
                ga[c * 256 + s * rows : c * 256 + s * rows + rows, vals.start - 256 : vals.stop - 256] = (
                    d_value[c * rows : c * rows + rows]
                )
        return carry

    for s in range(2):
        attend(s, 0)

    def dots_step(c, carry):
        there = at128(c * rows)
        pick = lax.broadcasted_iota(jnp.int32, (8, cols), 0)
        acc = jnp.zeros((8, 2 * rows), F32)
        for i in range(2):
            part = (raw[i, :, there] * dy[i, :, there]).reshape(2 * rows, cols) * gains_qk[i : i + 1]
            acc = acc + exact((pick == i).astype(F32), part, ((1,), (1,)))
        sq_own[c] = acc
        return carry

    lax.fori_loop(0, LINE, dots_step, 0)
    pair_sq = remote(sq_own, sq_pair, as_.at[0], ar.at[0], place.partner)
    pair_sq.start()
    pair_sq.wait_recv()
    sq_both[...] = sq_own[...] + sq_pair[...]

    def line_sq(step, source):
        return remote(
            sq_both, sq_line.at[source], as_.at[step], ar.at[1 + source], place.line((z + step) % LINE)
        )

    for step in range(1, LINE):
        line_sq(step, z).start()
    square_sum(UP, dg, du, 1024, o_gu.at[1])
    for step in range(1, LINE):
        line_sq(step, (z + step) % LINE).wait_recv()
    sq_line[z] = sq_both[...]

    def normalise(c, gains):
        there = at128(c * rows)
        means = ((sq_line[0, c] + sq_line[1, c]) + (sq_line[2, c] + sq_line[3, c])) / width
        now = scales[c]
        result = []
        for i in range(2):
            pick = (lax.broadcasted_iota(jnp.int32, (8, 128), 0) == i).astype(F32)
            scale = exact(now, pick, ((0,), (0,)))
            mean = exact(means, pick, ((0,), (0,)))
            gain_sum = []
            for h in range(2):
                lanes = slice(128 * h, 128 * h + 128)
                v = raw[i, :, there, lanes].reshape(2 * rows, 128)
                d = dy[i, :, there, lanes].reshape(2 * rows, 128)
                gain_sum.append(jnp.sum(d * v * scale, axis=0, keepdims=True))
                d = scale * gains_qk[i : i + 1, lanes] * d - v * (scale * scale * scale * mean)
                ga[chunk_rows(c), 256 * i + 128 * h : 256 * i + 128 * h + 128] = d.astype(BF16)
            result.append(gains[i] + jnp.concatenate(gain_sum, axis=1))
        return tuple(result)

    start = (jnp.zeros((1, cols), F32), jnp.zeros((1, cols), F32))
    gain_q, gain_k = lax.fori_loop(0, LINE, normalise, start)
    own_cols = at128(cols * (2 * z + k), cols)
    gn_own[0:1, own_cols] = gain_q
    gn_own[1:2, own_cols] = gain_k

    def token_step(s, carry):
        c = place.order(3 - s)
        left = ga[chunk_rows(c), 0:768]
        for h in range(2):
            term[...] = dot_rt(left, wg[1024 * h : 1024 * h + 1024, 0:768]).reshape(2, rows, 1024)
            sums[h].give(c, s)
        for h in range(2):
            pl.when(s > 0)(lambda h=h: sums[h].pass_on(place.order(4 - s), s + 1))
        return carry

    lax.fori_loop(0, 4, token_step, 0)
    for h in range(2):
        sums[h].pass_on(z, 3)

    def qkv_part(i):
        stage[0, :, 0:768] = dot(feature_rows(wd, chips[i]), ga[:, 0:768]).astype(BF16)
        sides = jnp.concatenate([gn_own[:, at128(512 * c + 128 * chips[i])] for c in range(LINE)], axis=1)
        lane = lax.broadcasted_iota(jnp.int32, (8, 128), 1)
        column = (lax.broadcasted_iota(jnp.int32, (8, 128), 0) == lane).astype(F32)
        stage[0, :, 768:896] = exact(sides, column, ((0,), (0,))).astype(BF16)
        put(QKV, i, stage.at[0], 3)

    qkv_part(2)
    for h in range(2):
        sums[h].relay(True)
    qkv_part(3)
    for s in range(2):
        for c in range(LINE):
            ua[c * 256 + s * rows : c * 256 + s * rows + rows, 0:256] = (
                wu[1024 + s * 512 + c * rows : 1024 + s * 512 + c * rows + rows, 768:1024]
            )

    def outer(t, carry):
        lanes = at128(t * 512, 512)
        stage_d[:, lanes] = dot_lt(ua[:, 0:256], db[:, lanes]).astype(BF16)
        return carry

    lax.fori_loop(0, 4, outer, 0)
    copy = pltpu.make_async_copy(stage_d, st_out, st_sem.at[0])
    copy.start()
    copy.wait()

    def out_part(i):
        return remote(
            st_out.at[at128(64 * chips[i], 64)], rc_out.at[i], in_send.at[OUT, i], in_recv.at[OUT, i], near[i]
        )

    qkv_part(0)
    qkv_part(1)
    for i in range(3):
        out_part(i).start()

    for h in range(2):
        sums[h].relay(False)

    near_part(DOWN, 0).wait_recv()
    near_part(DOWN, 1).wait_recv()
    fetch(
        DOWN,
        [
            (st_dn.at[3], ms.at[pl.ds(0, 256)]),
            (rc_dn.at[0], ms.at[pl.ds(256, 256)]),
            (rc_dn.at[1], ms.at[pl.ds(512, 256)]),
        ],
        3 * DOWN,
    )

    def add_down(t, carry):
        lanes = at128(t * 512, 512)
        acc = ms[0:256, lanes].astype(F32) + ms[256:512, lanes].astype(F32)
        dm[0:256, lanes] = (acc + ms[512:768, lanes].astype(F32)).astype(BF16)
        return carry

    lax.fori_loop(0, 4, add_down, 0)
    down_done = dm.at[pl.ds(0, 256)]
    fin_down = remote(down_done, o_down, fin_send.at[0], fin_recv.at[0], down_to)
    keep_down = pltpu.make_async_copy(down_done, o_down, fin_loc.at[0])
    pl.when(down_moves)(lambda: fin_down.start())
    pl.when(jnp.logical_not(down_moves))(lambda: keep_down.start())

    for h in range(2):
        out = slice(1024 * h, 1024 * h + 1024)
        o_tok[:, out] = (d_mid[:, out] + sums[h].total()).astype(BF16)
        sums[h].finish()

    square_sum(QKV, ua, du, 896, o_qkv)

    for i in range(3):
        out_part(i).wait_recv()
    sources = [rc_out.at[0], rc_out.at[1], rc_out.at[2], st_out.at[at128(64 * p, 64)]]
    copies = [
        pltpu.make_async_copy(src, ms.at[pl.ds(64 * i, 64)], sum_sem.at[16 + i])
        for i, src in enumerate(sources)
    ]
    for copy in copies:
        copy.start()
    for copy in copies:
        copy.wait()
    acc = ms[0:64].astype(F32) + ms[64:128].astype(F32)
    acc = acc + ms[128:192].astype(F32) + ms[192:256].astype(F32)
    ms[256:320] = acc.astype(BF16)
    out_done = ms.at[pl.ds(256, 64)]
    fin_out = remote(out_done, o_out, fin_send.at[1], fin_recv.at[1], out_to)
    keep_out = pltpu.make_async_copy(out_done, o_out, fin_loc.at[1])
    pl.when(out_moves)(lambda: fin_out.start())
    pl.when(jnp.logical_not(out_moves))(lambda: keep_out.start())

    gather_b.finish()
    pair_sq.wait_send()
    for step in range(1, LINE):
        line_sq(step, z).wait_send()
    for i in range(3):
        out_part(i).wait_send()
    for kind in kinds:
        for i in range(2):
            near_part(kind, i).wait_send()
            far_part(kind, i).wait_send()
    for wait in waits:
        wait()
    pl.when(down_moves)(lambda: fin_down.wait())
    pl.when(jnp.logical_not(down_moves))(lambda: keep_down.wait())
    pl.when(out_moves)(lambda: fin_out.wait())
    pl.when(jnp.logical_not(out_moves))(lambda: keep_out.wait())


def run_backward(gains_qk, gain_attn, d_mlp, cotangent, branch, scales, gm_part, kept):
    shape = jax.ShapeDtypeStruct
    dma = pltpu.SemaphoreType.DMA
    flat = [(2048, 768), (256, 2048), (2048, 1024), (2048, 1024), (1024, 2048), (1024, 2048), (1024, 2048),
            (1024, 1024), (1024, 1024), (1024, 1024), None, (3072, 256), (2048, 512), (1024, 256), None]
    kept = [a if s is None else a.reshape(s) for a, s in zip(kept, flat)]
    results = [
        shape((256, 2048), BF16),
        shape((64, 2048), BF16),
        shape((2, 4, 2, 64, 1024), BF16),
        shape((4, 2, 64, 896), BF16),
    ]
    transit = [
        shape((4, 512, 1024), BF16),
        shape((3, 512, 1024), BF16),
        shape((4, 512, 1024), BF16),
        shape((3, 512, 1024), BF16),
        shape((4, 256, 2048), BF16),
        shape((3, 256, 2048), BF16),
        shape((4, 512, 896), BF16),
        shape((3, 512, 896), BF16),
        shape((256, 2048), BF16),
        shape((3, 64, 2048), BF16),
    ]
    wide, square = pltpu.VMEM((1024, 2048), BF16), pltpu.VMEM((1024, 1024), BF16)
    tall = pltpu.VMEM((2048, 1024), BF16)
    rows = pltpu.VMEM((2, 4, 128, 1024), BF16)
    small = pltpu.VMEM((4, 8, 256), F32)
    return pl.pallas_call(
        backward_kernel,
        name="backward",
        out_shape=[shape((128, 2048), BF16)] + results + transit,
        in_specs=[vmem_spec()] * 7 + [any_spec()] * len(kept),
        out_specs=[vmem_spec()] + [any_spec()] * (len(results) + len(transit)),
        scratch_shapes=[
            wide, tall, tall, square, square, square, wide, square, square, wide, wide,
            pltpu.VMEM((2, 2, 512, 256), F32),
            pltpu.VMEM((2, 2, 512, 128), F32),
            pltpu.VMEM((2, 512, 256), BF16),
            pltpu.VMEM((2, 2, 512, 256), F32),
            pltpu.VMEM((2, 128, 1024), F32),
            rows,
            rows,
            pltpu.VMEM((2, 2, 128, 1024), F32),
            pltpu.VMEM((2, 128, 1024), F32),
            rows,
            rows,
            small,
            small,
            small,
            pltpu.VMEM((4, 4, 8, 256), F32),
            pltpu.VMEM((8, 2048), F32),
            pltpu.VMEM((128, 2048), F32),
            pltpu.VMEM((2, 512, 1024), BF16),
            pltpu.VMEM((256, 2048), BF16),
            pltpu.VMEM((256, 1024), BF16),
            dma((16,)),
            dma(()),
            dma((2, 2, 4)), dma((2, 4)), dma((2, 4)), dma((2, 4)),
            dma((2, 4)), dma((2, 4)), dma((2, 4)), dma((2, 4)),
            dma((4,)), dma((5,)),
            dma((5, 4)), dma((5, 4)),
            dma((4,)), dma((20,)),
            dma((2,)), dma((2,)), dma((2,)),
            dma((3, 4, 2)), dma((3, 4, 2)), dma((3,)),
        ],
        compiler_params=pltpu.CompilerParams(
            collective_id=1, has_side_effects=True, vmem_limit_bytes=64 * 1024 * 1024
        ),
    )(gains_qk, gain_attn, d_mlp, cotangent, branch, scales, gm_part, *kept)[:5]


def arrange_kernel(
    gate_up, qkv, out_rows, down, o_q, o_k, o_v, o_out, o_gate, o_up, o_down, g_q, g_k, g_attn, g_mlp,
    v_gu, v_qkv, v_out, v_down, w_gu, w_qkv, w_out, w_down, in_sem, out_sem,
):
    reads = [
        pltpu.make_async_copy(src, dst, in_sem.at[i])
        for i, (src, dst) in enumerate([(gate_up, v_gu), (down, v_down), (qkv, v_qkv), (out_rows, v_out)])
    ]
    for copy in reads:
        copy.start()
    writes = []

    def write(src, dst):
        copy = pltpu.make_async_copy(src, dst, out_sem.at[len(writes)])
        copy.start()
        writes.append(copy)

    reads[0].wait()
    for m, dst in enumerate((o_gate, o_up)):
        for z in range(LINE):
            for k in range(2):
                for q in range(PLANE):
                    at = 1024 * (2 * q + k) + 256 * z
                    w_gu[m, :, at : at + 256] = v_gu[m, z, k, :, 256 * q : 256 * q + 256].astype(F32)
        write(w_gu.at[m], dst)
    reads[1].wait()
    w_down[...] = v_down[...].astype(F32)
    write(w_down, o_down)
    reads[2].wait()
    total = jnp.zeros((64, 128), F32)
    for z in range(LINE):
        for k in range(2):
            at = 256 * (2 * z + k)
            for m in range(3):
                w_qkv[m, :, at : at + 256] = v_qkv[z, k, :, 256 * m : 256 * m + 256].astype(F32)
            total = total + v_qkv[z, k, :, 768:896].astype(F32)
    for m, dst in enumerate((o_q, o_k, o_v)):
        write(w_qkv.at[m], dst)
    lane = lax.broadcasted_iota(jnp.int32, (8, 128), 1)
    pick = (lax.broadcasted_iota(jnp.int32, (8, 128), 0) == lane).astype(F32)
    gains = exact(pick, total, ((1,), (1,)))
    for i, ref in enumerate((g_q, g_k, g_attn, g_mlp)):
        ref[...] = gains[i : i + 1]
    reads[3].wait()
    w_out[...] = v_out[...].astype(F32)
    write(w_out, o_out)
    for copy in writes:
        copy.wait()


def run_arrange(gate_up, qkv, out_rows, down):
    shape = jax.ShapeDtypeStruct
    arrays = (gate_up, qkv, out_rows, down)
    square = shape((64, 2048), F32)
    return pl.pallas_call(
        arrange_kernel,
        name="arrange",
        out_shape=[square] * 4 + [shape((64, 8192), F32)] * 2 + [shape((256, 2048), F32)]
        + [shape((1, 64), F32)] * 4,
        in_specs=[any_spec()] * 4,
        out_specs=[any_spec()] * 7 + [vmem_spec()] * 4,
        scratch_shapes=[pltpu.VMEM(a.shape, a.dtype) for a in arrays]
        + [
            pltpu.VMEM((2, 64, 8192), F32),
            pltpu.VMEM((3, 64, 2048), F32),
            pltpu.VMEM((64, 2048), F32),
            pltpu.VMEM((256, 2048), F32),
            pltpu.SemaphoreType.DMA((4,)),
            pltpu.SemaphoreType.DMA((7,)),
        ],
        compiler_params=pltpu.CompilerParams(vmem_limit_bytes=48 * 1024 * 1024),
    )(*arrays)


def shards_kernels(tokens, block_pairs, w_query, w_key, w_value, w_out, w_gate, w_up, w_down,
                   gain_query, gain_key, gain_attn, gain_mlp, cotangent):
    z = lax.axis_index("ctx")
    f = lax.axis_index("fsdp")
    start = 256 * (2 * z + f % 2)
    gains_qk = jnp.stack([
        lax.dynamic_slice_in_dim(gain_query, start, 256), lax.dynamic_slice_in_dim(gain_key, start, 256)
    ])
    out, d_mlp, gm_part, branch, scales, *kept = run_forward(
        block_pairs, gains_qk, gain_attn[None], gain_mlp[None], tokens[0], cotangent[0],
        (w_query, w_key, w_value, w_out, w_gate, w_up, w_down),
    )
    d_tokens, down, out_rows, gate_up, qkv = run_backward(
        gains_qk, gain_attn[None], d_mlp, cotangent[0], branch, scales, gm_part, kept
    )
    grads = run_arrange(gate_up, qkv, out_rows, down)
    return (out[None], d_tokens[None], *grads[:7], *[g[0] for g in grads[7:]])


def shards(*arrays):
    tokens, w_query, w_down = arrays[0], arrays[2], arrays[8]
    here = (lax.axis_size("ctx"), lax.axis_size("fsdp"), tokens.shape, w_query.shape, w_down.shape)
    if here == (LINE, 2 * PLANE, (1, 128, 2048), (256, 2048), (1024, 2048)):
        return shards_kernels(*arrays)
    return shards_general(*arrays)


def solution(mesh):
    in_specs = (
        P("fsdp", "ctx", None),
        P("fsdp", None),
        P("fsdp", None),
        P("fsdp", None),
        P("fsdp", None),
        P("fsdp", None),
        P("fsdp", None),
        P("fsdp", None),
        P("fsdp", None),
        P(),
        P(),
        P(),
        P(),
        P("fsdp", "ctx", None),
    )
    out_specs = (
        P("fsdp", "ctx", None),
        P("fsdp", "ctx", None),
        P(("ctx", "fsdp"), None),
        P(("ctx", "fsdp"), None),
        P(("ctx", "fsdp"), None),
        P(("ctx", "fsdp"), None),
        P(("ctx", "fsdp"), None),
        P(("ctx", "fsdp"), None),
        P(("ctx", "fsdp"), None),
        P(("ctx", "fsdp")),
        P(("ctx", "fsdp")),
        P(("ctx", "fsdp")),
        P(("ctx", "fsdp")),
    )
    return jax.shard_map(shards, mesh=mesh, in_specs=in_specs, out_specs=out_specs, check_vma=False)
```

```python
import math

import jax
import jax.numpy as jnp
from jax import lax
from jax.experimental import pallas as pl
from jax.experimental.pallas import tpu as pltpu
from jax.sharding import PartitionSpec as P

HD = 128


EPSILON = 1e-06
ROPE_BASE = 500000.0
NEGATIVE = -1e30


def norm_scale(values, gain_vec):
    return (
        values * lax.rsqrt(jnp.mean(values * values, axis=-1, keepdims=True) + EPSILON) * gain_vec
    )


def turn_half(values, cosine, sine):
    half_size = values.shape[-1] // 2
    turned = jnp.concatenate([-values[..., half_size:], values[..., :half_size]], axis=-1)
    return values * cosine + turned * sine


def angle_tables(positions, head_size):
    half_size = head_size // 2
    frequency = jnp.power(ROPE_BASE, -(jnp.arange(half_size).astype(jnp.float32) * 2.0 / head_size))
    angles = positions.astype(jnp.float32)[:, None] * frequency[None, :]
    angles = jnp.concatenate([angles, angles], axis=-1)
    return (jnp.cos(angles)[:, None, :], jnp.sin(angles)[:, None, :])


def row_positions(row_ids, pair_row, block_rows, ctx_count):
    rank_of = row_ids // (2 * block_rows)
    second = row_ids // block_rows % 2
    offset = row_ids % block_rows
    rank_match = (rank_of[:, None] == jnp.arange(ctx_count, dtype=jnp.int32)[None, :]).astype(
        jnp.int32
    )
    chosen = jnp.sum(rank_match * pair_row[None, :], axis=1)
    block_index = jnp.where(second == 0, chosen, 2 * ctx_count - 1 - chosen)
    return block_index * block_rows + offset


def times_transpose(left, right):
    return lax.dot_general(
        left, right, (((1,), (1,)), ((), ())), preferred_element_type=jnp.float32
    )


def transpose_times(left, right):
    return lax.dot_general(
        left, right, (((0,), (0,)), ((), ())), preferred_element_type=jnp.float32
    )


def activate(gate_in, up_in):
    return jax.nn.silu(gate_in) * up_in


def spread_rows(values, outer, inner):
    rows, width = values.shape
    return (
        values.reshape(outer, inner, rows // (outer * inner), width)
        .transpose(1, 0, 2, 3)
        .reshape(rows, width)
    )


def shards_general(
    tokens,
    block_pairs,
    w_query,
    w_key,
    w_value,
    w_out,
    w_gate,
    w_up,
    w_down,
    gain_query,
    gain_key,
    gain_attn,
    gain_mlp,
    cotangent,
):
    bf16 = jnp.bfloat16
    f32 = jnp.float32
    local_rows = tokens.shape[1]
    block_rows = local_rows // 2
    width = w_query.shape[1]
    hidden_width = w_gate.shape[1]
    ctx_count = lax.axis_size("ctx")
    fsdp_count = lax.axis_size("fsdp")
    ctx_index = lax.axis_index("ctx")
    seq = local_rows * ctx_count
    cols = width // ctx_count
    heads = cols // HD
    strip = hidden_width // (ctx_count * fsdp_count)
    hid = strip * fsdp_count
    scale = HD ** (-0.5)

    def ctx_cols(w):
        return lax.dynamic_slice_in_dim(w, ctx_index * cols, cols, 1)

    def ctx_strips(w):
        parts = w.reshape(w.shape[0], fsdp_count, ctx_count, strip)
        return lax.dynamic_index_in_dim(parts, ctx_index, 2, keepdims=False).reshape(w.shape[0], hid)

    token_rows = tokens[0]
    x_all = lax.all_gather(token_rows, "ctx", axis=0, tiled=True)
    qkv_w = lax.all_gather(
        jnp.concatenate([ctx_cols(w_query), ctx_cols(w_key), ctx_cols(w_value)], axis=1),
        "fsdp", axis=0, tiled=True,
    )
    out_w = lax.dynamic_slice_in_dim(
        lax.all_gather(w_out, "fsdp", axis=0, tiled=True), ctx_index * cols, cols, 0
    )
    gate_w = lax.all_gather(ctx_strips(w_gate), "fsdp", axis=0, tiled=True)
    up_w = lax.all_gather(ctx_strips(w_up), "fsdp", axis=0, tiled=True)
    down_w = lax.all_gather(
        lax.dynamic_slice_in_dim(w_down, ctx_index * strip, strip, 0), "fsdp", axis=0, tiled=True
    )

    pos = row_positions(jnp.arange(seq, dtype=jnp.int32), block_pairs[0], block_rows, ctx_count)
    cosine, sine = angle_tables(pos, HD)
    mask = pos[None, :] <= pos[:, None]
    gain_q = lax.dynamic_slice_in_dim(gain_query, ctx_index * cols, cols)
    gain_k = lax.dynamic_slice_in_dim(gain_key, ctx_index * cols, cols)

    qkv = jnp.dot(x_all, qkv_w, preferred_element_type=f32)
    q_raw, k_raw, v_raw = qkv[:, :cols], qkv[:, cols : 2 * cols], qkv[:, 2 * cols :]
    squares = jnp.stack([jnp.sum(q_raw * q_raw, axis=1), jnp.sum(k_raw * k_raw, axis=1)])
    squares = lax.psum(squares, "ctx")
    scales = lax.rsqrt(squares / width + EPSILON)
    c_q, c_k = scales[0][:, None], scales[1][:, None]

    def rope(v):
        return turn_half(v.reshape(seq, heads, HD), cosine, sine)

    def rope_back(w):
        w = w.reshape(seq, heads, HD)
        u = w * sine
        half = HD // 2
        turned = jnp.concatenate([u[..., half:], -u[..., :half]], axis=-1)
        return (w * cosine + turned).reshape(seq, cols)

    queries = rope(q_raw * c_q * gain_q).astype(bf16)
    keys = rope(k_raw * c_k * gain_k).astype(bf16)
    values = v_raw.astype(bf16).reshape(seq, heads, HD)
    scores = jnp.einsum("qhd,khd->hqk", queries, keys, preferred_element_type=f32) * scale
    scores = jnp.where(mask[None], scores, NEGATIVE)
    exponent = jnp.exp(scores - jnp.max(scores, axis=-1, keepdims=True))
    probs = exponent / jnp.sum(exponent, axis=-1, keepdims=True)
    prob_low = probs.astype(bf16)
    attended = (
        jnp.einsum("hqk,khd->qhd", prob_low, values, preferred_element_type=f32)
        .reshape(seq, cols)
        .astype(bf16)
    )
    branch = lax.psum_scatter(
        jnp.dot(attended, out_w, preferred_element_type=f32).astype(bf16),
        "ctx", scatter_dimension=0, tiled=True,
    ).astype(f32)
    mid = token_rows.astype(f32) + norm_scale(branch, gain_attn)
    mid_all = lax.all_gather(mid.astype(bf16), "ctx", axis=0, tiled=True)
    gate_act = jnp.dot(mid_all, gate_w, preferred_element_type=f32)
    up_act = jnp.dot(mid_all, up_w, preferred_element_type=f32)
    hidden = activate(gate_act, up_act).astype(bf16)
    mlp_out = lax.psum_scatter(
        jnp.dot(hidden, down_w, preferred_element_type=f32).astype(bf16),
        "ctx", scatter_dimension=0, tiled=True,
    ).astype(f32)
    output = (mid + norm_scale(mlp_out, gain_mlp)).astype(bf16)

    d_output = cotangent[0].astype(f32)
    unused_mlp, pull_mlp = jax.vjp(norm_scale, mlp_out, gain_mlp)
    d_mlp, grad_gm = pull_mlp(d_output)
    d_mlp_all = lax.all_gather(d_mlp.astype(bf16), "ctx", axis=0, tiled=True)
    d_hidden = times_transpose(d_mlp_all, down_w)
    unused_act, pull_act = jax.vjp(activate, gate_act, up_act)
    d_gate, d_up = pull_act(d_hidden)
    d_gate = d_gate.astype(bf16)
    d_up = d_up.astype(bf16)
    d_mid_part = times_transpose(d_gate, gate_w) + times_transpose(d_up, up_w)
    d_mid = d_output + lax.psum_scatter(
        d_mid_part.astype(bf16), "ctx", scatter_dimension=0, tiled=True
    ).astype(f32)

    down_sum = lax.psum_scatter(
        transpose_times(hidden, d_mlp_all).astype(bf16), "fsdp", scatter_dimension=0, tiled=True
    )
    moves = [
        (z * fsdp_count + f, f * ctx_count + z)
        for z in range(ctx_count)
        for f in range(fsdp_count)
    ]
    grad_down = lax.ppermute(down_sum, ("ctx", "fsdp"), moves).astype(f32)

    def column_grad(left, right):
        part = transpose_times(left, right).astype(bf16)
        mine = lax.psum_scatter(
            spread_rows(part, ctx_count, fsdp_count), "fsdp", scatter_dimension=0, tiled=True
        )
        mine = mine.reshape(ctx_count, mine.shape[0] // ctx_count, mine.shape[1])
        return lax.all_to_all(mine, "ctx", 0, 0, tiled=True)

    gate_up = column_grad(mid_all, jnp.concatenate([d_gate, d_up], axis=1))
    rows = gate_up.shape[1]

    def from_strips(part):
        return (
            part.reshape(ctx_count, rows, fsdp_count, strip)
            .transpose(1, 2, 0, 3)
            .reshape(rows, hidden_width)
            .astype(f32)
        )

    unused_branch, pull_branch = jax.vjp(norm_scale, branch, gain_attn)
    d_branch, grad_ga = pull_branch(d_mid)
    d_branch_all = lax.all_gather(d_branch.astype(bf16), "ctx", axis=0, tiled=True)
    d_attended = times_transpose(d_branch_all, out_w).astype(bf16).reshape(seq, heads, HD)
    grad_out = lax.psum_scatter(
        transpose_times(attended, d_branch_all).astype(bf16),
        "fsdp", scatter_dimension=0, tiled=True,
    ).astype(f32)

    d_values = jnp.einsum("hqk,qhd->khd", prob_low, d_attended, preferred_element_type=f32)
    d_values = d_values.astype(bf16).reshape(seq, cols)
    d_probs = jnp.einsum("qhd,khd->hqk", d_attended, values, preferred_element_type=f32)
    delta = jnp.sum(probs * d_probs, axis=-1, keepdims=True)
    d_scores = (probs * (d_probs - delta)).astype(bf16)
    d_queries = jnp.einsum("hqk,khd->qhd", d_scores, keys, preferred_element_type=f32) * scale
    d_keys = jnp.einsum("hqk,qhd->khd", d_scores, queries, preferred_element_type=f32) * scale
    dy_q = rope_back(d_queries)
    dy_k = rope_back(d_keys)
    dots = jnp.stack([
        jnp.sum(q_raw * gain_q * dy_q, axis=1), jnp.sum(k_raw * gain_k * dy_k, axis=1)
    ])
    dots = lax.psum(dots, "ctx") / width
    d_q = c_q * gain_q * dy_q - q_raw * (c_q * c_q * c_q * dots[0][:, None])
    d_k = c_k * gain_k * dy_k - k_raw * (c_k * c_k * c_k * dots[1][:, None])
    d_qkv = jnp.concatenate([d_q.astype(bf16), d_k.astype(bf16), d_values], axis=1)
    d_tokens = d_mid + lax.psum_scatter(
        times_transpose(d_qkv, qkv_w).astype(bf16), "ctx", scatter_dimension=0, tiled=True
    ).astype(f32)
    qkv_grad = column_grad(x_all, d_qkv).transpose(1, 0, 2)
    sum_gqk = lax.psum_scatter(
        jnp.stack([jnp.sum(dy_q * q_raw * c_q, axis=0), jnp.sum(dy_k * k_raw * c_k, axis=0)]),
        "fsdp", scatter_dimension=1, tiled=True,
    )
    sum_gam = lax.psum_scatter(
        jnp.stack([grad_ga, grad_gm]), ("ctx", "fsdp"), scatter_dimension=1, tiled=True
    )

    def whole(part):
        return part.reshape(part.shape[0], width).astype(f32)

    return (
        output[None],
        d_tokens.astype(bf16)[None],
        whole(qkv_grad[:, :, :cols]),
        whole(qkv_grad[:, :, cols : 2 * cols]),
        whole(qkv_grad[:, :, 2 * cols :]),
        grad_out,
        from_strips(gate_up[:, :, :hid]),
        from_strips(gate_up[:, :, hid:]),
        grad_down,
        sum_gqk[0],
        sum_gqk[1],
        sum_gam[0],
        sum_gam[1],
    )


MESH = pl.DeviceIdType.MESH
BF16 = jnp.bfloat16
F32 = jnp.float32
LINE = 4
PLANE = 4


def dot(left, right):
    return lax.dot_general(left, right, (((1,), (0,)), ((), ())), preferred_element_type=F32)


def dot_rt(left, right):
    return lax.dot_general(left, right, (((1,), (1,)), ((), ())), preferred_element_type=F32)


def dot_lt(left, right):
    return lax.dot_general(left, right, (((0,), (0,)), ((), ())), preferred_element_type=F32)


def exact(left, right, dims):
    return lax.dot_general(
        left, right, (dims, ((), ())), precision=lax.Precision.HIGHEST, preferred_element_type=F32
    )


def remote(src, dst, send, recv, device):
    return pltpu.make_async_remote_copy(
        src_ref=src, dst_ref=dst, send_sem=send, recv_sem=recv, device_id=device, device_id_type=MESH
    )


def at128(i, step=128):
    return pl.ds(i if isinstance(i, int) else pl.multiple_of(i, step), step)


class Place:
    def __init__(self):
        z = lax.axis_index("ctx")
        f = lax.axis_index("fsdp")
        self.z, self.f = z, f
        self.p, self.k = f // 2, f % 2
        self.p_x = self.p + 1 - 2 * (self.p % 2)
        self.p_y = (self.p + 2) % PLANE
        self.p_d = PLANE - 1 - self.p
        self.partner = (z, 2 * self.p + 1 - self.k)
        self.x = (z, 2 * self.p_x + self.k)
        self.y = (z, 2 * self.p_y + self.k)
        self.d = (z, 2 * self.p_d + self.k)
        self.ends = z // 3 + (3 - z) // 3

    def line(self, c):
        return (c, self.f)

    def order(self, s):
        z, e, t = self.z, self.ends, s // 3
        end = z + s * (1 - 2 * (z // 3))
        mid = (1 - t) * (z + (3 * s * s - 5 * s) // 2) + t * 3 * (2 - z)
        return e * end + (1 - e) * mid

    def cross(self, c):
        return (c, 2 * self.p + 1 - self.k)

    def barrier(self, more=(), senders=()):
        sem = pltpu.get_barrier_semaphore()

        def greet(peer):
            pl.semaphore_signal(sem, inc=1, device_id=peer, device_id_type=MESH)

        peers = [self.partner, self.x, self.y] + list(more)
        peers += [self.line((self.z + step) % LINE) for step in range(1, LINE)]
        for peer in peers:
            greet(peer)
        count = len(peers)
        for here, peer in senders:
            pl.when(here)(lambda peer=peer: greet(peer))
            count = count + here.astype(jnp.int32)
        pl.semaphore_wait(sem, count)


class Gather:
    def __init__(self, place, buf, z_send, z_recv, c_send, c_recv):
        self.pl, self.buf = place, buf
        self.sems = z_send, z_recv, c_send, c_recv

    def to_line(self, c, target, way):
        z_send, z_recv, _, _ = self.sems
        part = self.buf.at[c, self.pl.k]
        return remote(part, part, z_send.at[way, c], z_recv.at[c], self.pl.line(target))

    def to_core(self, c):
        _, _, c_send, c_recv = self.sems
        part = self.buf.at[c, self.pl.k]
        return remote(part, part, c_send.at[c], c_recv.at[c], self.pl.partner)

    def from_core(self, c):
        _, _, c_send, c_recv = self.sems
        part = self.buf.at[c, 1 - self.pl.k]
        return remote(part, part, c_send.at[c], c_recv.at[c], self.pl.partner)

    def start(self):
        z = self.pl.z
        pl.when(z < LINE - 1)(lambda: self.to_line(z, z + 1, 0).start())
        pl.when(z > 0)(lambda: self.to_line(z, z - 1, 1).start())
        self.to_core(z).start()

    def arrive(self, c):
        z = self.pl.z
        self.to_line(c, z, 0).wait_recv()
        pl.when(jnp.logical_and(c < z, z < LINE - 1))(lambda: self.to_line(c, z + 1, 0).start())
        pl.when(jnp.logical_and(c > z, z > 0))(lambda: self.to_line(c, z - 1, 1).start())
        self.to_core(c).start()

    def arrive_first(self):
        self.arrive(self.pl.order(1))
        pl.when(self.pl.ends == 0)(lambda: self.arrive(self.pl.order(2)))

    def arrive_second(self):
        self.arrive(self.pl.order(3 - self.pl.ends))

    def arrive_third(self):
        pl.when(self.pl.ends == 1)(lambda: self.arrive(self.pl.order(3)))

    def ready(self, c):
        self.from_core(c).wait_recv()

    def finish(self):
        z = self.pl.z

        def body(c, carry):
            pl.when(jnp.logical_and(c <= z, z < LINE - 1))(
                lambda: self.to_line(c, z, 0).wait_send()
            )
            pl.when(jnp.logical_and(c >= z, z > 0))(lambda: self.to_line(c, z, 1).wait_send())
            self.to_core(c).wait_send()
            return carry

        lax.fori_loop(0, LINE, body, 0)


class RowSum:
    def __init__(self, place, h, buffers, sems):
        self.pl, self.h = place, h
        self.term, self.pair_out, self.pair_in, self.keep, self.mine, self.line_out, self.line_in = buffers
        self.p_send, self.p_recv, self.l_send, self.l_recv = sems

    def pair(self, c):
        h = self.h
        return remote(
            self.pair_out.at[h, c], self.pair_in.at[h, c], self.p_send.at[h, c], self.p_recv.at[h, c],
            self.pl.partner,
        )

    def line(self, c, slot, target):
        h = self.h
        return remote(
            self.line_out.at[h, c], self.line_in.at[h, slot], self.l_send.at[h, c],
            self.l_recv.at[h, slot], self.pl.line(target),
        )

    def mate(self):
        return self.pl.z + 1 - 2 * (self.pl.z % 2)

    def give(self, c, s):
        h, k = self.h, self.pl.k
        self.pair_out[h, c] = self.term[1 - k].astype(BF16)
        self.pair(c).start()
        self.keep[h, s % 2] = self.term[k]

    def pass_on(self, c, s):
        h, z = self.h, self.pl.z
        near = c // 2 == z // 2
        end = self.pl.ends == 1
        self.pair(c).wait_recv()

        @pl.when(c == z)
        def _():
            self.mine[h] = self.keep[h, s % 2] + self.pair_in[h, c].astype(F32)

        @pl.when(c != z)
        def _():
            self.line_out[h, c] = (self.keep[h, s % 2] + self.pair_in[h, c].astype(F32)).astype(BF16)

        pl.when(jnp.logical_and(c != z, near))(lambda: self.line(c, z, c).start())
        pl.when(jnp.logical_and(jnp.logical_not(near), end))(
            lambda: self.line(c, 2 * c - 3 * (1 - z // 2), self.mate()).start()
        )

    def relay(self, far):
        h, z = self.h, self.pl.z

        @pl.when(self.pl.ends == 0)
        def _():
            c = 3 * (2 - z) if far else 3 - z
            slot = 2 * c - 3 * (2 - z)
            self.line(c, slot, z).wait_recv()
            self.line_out[h, c] = (
                self.line_out[h, c].astype(F32) + self.line_in[h, slot].astype(F32)
            ).astype(BF16)
            self.line(c, z, c).start()

    def total(self):
        h, z = self.h, self.pl.z
        result = self.mine[h]
        for source in (self.mate(), 2 - z // 2):
            self.line(source, source, source).wait_recv()
            result = result + self.line_in[h, source].astype(F32)
        return result

    def finish(self):
        z = self.pl.z

        def body(c, carry):
            self.pair(c).wait_send()
            pl.when(c != z)(lambda: self.line(c, z, c).wait_send())
            return carry

        lax.fori_loop(0, LINE, body, 0)


class Ring:
    def __init__(self, place, buf, rows, send, recv):
        self.pl, self.buf, self.rows = place, buf, rows
        self.send, self.recv = send, recv

    def block(self, p):
        return self.buf.at[at128(p * self.rows, self.rows)]

    def half(self, p, i):
        size = self.rows // 2
        return self.buf.at[at128(p * self.rows + i * size, size)]

    def own(self, way):
        part = self.block(self.pl.p)
        return remote(part, part, self.send.at[way], self.recv.at[way], (self.pl.x, self.pl.y)[way])

    def far(self, i):
        part = self.half((self.pl.p_x, self.pl.p_y)[i], i)
        return remote(part, part, self.send.at[2 + i], self.recv.at[2 + i], (self.pl.y, self.pl.x)[i])

    def start(self):
        self.own(0).start()
        self.own(1).start()

    def forward(self):
        for i in range(2):
            part = self.block((self.pl.p_x, self.pl.p_y)[i])
            remote(part, part, self.send.at[i], self.recv.at[i], (self.pl.x, self.pl.y)[i]).wait_recv()
            self.far(i).start()

    def ready(self):
        for i in range(2):
            part = self.half(self.pl.p_d, i)
            remote(part, part, self.send.at[2 + i], self.recv.at[2 + i], self.pl.x).wait_recv()

    def finish(self):
        for i in range(2):
            self.own(i).wait_send()
            self.far(i).wait_send()


def scale_columns(totals, rows, which):
    pick = (lax.broadcasted_iota(jnp.int32, (8, 128), 0) == which).astype(F32)
    return exact(totals[:, rows], pick, ((0,), (0,)))


def forward_kernel(
    pairs, gain_query, gain_key, gain_attn, gain_mlp, tokens, cotangent,
    w_query, w_key, w_value, w_out, w_gate, w_up, w_down,
    o_out, o_dmlp, o_gm, o_branch, o_tot,
    o_qkv, o_wo, o_g, o_u, o_dn, o_x, o_m, o_ga, o_ua, o_hid, o_raw, o_heads, o_probs, o_att, o_tab,
    qkv, wo, wg, wu, wd, xs, ms, ga, ua, hid, raw, heads, probs, att, tab, posr, posc,
    term, pair_out, pair_in, keep, mine, line_out, line_in,
    sq_own, sq_pair, sq_both, sq_line, mid, gains_qk, branch_kept,
    loc_sem, swap_send, swap_recv, ring_send, ring_recv, wo_send, wo_recv,
    zs, zr, cs, cr, ps, pr, ls, lr, ts, tr, as_, ar, out_sem,
):
    place = Place()
    z, f, p, k = place.z, place.f, place.p, place.k
    rows = 128
    width = 2048
    cols = 256
    seq = 512
    place.barrier()

    for i, ref in enumerate((gain_query, gain_key)):
        gains_qk[i : i + 1, :] = ref[:, at128(256 * (2 * z + k), 256)]

    def own_rows(n):
        return at128(n * (2 * p + k), n)

    def strips(core):
        return [1024 * (2 * q + core) + 256 * z for q in range(PLANE)]

    local, swap = {}, {}

    def split(name, w, buf, sources, first):
        local[name], swap[name] = [], []
        for i, (mine, theirs) in enumerate(sources):
            dst = buf.at[own_rows(256), pl.ds(256 * i + first[1], 256)]
            local[name].append(
                pltpu.make_async_copy(w.at[:, at128(mine, 256)], dst, loc_sem.at[first[0] + i])
            )
            swap[name].append(
                remote(
                    w.at[:, at128(theirs, 256)], dst, swap_send.at[first[0] + i],
                    swap_recv.at[first[0] + i], place.partner,
                )
            )

    head_cols = [(256 * (2 * z + k), 256 * (2 * z + 1 - k))]
    hid_cols = list(zip(strips(k), strips(1 - k)))
    split("q", w_query, qkv, head_cols, (0, 0))
    split("k", w_key, qkv, head_cols, (1, 256))
    split("v", w_value, qkv, head_cols, (2, 512))
    split("g", w_gate, wg, hid_cols, (3, 0))
    split("u", w_up, wu, hid_cols, (7, 0))

    def begin(*names):
        for name in names:
            for a, b in zip(local[name], swap[name]):
                b.start()
                a.start()

    def settle(*names):
        for name in names:
            for a, b in zip(local[name], swap[name]):
                a.wait()
                b.wait_recv()

    dx, dy = (p % 2 + z % 2) % 2, (p // 2 + z // 2) % 2
    top, low = wo.at[pl.ds(0, 128)], wo.at[pl.ds(128, 128)]
    wo_copy = pltpu.make_async_copy(w_out, wo, loc_sem.at[12])

    def wo_first(i, device):
        rows_i = pl.ds(128 * i, 128)
        return remote(w_out.at[rows_i], wo.at[rows_i], wo_send.at[i], wo_recv.at[i], device)

    def wo_send_to(i, part, device):
        return remote(part, part, wo_send.at[i], wo_recv.at[i], device)

    is_source = jnp.logical_and(dx == 0, dy == 0)
    is_x = jnp.logical_and(dx == 1, dy == 0)
    is_y = jnp.logical_and(dx == 0, dy == 1)
    is_d = jnp.logical_and(dx == 1, dy == 1)

    @pl.when(is_source)
    def _():
        wo_copy.start()
        wo_first(0, place.x).start()
        wo_first(1, place.y).start()

    begin("q", "k", "v")
    xs[z, k] = tokens[...]
    gather_x = Gather(place, xs, zs.at[0], zr.at[0], cs.at[0], cr.at[0])
    gather_x.start()
    down_copies = [
        pltpu.make_async_copy(
            w_down.at[at128(256 * z, 256), pl.ds(1024 * h, 1024)], wd.at[h, at128(256 * p, 256)],
            loc_sem.at[(11, 13)[h]],
        )
        for h in range(2)
    ]
    for copy in down_copies:
        copy.start()
    begin("g", "u")
    ring_qkv = Ring(place, qkv, 512, ring_send.at[0], ring_recv.at[0])
    ring_g = Ring(place, wg, 512, ring_send.at[1], ring_recv.at[1])
    ring_u = Ring(place, wu, 512, ring_send.at[2], ring_recv.at[2])
    ring_d = [Ring(place, wd.at[h], 256, ring_send.at[3 + h], ring_recv.at[3 + h]) for h in range(2)]
    settle("q", "k", "v")
    ring_qkv.start()

    def positions(shape, axis):
        i = lax.broadcasted_iota(jnp.int32, shape, axis)
        block = i // 64
        pos = jnp.zeros(shape, jnp.int32)
        for r in range(LINE):
            b = pairs[0, r]
            pos = pos + jnp.where(block == 2 * r, b * 64, 0)
            pos = pos + jnp.where(block == 2 * r + 1, (2 * LINE - 1 - b) * 64, 0)
        return (pos + i % 64).astype(F32)

    posr[k] = positions((8, seq), 1)
    col = positions((seq, 128), 0)
    posc[k] = col
    lane = lax.broadcasted_iota(jnp.int32, (seq, 128), 1)
    freq = jnp.exp((lane % 64).astype(F32) * (-2.0 / HD * math.log(ROPE_BASE)))
    angle = col * freq
    tab[0, k] = jnp.cos(angle)
    sine = jnp.sin(angle)
    tab[1, k] = jnp.where(lane < 64, -sine, sine)
    tables = [
        remote(r, r, ts.at[i], tr.at[i], place.partner)
        for i, r in enumerate([posr.at[k], posc.at[k], tab.at[0, k], tab.at[1, k]])
    ]
    for t in tables:
        t.start()

    gather_x.arrive_first()
    pl.when(is_x)(lambda: wo_send_to(0, top, place.x).wait_recv())
    pl.when(is_x)(lambda: wo_send_to(0, top, place.y).start())
    pl.when(is_y)(lambda: wo_send_to(1, low, place.x).wait_recv())
    pl.when(is_y)(lambda: wo_send_to(1, low, place.x).start())
    ring_qkv.forward()
    settle("g", "u")
    gather_x.arrive_second()

    @pl.when(is_d)
    def _():
        wo_send_to(0, top, place.x).wait_recv()
        wo_send_to(0, top, place.x).start()
        wo_send_to(1, low, place.x).wait_recv()
        wo_send_to(1, low, place.y).start()

    ring_g.start()
    ring_qkv.ready()

    def project(c):
        gather_x.ready(c)
        chunk = xs[c].reshape(2 * rows, width)
        there = at128(c * rows)
        sums = jnp.zeros((8, 2 * rows), F32)
        pick = lax.broadcasted_iota(jnp.int32, (8, cols), 0)
        for i in range(2):
            part = dot(chunk, qkv[:, i * cols : (i + 1) * cols])
            raw[i, :, there] = part.reshape(2, rows, cols)
            sums = sums + exact((pick == i).astype(F32), part * part, ((1,), (1,)))
        part = dot(chunk, qkv[:, 2 * cols :])
        heads[2, :, there] = part.astype(BF16).reshape(2, rows, cols)
        sq_own[c] = sums

    def project_step(s, carry):
        project(place.order(s))
        return carry

    lax.fori_loop(0, 3, project_step, 0)
    gather_x.arrive_third()
    lax.fori_loop(3, 4, project_step, 0)

    pair_sq = remote(sq_own, sq_pair, as_.at[0], ar.at[0], place.partner)
    pair_sq.start()
    ring_u.start()
    pair_sq.wait_recv()
    sq_both[...] = sq_own[...] + sq_pair[...]

    def line_sq(step, source):
        return remote(
            sq_both, sq_line.at[source], as_.at[step], ar.at[1 + source],
            place.line((z + step) % LINE),
        )

    for step in range(1, LINE):
        line_sq(step, z).start()
    for t in tables:
        t.wait_recv()
    for step in range(1, LINE):
        line_sq(step, (z + step) % LINE).wait_recv()
    sq_line[z] = sq_both[...]
    total = (sq_line[0] + sq_line[1]) + (sq_line[2] + sq_line[3])
    scales = lax.rsqrt(total / width + EPSILON)
    o_tot[...] = scales

    def rotate(c, carry):
        there = at128(c * rows)
        now = o_tot[c]
        for i in range(2):
            pick = (lax.broadcasted_iota(jnp.int32, (8, 128), 0) == i).astype(F32)
            column = exact(now, pick, ((0,), (0,)))
            for s in range(2):
                for h in range(2):
                    lanes = slice(128 * h, 128 * h + 128)
                    v = raw[i, s, there, lanes] * column[128 * s : 128 * s + 128]
                    v = v * gains_qk[i : i + 1, lanes]
                    v = v * tab[0, s, there] + pltpu.roll(v, 64, 1) * tab[1, s, there]
                    heads[i, s, there, lanes] = v.astype(BF16)
        return carry

    lax.fori_loop(0, LINE, rotate, 0)

    def attend(s, carry):
        mask = posr[s, 0:1, :] <= posc[s][:, 0:1]
        for h in range(2):
            lanes = slice(128 * h, 128 * h + 128)
            scores = dot_rt(heads[0, s, :, lanes], heads[1, s, :, lanes]) * (HD ** -0.5)
            scores = jnp.where(mask, scores, NEGATIVE)
            e = jnp.exp(scores - jnp.max(scores, axis=1, keepdims=True))
            low_p = (e / jnp.sum(e, axis=1, keepdims=True)).astype(BF16)
            probs[s, h] = low_p
            att[s, :, lanes] = dot(low_p, heads[2, s, :, lanes]).astype(BF16)
        return carry

    lax.fori_loop(0, 2, attend, 0)

    pl.when(is_source)(lambda: wo_copy.wait())
    pl.when(is_x)(lambda: wo_send_to(1, low, place.x).wait_recv())
    pl.when(is_y)(lambda: wo_send_to(0, top, place.x).wait_recv())

    ring_g.forward()
    buffers = (term, pair_out, pair_in, keep, mine, line_out, line_in)
    sums = [RowSum(place, h, buffers, (ps, pr, ls, lr)) for h in range(2)]

    def branch_step(s, carry):
        c = place.order(3 - s)
        left = att[:, at128(c * rows)].reshape(2 * rows, cols)
        for h in range(2):
            term[...] = dot(left, wo[:, 1024 * h : 1024 * h + 1024]).reshape(2, rows, 1024)
            sums[h].give(c, s)
        for h in range(2):
            pl.when(s > 0)(lambda h=h: sums[h].pass_on(place.order(4 - s), s + 1))
        return carry

    lax.fori_loop(0, 4, branch_step, 0)
    for h in range(2):
        sums[h].pass_on(z, 3)
    for h in range(2):
        sums[h].relay(True)
    ring_u.forward()
    for h in range(2):
        sums[h].relay(False)
    for copy in down_copies:
        copy.wait()
    ring_d[0].start()
    branch = jnp.concatenate([sums[h].total() for h in range(2)], axis=1)
    for h in range(2):
        sums[h].finish()
    branch_kept[...] = branch

    def mean_sq(v):
        return jnp.sum(v * v, axis=1, keepdims=True) / width

    mid[...] = tokens[...].astype(F32) + branch * lax.rsqrt(mean_sq(branch) + EPSILON) * gain_attn[...]
    ms[z, k] = mid[...].astype(BF16)
    gather_m = Gather(place, ms, zs.at[1], zr.at[1], cs.at[1], cr.at[1])
    gather_m.start()

    ring_d[0].forward()
    ring_d[1].start()
    ring_g.ready()
    ring_u.ready()

    def expand(s, carry):
        c = place.order(s)
        gather_m.ready(c)
        chunk = ms[c].reshape(2 * rows, width)

        def body(t, inner):
            lanes = at128(t * 256, 256)
            g = dot(chunk, wg[:, lanes])
            u = dot(chunk, wu[:, lanes])
            ga[c, :, lanes] = g.astype(BF16)
            ua[c, :, lanes] = u.astype(BF16)
            hid[c, :, lanes] = (g / (1.0 + jnp.exp(-g)) * u).astype(BF16)
            return inner

        lax.fori_loop(0, 4, body, 0)
        return carry

    def contract(h, first, last):
        def step(s, carry):
            c = place.order(s)
            term[...] = dot(hid[c], wd[h]).reshape(2, rows, 1024)
            sums[h].give(c, s)
            pl.when(s > first)(lambda: sums[h].pass_on(place.order(s - 1), s + 1))
            return carry

        lax.fori_loop(first, last, step, 0)

    def flush(h, last):
        sums[h].pass_on(place.order(last - 1), last - 1)

    lax.fori_loop(0, 1, expand, 0)
    gather_m.arrive_first()
    lax.fori_loop(1, 2, expand, 0)
    ring_d[0].ready()
    contract(0, 0, 2)
    gather_m.arrive_second()
    flush(0, 2)
    ring_d[1].forward()
    lax.fori_loop(2, 3, expand, 0)
    contract(0, 2, 3)
    ring_d[1].ready()
    flush(0, 3)
    contract(1, 0, 3)
    gather_m.arrive_third()
    flush(1, 3)
    lax.fori_loop(3, 4, expand, 0)
    contract(0, 3, 4)
    contract(1, 3, 4)
    for h in range(2):
        flush(h, 4)
    for h in range(2):
        sums[h].relay(False)
    for h in range(2):
        sums[h].relay(True)

    saves = [
        (qkv, o_qkv), (wo, o_wo), (wg, o_g), (wu, o_u), (wd.at[0], o_dn.at[:, pl.ds(0, 1024)]),
        (wd.at[1], o_dn.at[:, pl.ds(1024, 1024)]), (xs, o_x), (ms, o_m), (ga, o_ga),
        (ua, o_ua), (hid, o_hid), (raw, o_raw), (heads, o_heads), (probs, o_probs), (att, o_att),
        (tab, o_tab), (branch_kept, o_branch),
    ]
    copies = [pltpu.make_async_copy(a, b, out_sem.at[i]) for i, (a, b) in enumerate(saves)]
    for copy in copies:
        copy.start()

    mlp = jnp.concatenate([sums[h].total() for h in range(2)], axis=1)
    for h in range(2):
        sums[h].finish()
    c_m = lax.rsqrt(mean_sq(mlp) + EPSILON)
    gain = gain_mlp[...]
    o_out[...] = (mid[...] + mlp * c_m * gain).astype(BF16)
    dy = cotangent[...].astype(F32)
    gdy = gain * dy
    inner = jnp.sum(mlp * gdy, axis=1, keepdims=True) / width
    o_dmlp[...] = (c_m * gdy - mlp * (c_m * c_m * c_m * inner)).astype(BF16)
    o_gm[...] = jnp.sum(dy * mlp * c_m, axis=0, keepdims=True)

    gather_x.finish()
    gather_m.finish()
    for ring in (ring_qkv, ring_g, ring_u, *ring_d):
        ring.finish()
    for group in swap.values():
        for copy in group:
            copy.wait_send()
    for t in tables:
        t.wait_send()
    pair_sq.wait_send()
    for step in range(1, LINE):
        line_sq(step, z).wait_send()

    @pl.when(is_source)
    def _():
        wo_first(0, place.x).wait_send()
        wo_first(1, place.y).wait_send()

    pl.when(is_x)(lambda: wo_send_to(0, top, place.y).wait_send())
    pl.when(is_y)(lambda: wo_send_to(1, low, place.x).wait_send())

    @pl.when(is_d)
    def _():
        wo_send_to(0, top, place.x).wait_send()
        wo_send_to(1, low, place.y).wait_send()

    for copy in copies:
        copy.wait()


def any_spec():
    return pl.BlockSpec(memory_space=pl.ANY)


def vmem_spec():
    return pl.BlockSpec(memory_space=pltpu.VMEM)


def run_forward(pairs, gain_query, gain_key, gain_attn, gain_mlp, tokens, cotangent, weights):
    shape = jax.ShapeDtypeStruct
    dma = pltpu.SemaphoreType.DMA
    kept = [
        shape((2048, 768), BF16),
        shape((256, 2048), BF16),
        shape((2048, 1024), BF16),
        shape((2048, 1024), BF16),
        shape((1024, 2048), BF16),
        shape((4, 2, 128, 2048), BF16),
        shape((4, 2, 128, 2048), BF16),
        shape((4, 256, 1024), BF16),
        shape((4, 256, 1024), BF16),
        shape((4, 256, 1024), BF16),
        shape((2, 2, 512, 256), F32),
        shape((3, 2, 512, 256), BF16),
        shape((2, 2, 512, 512), BF16),
        shape((2, 512, 256), BF16),
        shape((2, 2, 512, 128), F32),
    ]
    return pl.pallas_call(
        forward_kernel,
        name="forward",
        out_shape=[
            shape((128, 2048), BF16),
            shape((128, 2048), BF16),
            shape((1, 2048), F32),
            shape((128, 2048), F32),
            shape((4, 8, 256), F32),
        ]
        + kept,
        in_specs=[pl.BlockSpec(memory_space=pltpu.SMEM)] + [vmem_spec()] * 6 + [any_spec()] * 7,
        out_specs=[vmem_spec()] * 3 + [any_spec(), vmem_spec()] + [any_spec()] * len(kept),
        scratch_shapes=[pltpu.VMEM((2, 1024, 1024) if i == 4 else k.shape, k.dtype) for i, k in enumerate(kept)]
        + [
            pltpu.VMEM((2, 8, 512), F32),
            pltpu.VMEM((2, 512, 128), F32),
            pltpu.VMEM((2, 128, 1024), F32),
            pltpu.VMEM((2, 4, 128, 1024), BF16),
            pltpu.VMEM((2, 4, 128, 1024), BF16),
            pltpu.VMEM((2, 2, 128, 1024), F32),
            pltpu.VMEM((2, 128, 1024), F32),
            pltpu.VMEM((2, 4, 128, 1024), BF16),
            pltpu.VMEM((2, 4, 128, 1024), BF16),
            pltpu.VMEM((4, 8, 256), F32),
            pltpu.VMEM((4, 8, 256), F32),
            pltpu.VMEM((4, 8, 256), F32),
            pltpu.VMEM((4, 4, 8, 256), F32),
            pltpu.VMEM((128, 2048), F32),
            pltpu.VMEM((2, 256), F32),
            pltpu.VMEM((128, 2048), F32),
            dma((14,)),
            dma((11,)),
            dma((11,)),
            dma((5, 4)),
            dma((5, 4)),
            dma((2,)),
            dma((2,)),
            dma((2, 2, 4)),
            dma((2, 4)),
            dma((2, 4)),
            dma((2, 4)),
            dma((2, 4)),
            dma((2, 4)),
            dma((2, 4)),
            dma((2, 4)),
            dma((4,)),
            dma((4,)),
            dma((4,)),
            dma((5,)),
            dma((len(kept) + 2,)),
        ],
        compiler_params=pltpu.CompilerParams(
            collective_id=0, has_side_effects=True, vmem_limit_bytes=64 * 1024 * 1024
        ),
    )(pairs, gain_query, gain_key, gain_attn, gain_mlp, tokens, cotangent, *weights)


def backward_kernel(
    gain_query, gain_key, gain_attn, d_mlp, h_cot, h_branch, scales, gm_part,
    h_qkv, h_wo, h_g, h_u, h_dn, h_x, h_m, h_ga, h_ua, h_hid, h_raw, h_heads, h_probs, h_att, h_tab,
    o_tok, o_down, o_out, o_gu, o_qkv,
    st_g, rc_g, st_u, rc_u, st_dn, rc_dn, st_qkv, rc_qkv, st_out, rc_out,
    wd, wg, wu, ga, ua, hid, dm, dg, du, ms, db, raw, tab, datt, dy,
    term, pair_out, pair_in, keep, mine, line_out, line_in,
    sq_own, sq_pair, sq_both, sq_line, gn_own, d_mid, stage, stage_d, far_in, gains_qk, cotangent, branch,
    ld, far_sem, zs, zr, cs, cr, ps, pr, ls, lr, as_, ar, in_send, in_recv, st_sem, sum_sem,
    fin_send, fin_recv, fin_loc, al_send, al_recv, al_loc,
):
    place = Place()
    z, f, p, k = place.z, place.f, place.p, place.k
    rows, width, cols = 128, 2048, 256

    def strip_of(chip, plane):
        return (chip % 2 + plane // 2) % 2 + 2 * ((chip // 2 + plane % 2) % 2)

    down_to = (strip_of(p, z), 4 * k + z)
    down_from = (f % 4, 2 * strip_of(z, f % 4) + f // 4)
    down_moves = jnp.logical_or(down_to[0] != z, down_to[1] != f)
    out_to = (z, 4 * k + p)
    out_from = (z, 2 * (f % 4) + f // 4)
    out_moves = out_to[1] != f
    place.barrier(
        [place.d] + [place.cross((z + step) % LINE) for step in range(1, LINE)],
        [(down_moves, down_from), (out_moves, out_from)],
    )

    for i, ref in enumerate((gain_query, gain_key)):
        gains_qk[i : i + 1, :] = ref[:, at128(256 * (2 * z + k), 256)]
    loads = {}

    def load(name, src, dst):
        loads[name] = pltpu.make_async_copy(src, dst, ld.at[len(loads)])
        loads[name].start()

    dm[at128(z * 256 + k * rows)] = d_mlp[...]

    class Rows:
        def __init__(self, ref):
            self.ref = ref

        @property
        def at(self):
            ref = self.ref

            class At:
                def __getitem__(self, key):
                    c, core = key
                    return ref.at[at128(c * 256 + core * rows)]

            return At()

    gather_d = Gather(place, Rows(dm), zs.at[0], zr.at[0], cs.at[0], cr.at[0])
    gather_d.start()
    load("wd", h_dn, wd)
    load("ga", h_ga, ga)
    load("ua", h_ua, ua)
    load("wg", h_g, wg)
    load("wu", h_u, wu)
    load("hid", h_hid, hid)
    load("ms", h_m, ms)
    load("cot", h_cot, cotangent)
    load("branch", h_branch, branch)
    load("raw", h_raw, raw)
    load("tab", h_tab, tab)

    buffers = (term, pair_out, pair_in, keep, mine, line_out, line_in)
    sums = [RowSum(place, h, buffers, (ps, pr, ls, lr)) for h in range(2)]

    def chunk_rows(c):
        return at128(c * 256, 256)

    def expand(s, carry):
        c = place.order(s)
        gather_d.ready(c)
        here = chunk_rows(c)
        grad = dm[here]

        def act(t, inner):
            lanes = at128(t * 256, 256)
            dh = dot_rt(grad, wd[lanes])
            g = ga[here, lanes].astype(F32)
            u = ua[here, lanes].astype(F32)
            sig = 1.0 / (1.0 + jnp.exp(-g))
            dg[here, lanes] = (dh * u * sig * (1.0 + g * (1.0 - sig))).astype(BF16)
            du[here, lanes] = (dh * g * sig).astype(BF16)
            return inner

        lax.fori_loop(0, 4, act, 0)
        return carry

    def contract(s, carry):
        c = place.order(s)
        here = chunk_rows(c)
        left_g, left_u = dg[here], du[here]
        for h in range(2):
            out = slice(1024 * h, 1024 * h + 1024)
            term[...] = (dot_rt(left_g, wg[out]) + dot_rt(left_u, wu[out])).reshape(2, rows, 1024)
            sums[h].give(c, s)
        for h in range(2):
            pl.when(s > 0)(lambda h=h: sums[h].pass_on(place.order(s - 1), s + 1))
        return carry

    for name in ("wd", "ga", "ua"):
        loads[name].wait()
    lax.fori_loop(0, 1, expand, 0)
    for name in ("wg", "wu"):
        loads[name].wait()
    gather_d.arrive_first()
    lax.fori_loop(0, 1, contract, 0)
    for s in (1, 2):
        if s == 2:
            gather_d.arrive_second()
        lax.fori_loop(s, s + 1, expand, 0)
        lax.fori_loop(s, s + 1, contract, 0)
    gather_d.arrive_third()
    lax.fori_loop(3, 4, expand, 0)
    lax.fori_loop(3, 4, contract, 0)
    for h in range(2):
        sums[h].pass_on(place.order(3), 3)
    load("x", h_x, wd)
    load("qkv", h_qkv, wg.at[:, pl.ds(0, 768)])
    load("probs", h_probs, wu.at[:, pl.ds(0, 512)])
    load("qk", h_heads.at[pl.ds(0, 2048)], wu.at[:, pl.ds(512, 256)])
    load("v", h_heads.at[pl.ds(2048, 1024)], wu.at[pl.ds(0, 1024), pl.ds(768, 256)])
    load("att", h_att, wu.at[pl.ds(1024, 1024), pl.ds(768, 256)])

    chips = [place.p_x, place.p_y, place.p_d, p]
    near = [place.x, place.y, place.d]
    GATE, UP, DOWN, QKV, OUT = range(5)
    kinds = {GATE: (st_g, rc_g), UP: (st_u, rc_u), DOWN: (st_dn, rc_dn), QKV: (st_qkv, rc_qkv)}

    def half_of(kind, ref, i, half):
        if kind == DOWN:
            return ref.at[i, :, pl.ds(1024 * half, 1024)]
        return ref.at[i, pl.ds(256 * half, 256)]

    def far_part(kind, half):
        st, rc = kinds[kind]
        return remote(
            half_of(kind, st, 2, half), half_of(kind, rc, 2, half), in_send.at[kind, 2 + half],
            in_recv.at[kind, 2 + half], near[half],
        )

    def near_part(kind, i):
        st, rc = kinds[kind]
        return remote(st.at[i], rc.at[i], in_send.at[kind, i], in_recv.at[kind, i], near[i])

    def put(kind, i, buf, sem):
        wide = 896 if kind == QKV else 1024
        if i < 2:
            half = 1 - i
            far_part(kind, half).wait_recv()
            got = far_in.at[:, pl.ds(0, wide)]
            copy = pltpu.make_async_copy(half_of(kind, kinds[kind][1], 2, half), got, far_sem)
            copy.start()
            copy.wait()
            if kind == DOWN:
                now = (slice(None), slice(1024 * half, 1024 * half + 1024))
            else:
                now = (slice(256 * half, 256 * half + 256), slice(0, wide))
            buf[now] = (buf[now].astype(F32) + far_in[:, 0:wide].astype(F32)).astype(BF16)
        src = buf.at[:, pl.ds(0, 896)] if kind == QKV else buf
        copy = pltpu.make_async_copy(src, kinds[kind][0].at[i], st_sem.at[sem])
        copy.start()
        copy.wait()
        if i == 2:
            far_part(kind, 0).start()
            far_part(kind, 1).start()
        elif i < 2:
            near_part(kind, i).start()

    def feature_rows(ref, chip):
        return jnp.concatenate([ref[:, at128(512 * c + 128 * chip)] for c in range(LINE)], axis=1).T

    def gate_up_part(i):
        left = feature_rows(ms, chips[i])
        for m, right in enumerate((dg, du)):
            for t in range(2):
                lanes = slice(512 * t, 512 * t + 512)
                stage[m, :, lanes] = dot(left, right[:, lanes]).astype(BF16)
            put(m, i, stage.at[m], m)

    def down_part(i):
        left = hid[:, at128(strip_of(chips[i], z) * 256, 256)].T
        for t in range(4):
            lanes = slice(512 * t, 512 * t + 512)
            stage_d[:, lanes] = dot(left, dm[:, lanes]).astype(BF16)
        put(DOWN, i, stage_d, 2)

    loads["ms"].wait()
    loads["hid"].wait()
    gate_up_part(2)
    for h in range(2):
        sums[h].relay(False)
    down_part(2)
    gate_up_part(3)
    for h in range(2):
        sums[h].relay(True)
    gate_up_part(0)
    gate_up_part(1)
    gather_d.finish()

    def mean_of(v):
        return jnp.sum(v, axis=1, keepdims=True) / width

    loads["cot"].wait()
    loads["branch"].wait()
    d_mid[...] = cotangent[...].astype(F32) + jnp.concatenate([sums[h].total() for h in range(2)], axis=1)
    for h in range(2):
        sums[h].finish()
    b = branch[...]
    c_b = lax.rsqrt(mean_of(b * b) + EPSILON)
    gdy = gain_attn[...] * d_mid[...]
    db[at128(z * 256 + k * rows)] = (
        c_b * gdy - b * (c_b * c_b * c_b * mean_of(b * gdy))
    ).astype(BF16)
    gather_b = Gather(place, Rows(db), zs.at[1], zr.at[1], cs.at[1], cr.at[1])
    gather_b.start()
    gn_own[...] = jnp.zeros((8, width), F32)
    gn_own[2:3, :] = jnp.sum(d_mid[...] * b * c_b, axis=0, keepdims=True)
    gn_own[3:4, :] = gm_part[...]

    down_part(3)
    down_part(0)
    down_part(1)
    load("wo", h_wo, stage_d)

    for name in ("wo", "raw", "tab", "x", "qkv", "probs", "qk", "v", "att"):
        loads[name].wait()

    def attended_step(s, carry):
        c = place.order(s)
        gather_b.ready(c)
        part = dot_rt(db[chunk_rows(c)], stage_d[...]).astype(BF16)
        datt[:, at128(c * rows)] = part.reshape(2, rows, cols)
        return carry

    gather_b.arrive_first()
    lax.fori_loop(0, 2, attended_step, 0)
    gather_b.arrive_second()
    lax.fori_loop(2, 3, attended_step, 0)

    def fetch(kind, parts, first):
        copies = [
            pltpu.make_async_copy(src, dst, sum_sem.at[first + n]) for n, (src, dst) in enumerate(parts)
        ]
        for copy in copies:
            copy.start()
        for copy in copies:
            copy.wait()

    def to_owner(kind, src, dst):
        def go(c, core, device):
            return remote(
                src(c, core), dst.at[z, k], al_send.at[kind, c, core], al_recv.at[kind, z, k], device
            )

        def each(action):
            for step in range(1, LINE):
                c = (z + step) % LINE
                action(go(c, k, place.line(c)))
                action(go(c, 1 - k, place.cross(c)))
            action(go(z, 1 - k, place.partner))

        here = pltpu.make_async_copy(src(z, k), dst.at[z, k], al_loc.at[kind])
        each(lambda copy: copy.start())
        here.start()

        def wait():
            here.wait()
            each(lambda copy: copy.wait_send())
            for step in range(LINE):
                c = (z + step) % LINE
                for core in (0, 1):
                    got = remote(
                        src(c, k), dst.at[c, core], al_send.at[kind, c, core], al_recv.at[kind, c, core],
                        place.partner,
                    )
                    if step == 0:
                        pl.when(k != core)(lambda got=got: got.wait_recv())
                    else:
                        got.wait_recv()

        return wait

    waits = []

    def square_sum(kind, buf, other, lanes, dst):
        st, rc = kinds[kind]
        cut = pl.ds(0, lanes)
        near_part(kind, 0).wait_recv()
        near_part(kind, 1).wait_recv()
        fetch(
            kind,
            [
                (st.at[3], buf.at[pl.ds(0, 512), cut]),
                (rc.at[0], buf.at[pl.ds(512, 512), cut]),
                (rc.at[1], other.at[pl.ds(0, 512), cut]),
            ],
            3 * kind,
        )

        def add_up(t, carry):
            there = at128(t * 128)
            acc = buf[there, 0:lanes].astype(F32) + buf[at128(512 + t * 128), 0:lanes].astype(F32)
            buf[there, 0:lanes] = (acc + other[there, 0:lanes].astype(F32)).astype(BF16)
            return carry

        lax.fori_loop(0, 4, add_up, 0)
        waits.append(
            to_owner(
                min(kind, 2), lambda c, core: buf.at[at128(c * 128 + core * 64, 64), cut], dst
            )
        )

    square_sum(GATE, hid, ua, 1024, o_gu.at[0])
    gather_b.arrive_third()
    lax.fori_loop(3, 4, attended_step, 0)

    def attend(s, carry):
        there = at128(s * 512, 512)
        for h in range(2):
            lanes = slice(128 * h, 128 * h + 128)
            more = slice(512 + 128 * h, 640 + 128 * h)
            vals = slice(768 + 128 * h, 896 + 128 * h)
            low_p = wu[at128((2 * s + h) * 512, 512), 0:512]
            grad = datt[s, :, lanes]
            q = wu[there, more]
            key = wu[at128(1024 + s * 512, 512), more]
            value = wu[there, vals]
            d_value = dot_lt(low_p, grad).astype(BF16)
            d_probs = dot_rt(grad, value)
            pr32 = low_p.astype(F32)
            delta = jnp.sum(pr32 * d_probs, axis=1, keepdims=True)
            d_scores = (pr32 * (d_probs - delta)).astype(BF16)
            d_q = dot(d_scores, key) * (HD ** -0.5)
            d_k = dot_lt(d_scores, q) * (HD ** -0.5)
            for i, d in enumerate((d_q, d_k)):
                dy[i, s, :, lanes] = d * tab[0, s] - pltpu.roll(d, 64, 1) * tab[1, s]
            for c in range(LINE):
                ga[c * 256 + s * rows : c * 256 + s * rows + rows, vals.start - 256 : vals.stop - 256] = (
                    d_value[c * rows : c * rows + rows]
                )
        return carry

    for s in range(2):
        attend(s, 0)

    def dots_step(c, carry):
        there = at128(c * rows)
        pick = lax.broadcasted_iota(jnp.int32, (8, cols), 0)
        acc = jnp.zeros((8, 2 * rows), F32)
        for i in range(2):
            part = (raw[i, :, there] * dy[i, :, there]).reshape(2 * rows, cols) * gains_qk[i : i + 1]
            acc = acc + exact((pick == i).astype(F32), part, ((1,), (1,)))
        sq_own[c] = acc
        return carry

    lax.fori_loop(0, LINE, dots_step, 0)
    pair_sq = remote(sq_own, sq_pair, as_.at[0], ar.at[0], place.partner)
    pair_sq.start()
    pair_sq.wait_recv()
    sq_both[...] = sq_own[...] + sq_pair[...]

    def line_sq(step, source):
        return remote(
            sq_both, sq_line.at[source], as_.at[step], ar.at[1 + source], place.line((z + step) % LINE)
        )

    for step in range(1, LINE):
        line_sq(step, z).start()
    square_sum(UP, dg, du, 1024, o_gu.at[1])
    for step in range(1, LINE):
        line_sq(step, (z + step) % LINE).wait_recv()
    sq_line[z] = sq_both[...]

    def normalise(c, gains):
        there = at128(c * rows)
        means = ((sq_line[0, c] + sq_line[1, c]) + (sq_line[2, c] + sq_line[3, c])) / width
        now = scales[c]
        result = []
        for i in range(2):
            pick = (lax.broadcasted_iota(jnp.int32, (8, 128), 0) == i).astype(F32)
            scale = exact(now, pick, ((0,), (0,)))
            mean = exact(means, pick, ((0,), (0,)))
            gain_sum = []
            for h in range(2):
                lanes = slice(128 * h, 128 * h + 128)
                v = raw[i, :, there, lanes].reshape(2 * rows, 128)
                d = dy[i, :, there, lanes].reshape(2 * rows, 128)
                gain_sum.append(jnp.sum(d * v * scale, axis=0, keepdims=True))
                d = scale * gains_qk[i : i + 1, lanes] * d - v * (scale * scale * scale * mean)
                ga[chunk_rows(c), 256 * i + 128 * h : 256 * i + 128 * h + 128] = d.astype(BF16)
            result.append(gains[i] + jnp.concatenate(gain_sum, axis=1))
        return tuple(result)

    start = (jnp.zeros((1, cols), F32), jnp.zeros((1, cols), F32))
    gain_q, gain_k = lax.fori_loop(0, LINE, normalise, start)
    own_cols = at128(cols * (2 * z + k), cols)
    gn_own[0:1, own_cols] = gain_q
    gn_own[1:2, own_cols] = gain_k

    def token_step(s, carry):
        c = place.order(3 - s)
        left = ga[chunk_rows(c), 0:768]
        for h in range(2):
            term[...] = dot_rt(left, wg[1024 * h : 1024 * h + 1024, 0:768]).reshape(2, rows, 1024)
            sums[h].give(c, s)
        for h in range(2):
            pl.when(s > 0)(lambda h=h: sums[h].pass_on(place.order(4 - s), s + 1))
        return carry

    lax.fori_loop(0, 4, token_step, 0)
    for h in range(2):
        sums[h].pass_on(z, 3)

    def qkv_part(i):
        stage[0, :, 0:768] = dot(feature_rows(wd, chips[i]), ga[:, 0:768]).astype(BF16)
        sides = jnp.concatenate([gn_own[:, at128(512 * c + 128 * chips[i])] for c in range(LINE)], axis=1)
        lane = lax.broadcasted_iota(jnp.int32, (8, 128), 1)
        column = (lax.broadcasted_iota(jnp.int32, (8, 128), 0) == lane).astype(F32)
        stage[0, :, 768:896] = exact(sides, column, ((0,), (0,))).astype(BF16)
        put(QKV, i, stage.at[0], 3)

    qkv_part(2)
    for h in range(2):
        sums[h].relay(True)
    qkv_part(3)
    for s in range(2):
        for c in range(LINE):
            ua[c * 256 + s * rows : c * 256 + s * rows + rows, 0:256] = (
                wu[1024 + s * 512 + c * rows : 1024 + s * 512 + c * rows + rows, 768:1024]
            )

    def outer(t, carry):
        lanes = at128(t * 512, 512)
        stage_d[:, lanes] = dot_lt(ua[:, 0:256], db[:, lanes]).astype(BF16)
        return carry

    lax.fori_loop(0, 4, outer, 0)
    copy = pltpu.make_async_copy(stage_d, st_out, st_sem.at[0])
    copy.start()
    copy.wait()

    def out_part(i):
        return remote(
            st_out.at[at128(64 * chips[i], 64)], rc_out.at[i], in_send.at[OUT, i], in_recv.at[OUT, i], near[i]
        )

    qkv_part(0)
    qkv_part(1)
    for i in range(3):
        out_part(i).start()

    for h in range(2):
        sums[h].relay(False)

    near_part(DOWN, 0).wait_recv()
    near_part(DOWN, 1).wait_recv()
    fetch(
        DOWN,
        [
            (st_dn.at[3], ms.at[pl.ds(0, 256)]),
            (rc_dn.at[0], ms.at[pl.ds(256, 256)]),
            (rc_dn.at[1], ms.at[pl.ds(512, 256)]),
        ],
        3 * DOWN,
    )

    def add_down(t, carry):
        lanes = at128(t * 512, 512)
        acc = ms[0:256, lanes].astype(F32) + ms[256:512, lanes].astype(F32)
        dm[0:256, lanes] = (acc + ms[512:768, lanes].astype(F32)).astype(BF16)
        return carry

    lax.fori_loop(0, 4, add_down, 0)
    down_done = dm.at[pl.ds(0, 256)]
    fin_down = remote(down_done, o_down, fin_send.at[0], fin_recv.at[0], down_to)
    keep_down = pltpu.make_async_copy(down_done, o_down, fin_loc.at[0])
    pl.when(down_moves)(lambda: fin_down.start())
    pl.when(jnp.logical_not(down_moves))(lambda: keep_down.start())

    for h in range(2):
        out = slice(1024 * h, 1024 * h + 1024)
        o_tok[:, out] = (d_mid[:, out] + sums[h].total()).astype(BF16)
        sums[h].finish()

    square_sum(QKV, ua, du, 896, o_qkv)

    for i in range(3):
        out_part(i).wait_recv()
    sources = [rc_out.at[0], rc_out.at[1], rc_out.at[2], st_out.at[at128(64 * p, 64)]]
    copies = [
        pltpu.make_async_copy(src, ms.at[pl.ds(64 * i, 64)], sum_sem.at[16 + i])
        for i, src in enumerate(sources)
    ]
    for copy in copies:
        copy.start()
    for copy in copies:
        copy.wait()
    acc = ms[0:64].astype(F32) + ms[64:128].astype(F32)
    acc = acc + ms[128:192].astype(F32) + ms[192:256].astype(F32)
    ms[256:320] = acc.astype(BF16)
    out_done = ms.at[pl.ds(256, 64)]
    fin_out = remote(out_done, o_out, fin_send.at[1], fin_recv.at[1], out_to)
    keep_out = pltpu.make_async_copy(out_done, o_out, fin_loc.at[1])
    pl.when(out_moves)(lambda: fin_out.start())
    pl.when(jnp.logical_not(out_moves))(lambda: keep_out.start())

    gather_b.finish()
    pair_sq.wait_send()
    for step in range(1, LINE):
        line_sq(step, z).wait_send()
    for i in range(3):
        out_part(i).wait_send()
    for kind in kinds:
        for i in range(2):
            near_part(kind, i).wait_send()
            far_part(kind, i).wait_send()
    for wait in waits:
        wait()
    pl.when(down_moves)(lambda: fin_down.wait())
    pl.when(jnp.logical_not(down_moves))(lambda: keep_down.wait())
    pl.when(out_moves)(lambda: fin_out.wait())
    pl.when(jnp.logical_not(out_moves))(lambda: keep_out.wait())


def run_backward(gain_query, gain_key, gain_attn, d_mlp, cotangent, branch, scales, gm_part, kept):
    shape = jax.ShapeDtypeStruct
    dma = pltpu.SemaphoreType.DMA
    flat = [(2048, 768), (256, 2048), (2048, 1024), (2048, 1024), (1024, 2048), (1024, 2048), (1024, 2048),
            (1024, 1024), (1024, 1024), (1024, 1024), None, (3072, 256), (2048, 512), (1024, 256), None]
    kept = [a if s is None else a.reshape(s) for a, s in zip(kept, flat)]
    results = [
        shape((256, 2048), BF16),
        shape((64, 2048), BF16),
        shape((2, 4, 2, 64, 1024), BF16),
        shape((4, 2, 64, 896), BF16),
    ]
    transit = [
        shape((4, 512, 1024), BF16),
        shape((3, 512, 1024), BF16),
        shape((4, 512, 1024), BF16),
        shape((3, 512, 1024), BF16),
        shape((4, 256, 2048), BF16),
        shape((3, 256, 2048), BF16),
        shape((4, 512, 896), BF16),
        shape((3, 512, 896), BF16),
        shape((256, 2048), BF16),
        shape((3, 64, 2048), BF16),
    ]
    wide, square = pltpu.VMEM((1024, 2048), BF16), pltpu.VMEM((1024, 1024), BF16)
    tall = pltpu.VMEM((2048, 1024), BF16)
    rows = pltpu.VMEM((2, 4, 128, 1024), BF16)
    small = pltpu.VMEM((4, 8, 256), F32)
    return pl.pallas_call(
        backward_kernel,
        name="backward",
        out_shape=[shape((128, 2048), BF16)] + results + transit,
        in_specs=[vmem_spec()] * 4 + [any_spec()] * 2 + [vmem_spec()] * 2 + [any_spec()] * len(kept),
        out_specs=[vmem_spec()] + [any_spec()] * (len(results) + len(transit)),
        scratch_shapes=[
            wide, tall, tall, square, square, square, wide, square, square, wide, wide,
            pltpu.VMEM((2, 2, 512, 256), F32),
            pltpu.VMEM((2, 2, 512, 128), F32),
            pltpu.VMEM((2, 512, 256), BF16),
            pltpu.VMEM((2, 2, 512, 256), F32),
            pltpu.VMEM((2, 128, 1024), F32),
            rows,
            rows,
            pltpu.VMEM((2, 2, 128, 1024), F32),
            pltpu.VMEM((2, 128, 1024), F32),
            rows,
            rows,
            small,
            small,
            small,
            pltpu.VMEM((4, 4, 8, 256), F32),
            pltpu.VMEM((8, 2048), F32),
            pltpu.VMEM((128, 2048), F32),
            pltpu.VMEM((2, 512, 1024), BF16),
            pltpu.VMEM((256, 2048), BF16),
            pltpu.VMEM((256, 1024), BF16),
            pltpu.VMEM((2, 256), F32),
            pltpu.VMEM((128, 2048), BF16),
            pltpu.VMEM((128, 2048), F32),
            dma((18,)),
            dma(()),
            dma((2, 2, 4)), dma((2, 4)), dma((2, 4)), dma((2, 4)),
            dma((2, 4)), dma((2, 4)), dma((2, 4)), dma((2, 4)),
            dma((4,)), dma((5,)),
            dma((5, 4)), dma((5, 4)),
            dma((4,)), dma((20,)),
            dma((2,)), dma((2,)), dma((2,)),
            dma((3, 4, 2)), dma((3, 4, 2)), dma((3,)),
        ],
        compiler_params=pltpu.CompilerParams(
            collective_id=1, has_side_effects=True, vmem_limit_bytes=64 * 1024 * 1024
        ),
    )(gain_query, gain_key, gain_attn, d_mlp, cotangent, branch, scales, gm_part, *kept)[:5]


def arrange_kernel(
    gate_up, qkv, out_rows, down, result, d_tokens,
    o_result, o_tokens, o_q, o_k, o_v, o_out, o_gate, o_up, o_down, g_q, g_k, g_attn, g_mlp,
    v_gu, v_qkv, v_out, v_down, v_result, v_tokens, w_gu, w_qkv, w_out, w_down, in_sem, out_sem,
):
    reads = [
        pltpu.make_async_copy(src, dst, in_sem.at[i])
        for i, (src, dst) in enumerate([
            (gate_up, v_gu), (down, v_down), (qkv, v_qkv), (out_rows, v_out), (result, v_result),
            (d_tokens, v_tokens),
        ])
    ]
    for copy in reads:
        copy.start()
    writes = []

    def write(src, dst):
        copy = pltpu.make_async_copy(src, dst, out_sem.at[len(writes)])
        copy.start()
        writes.append(copy)

    reads[0].wait()
    for m, dst in enumerate((o_gate, o_up)):
        for z in range(LINE):
            for k in range(2):
                for q in range(PLANE):
                    at = 1024 * (2 * q + k) + 256 * z
                    w_gu[m, :, at : at + 256] = v_gu[m, z, k, :, 256 * q : 256 * q + 256].astype(F32)
        write(w_gu.at[m], dst)
    reads[1].wait()
    w_down[...] = v_down[...].astype(F32)
    write(w_down, o_down)
    reads[2].wait()
    total = jnp.zeros((64, 128), F32)
    for z in range(LINE):
        for k in range(2):
            at = 256 * (2 * z + k)
            for m in range(3):
                w_qkv[m, :, at : at + 256] = v_qkv[z, k, :, 256 * m : 256 * m + 256].astype(F32)
            total = total + v_qkv[z, k, :, 768:896].astype(F32)
    for m, dst in enumerate((o_q, o_k, o_v)):
        write(w_qkv.at[m], dst)
    lane = lax.broadcasted_iota(jnp.int32, (8, 128), 1)
    pick = (lax.broadcasted_iota(jnp.int32, (8, 128), 0) == lane).astype(F32)
    gains = exact(pick, total, ((1,), (1,)))
    for i, ref in enumerate((g_q, g_k, g_attn, g_mlp)):
        ref[...] = gains[i : i + 1]
    reads[3].wait()
    w_out[...] = v_out[...].astype(F32)
    write(w_out, o_out)
    reads[4].wait()
    write(v_result, o_result)
    reads[5].wait()
    write(v_tokens, o_tokens)
    for copy in writes:
        copy.wait()


def run_arrange(*arrays):
    shape = jax.ShapeDtypeStruct
    square = shape((64, 2048), F32)
    return pl.pallas_call(
        arrange_kernel,
        name="arrange",
        out_shape=[shape((128, 2048), BF16)] * 2 + [square] * 4 + [shape((64, 8192), F32)] * 2 + [shape((256, 2048), F32)]
        + [shape((1, 64), F32)] * 4,
        in_specs=[any_spec()] * 6,
        out_specs=[any_spec()] * 9 + [vmem_spec()] * 4,
        scratch_shapes=[pltpu.VMEM(a.shape, a.dtype) for a in arrays]
        + [
            pltpu.VMEM((2, 64, 8192), F32),
            pltpu.VMEM((3, 64, 2048), F32),
            pltpu.VMEM((64, 2048), F32),
            pltpu.VMEM((256, 2048), F32),
            pltpu.SemaphoreType.DMA((6,)),
            pltpu.SemaphoreType.DMA((9,)),
        ],
        compiler_params=pltpu.CompilerParams(vmem_limit_bytes=64 * 1024 * 1024),
    )(*arrays)


def shards_kernels(tokens, block_pairs, w_query, w_key, w_value, w_out, w_gate, w_up, w_down,
                   gain_query, gain_key, gain_attn, gain_mlp, cotangent):
    gains = [gain_query[None], gain_key[None], gain_attn[None]]
    out, d_mlp, gm_part, branch, scales, *kept = run_forward(
        block_pairs, *gains, gain_mlp[None], tokens[0], cotangent[0],
        (w_query, w_key, w_value, w_out, w_gate, w_up, w_down),
    )
    d_tokens, down, out_rows, gate_up, qkv = run_backward(
        *gains, d_mlp, cotangent[0], branch, scales, gm_part, kept
    )
    out, d_tokens, *grads = run_arrange(gate_up, qkv, out_rows, down, out, d_tokens)
    return (out[None], d_tokens[None], *grads[:7], *[g[0] for g in grads[7:]])


def shards(*arrays):
    tokens, w_query, w_down = arrays[0], arrays[2], arrays[8]
    here = (lax.axis_size("ctx"), lax.axis_size("fsdp"), tokens.shape, w_query.shape, w_down.shape)
    if here == (LINE, 2 * PLANE, (1, 128, 2048), (256, 2048), (1024, 2048)):
        return shards_kernels(*arrays)
    return shards_general(*arrays)


def solution(mesh):
    in_specs = (
        P("fsdp", "ctx", None),
        P("fsdp", None),
        P("fsdp", None),
        P("fsdp", None),
        P("fsdp", None),
        P("fsdp", None),
        P("fsdp", None),
        P("fsdp", None),
        P("fsdp", None),
        P(),
        P(),
        P(),
        P(),
        P("fsdp", "ctx", None),
    )
    out_specs = (
        P("fsdp", "ctx", None),
        P("fsdp", "ctx", None),
        P(("ctx", "fsdp"), None),
        P(("ctx", "fsdp"), None),
        P(("ctx", "fsdp"), None),
        P(("ctx", "fsdp"), None),
        P(("ctx", "fsdp"), None),
        P(("ctx", "fsdp"), None),
        P(("ctx", "fsdp"), None),
        P(("ctx", "fsdp")),
        P(("ctx", "fsdp")),
        P(("ctx", "fsdp")),
        P(("ctx", "fsdp")),
    )
    return jax.shard_map(shards, mesh=mesh, in_specs=in_specs, out_specs=out_specs, check_vma=False)
```

```python
import math

import jax
import jax.numpy as jnp
from jax import lax
from jax.experimental import pallas as pl
from jax.experimental.pallas import tpu as pltpu
from jax.sharding import PartitionSpec as P

HD = 128


EPSILON = 1e-06
ROPE_BASE = 500000.0
NEGATIVE = -1e30


def norm_scale(values, gain_vec):
    return (
        values * lax.rsqrt(jnp.mean(values * values, axis=-1, keepdims=True) + EPSILON) * gain_vec
    )


def turn_half(values, cosine, sine):
    half_size = values.shape[-1] // 2
    turned = jnp.concatenate([-values[..., half_size:], values[..., :half_size]], axis=-1)
    return values * cosine + turned * sine


def angle_tables(positions, head_size):
    half_size = head_size // 2
    frequency = jnp.power(ROPE_BASE, -(jnp.arange(half_size).astype(jnp.float32) * 2.0 / head_size))
    angles = positions.astype(jnp.float32)[:, None] * frequency[None, :]
    angles = jnp.concatenate([angles, angles], axis=-1)
    return (jnp.cos(angles)[:, None, :], jnp.sin(angles)[:, None, :])


def row_positions(row_ids, pair_row, block_rows, ctx_count):
    rank_of = row_ids // (2 * block_rows)
    second = row_ids // block_rows % 2
    offset = row_ids % block_rows
    rank_match = (rank_of[:, None] == jnp.arange(ctx_count, dtype=jnp.int32)[None, :]).astype(
        jnp.int32
    )
    chosen = jnp.sum(rank_match * pair_row[None, :], axis=1)
    block_index = jnp.where(second == 0, chosen, 2 * ctx_count - 1 - chosen)
    return block_index * block_rows + offset


def times_transpose(left, right):
    return lax.dot_general(
        left, right, (((1,), (1,)), ((), ())), preferred_element_type=jnp.float32
    )


def transpose_times(left, right):
    return lax.dot_general(
        left, right, (((0,), (0,)), ((), ())), preferred_element_type=jnp.float32
    )


def activate(gate_in, up_in):
    return jax.nn.silu(gate_in) * up_in


def spread_rows(values, outer, inner):
    rows, width = values.shape
    return (
        values.reshape(outer, inner, rows // (outer * inner), width)
        .transpose(1, 0, 2, 3)
        .reshape(rows, width)
    )


def shards_general(
    tokens,
    block_pairs,
    w_query,
    w_key,
    w_value,
    w_out,
    w_gate,
    w_up,
    w_down,
    gain_query,
    gain_key,
    gain_attn,
    gain_mlp,
    cotangent,
):
    bf16 = jnp.bfloat16
    f32 = jnp.float32
    local_rows = tokens.shape[1]
    block_rows = local_rows // 2
    width = w_query.shape[1]
    hidden_width = w_gate.shape[1]
    ctx_count = lax.axis_size("ctx")
    fsdp_count = lax.axis_size("fsdp")
    ctx_index = lax.axis_index("ctx")
    seq = local_rows * ctx_count
    cols = width // ctx_count
    heads = cols // HD
    strip = hidden_width // (ctx_count * fsdp_count)
    hid = strip * fsdp_count
    scale = HD ** (-0.5)

    def ctx_cols(w):
        return lax.dynamic_slice_in_dim(w, ctx_index * cols, cols, 1)

    def ctx_strips(w):
        parts = w.reshape(w.shape[0], fsdp_count, ctx_count, strip)
        return lax.dynamic_index_in_dim(parts, ctx_index, 2, keepdims=False).reshape(w.shape[0], hid)

    token_rows = tokens[0]
    x_all = lax.all_gather(token_rows, "ctx", axis=0, tiled=True)
    qkv_w = lax.all_gather(
        jnp.concatenate([ctx_cols(w_query), ctx_cols(w_key), ctx_cols(w_value)], axis=1),
        "fsdp", axis=0, tiled=True,
    )
    out_w = lax.dynamic_slice_in_dim(
        lax.all_gather(w_out, "fsdp", axis=0, tiled=True), ctx_index * cols, cols, 0
    )
    gate_w = lax.all_gather(ctx_strips(w_gate), "fsdp", axis=0, tiled=True)
    up_w = lax.all_gather(ctx_strips(w_up), "fsdp", axis=0, tiled=True)
    down_w = lax.all_gather(
        lax.dynamic_slice_in_dim(w_down, ctx_index * strip, strip, 0), "fsdp", axis=0, tiled=True
    )

    pos = row_positions(jnp.arange(seq, dtype=jnp.int32), block_pairs[0], block_rows, ctx_count)
    cosine, sine = angle_tables(pos, HD)
    mask = pos[None, :] <= pos[:, None]
    gain_q = lax.dynamic_slice_in_dim(gain_query, ctx_index * cols, cols)
    gain_k = lax.dynamic_slice_in_dim(gain_key, ctx_index * cols, cols)

    qkv = jnp.dot(x_all, qkv_w, preferred_element_type=f32)
    q_raw, k_raw, v_raw = qkv[:, :cols], qkv[:, cols : 2 * cols], qkv[:, 2 * cols :]
    squares = jnp.stack([jnp.sum(q_raw * q_raw, axis=1), jnp.sum(k_raw * k_raw, axis=1)])
    squares = lax.psum(squares, "ctx")
    scales = lax.rsqrt(squares / width + EPSILON)
    c_q, c_k = scales[0][:, None], scales[1][:, None]

    def rope(v):
        return turn_half(v.reshape(seq, heads, HD), cosine, sine)

    def rope_back(w):
        w = w.reshape(seq, heads, HD)
        u = w * sine
        half = HD // 2
        turned = jnp.concatenate([u[..., half:], -u[..., :half]], axis=-1)
        return (w * cosine + turned).reshape(seq, cols)

    queries = rope(q_raw * c_q * gain_q).astype(bf16)
    keys = rope(k_raw * c_k * gain_k).astype(bf16)
    values = v_raw.astype(bf16).reshape(seq, heads, HD)
    scores = jnp.einsum("qhd,khd->hqk", queries, keys, preferred_element_type=f32) * scale
    scores = jnp.where(mask[None], scores, NEGATIVE)
    exponent = jnp.exp(scores - jnp.max(scores, axis=-1, keepdims=True))
    probs = exponent / jnp.sum(exponent, axis=-1, keepdims=True)
    prob_low = probs.astype(bf16)
    attended = (
        jnp.einsum("hqk,khd->qhd", prob_low, values, preferred_element_type=f32)
        .reshape(seq, cols)
        .astype(bf16)
    )
    branch = lax.psum_scatter(
        jnp.dot(attended, out_w, preferred_element_type=f32).astype(bf16),
        "ctx", scatter_dimension=0, tiled=True,
    ).astype(f32)
    mid = token_rows.astype(f32) + norm_scale(branch, gain_attn)
    mid_all = lax.all_gather(mid.astype(bf16), "ctx", axis=0, tiled=True)
    gate_act = jnp.dot(mid_all, gate_w, preferred_element_type=f32)
    up_act = jnp.dot(mid_all, up_w, preferred_element_type=f32)
    hidden = activate(gate_act, up_act).astype(bf16)
    mlp_out = lax.psum_scatter(
        jnp.dot(hidden, down_w, preferred_element_type=f32).astype(bf16),
        "ctx", scatter_dimension=0, tiled=True,
    ).astype(f32)
    output = (mid + norm_scale(mlp_out, gain_mlp)).astype(bf16)

    d_output = cotangent[0].astype(f32)
    unused_mlp, pull_mlp = jax.vjp(norm_scale, mlp_out, gain_mlp)
    d_mlp, grad_gm = pull_mlp(d_output)
    d_mlp_all = lax.all_gather(d_mlp.astype(bf16), "ctx", axis=0, tiled=True)
    d_hidden = times_transpose(d_mlp_all, down_w)
    unused_act, pull_act = jax.vjp(activate, gate_act, up_act)
    d_gate, d_up = pull_act(d_hidden)
    d_gate = d_gate.astype(bf16)
    d_up = d_up.astype(bf16)
    d_mid_part = times_transpose(d_gate, gate_w) + times_transpose(d_up, up_w)
    d_mid = d_output + lax.psum_scatter(
        d_mid_part.astype(bf16), "ctx", scatter_dimension=0, tiled=True
    ).astype(f32)

    down_sum = lax.psum_scatter(
        transpose_times(hidden, d_mlp_all).astype(bf16), "fsdp", scatter_dimension=0, tiled=True
    )
    moves = [
        (z * fsdp_count + f, f * ctx_count + z)
        for z in range(ctx_count)
        for f in range(fsdp_count)
    ]
    grad_down = lax.ppermute(down_sum, ("ctx", "fsdp"), moves).astype(f32)

    def column_grad(left, right):
        part = transpose_times(left, right).astype(bf16)
        mine = lax.psum_scatter(
            spread_rows(part, ctx_count, fsdp_count), "fsdp", scatter_dimension=0, tiled=True
        )
        mine = mine.reshape(ctx_count, mine.shape[0] // ctx_count, mine.shape[1])
        return lax.all_to_all(mine, "ctx", 0, 0, tiled=True)

    gate_up = column_grad(mid_all, jnp.concatenate([d_gate, d_up], axis=1))
    rows = gate_up.shape[1]

    def from_strips(part):
        return (
            part.reshape(ctx_count, rows, fsdp_count, strip)
            .transpose(1, 2, 0, 3)
            .reshape(rows, hidden_width)
            .astype(f32)
        )

    unused_branch, pull_branch = jax.vjp(norm_scale, branch, gain_attn)
    d_branch, grad_ga = pull_branch(d_mid)
    d_branch_all = lax.all_gather(d_branch.astype(bf16), "ctx", axis=0, tiled=True)
    d_attended = times_transpose(d_branch_all, out_w).astype(bf16).reshape(seq, heads, HD)
    grad_out = lax.psum_scatter(
        transpose_times(attended, d_branch_all).astype(bf16),
        "fsdp", scatter_dimension=0, tiled=True,
    ).astype(f32)

    d_values = jnp.einsum("hqk,qhd->khd", prob_low, d_attended, preferred_element_type=f32)
    d_values = d_values.astype(bf16).reshape(seq, cols)
    d_probs = jnp.einsum("qhd,khd->hqk", d_attended, values, preferred_element_type=f32)
    delta = jnp.sum(probs * d_probs, axis=-1, keepdims=True)
    d_scores = (probs * (d_probs - delta)).astype(bf16)
    d_queries = jnp.einsum("hqk,khd->qhd", d_scores, keys, preferred_element_type=f32) * scale
    d_keys = jnp.einsum("hqk,qhd->khd", d_scores, queries, preferred_element_type=f32) * scale
    dy_q = rope_back(d_queries)
    dy_k = rope_back(d_keys)
    dots = jnp.stack([
        jnp.sum(q_raw * gain_q * dy_q, axis=1), jnp.sum(k_raw * gain_k * dy_k, axis=1)
    ])
    dots = lax.psum(dots, "ctx") / width
    d_q = c_q * gain_q * dy_q - q_raw * (c_q * c_q * c_q * dots[0][:, None])
    d_k = c_k * gain_k * dy_k - k_raw * (c_k * c_k * c_k * dots[1][:, None])
    d_qkv = jnp.concatenate([d_q.astype(bf16), d_k.astype(bf16), d_values], axis=1)
    d_tokens = d_mid + lax.psum_scatter(
        times_transpose(d_qkv, qkv_w).astype(bf16), "ctx", scatter_dimension=0, tiled=True
    ).astype(f32)
    qkv_grad = column_grad(x_all, d_qkv).transpose(1, 0, 2)
    sum_gqk = lax.psum_scatter(
        jnp.stack([jnp.sum(dy_q * q_raw * c_q, axis=0), jnp.sum(dy_k * k_raw * c_k, axis=0)]),
        "fsdp", scatter_dimension=1, tiled=True,
    )
    sum_gam = lax.psum_scatter(
        jnp.stack([grad_ga, grad_gm]), ("ctx", "fsdp"), scatter_dimension=1, tiled=True
    )

    def whole(part):
        return part.reshape(part.shape[0], width).astype(f32)

    return (
        output[None],
        d_tokens.astype(bf16)[None],
        whole(qkv_grad[:, :, :cols]),
        whole(qkv_grad[:, :, cols : 2 * cols]),
        whole(qkv_grad[:, :, 2 * cols :]),
        grad_out,
        from_strips(gate_up[:, :, :hid]),
        from_strips(gate_up[:, :, hid:]),
        grad_down,
        sum_gqk[0],
        sum_gqk[1],
        sum_gam[0],
        sum_gam[1],
    )


MESH = pl.DeviceIdType.MESH
BF16 = jnp.bfloat16
F32 = jnp.float32
LINE = 4
PLANE = 4


def dot(left, right):
    return lax.dot_general(left, right, (((1,), (0,)), ((), ())), preferred_element_type=F32)


def dot_rt(left, right):
    return lax.dot_general(left, right, (((1,), (1,)), ((), ())), preferred_element_type=F32)


def dot_lt(left, right):
    return lax.dot_general(left, right, (((0,), (0,)), ((), ())), preferred_element_type=F32)


def exact(left, right, dims):
    return lax.dot_general(
        left, right, (dims, ((), ())), precision=lax.Precision.HIGHEST, preferred_element_type=F32
    )


def remote(src, dst, send, recv, device):
    return pltpu.make_async_remote_copy(
        src_ref=src, dst_ref=dst, send_sem=send, recv_sem=recv, device_id=device, device_id_type=MESH
    )


def at128(i, step=128):
    return pl.ds(i if isinstance(i, int) else pl.multiple_of(i, step), step)


class Place:
    def __init__(self):
        z = lax.axis_index("ctx")
        f = lax.axis_index("fsdp")
        self.z, self.f = z, f
        self.p, self.k = f // 2, f % 2
        self.p_x = self.p + 1 - 2 * (self.p % 2)
        self.p_y = (self.p + 2) % PLANE
        self.p_d = PLANE - 1 - self.p
        self.partner = (z, 2 * self.p + 1 - self.k)
        self.x = (z, 2 * self.p_x + self.k)
        self.y = (z, 2 * self.p_y + self.k)
        self.d = (z, 2 * self.p_d + self.k)
        self.ends = z // 3 + (3 - z) // 3

    def line(self, c):
        return (c, self.f)

    def order(self, s):
        z, e, t = self.z, self.ends, s // 3
        end = z + s * (1 - 2 * (z // 3))
        mid = (1 - t) * (z + (3 * s * s - 5 * s) // 2) + t * 3 * (2 - z)
        return e * end + (1 - e) * mid

    def cross(self, c):
        return (c, 2 * self.p + 1 - self.k)

    def barrier(self, more=(), senders=()):
        sem = pltpu.get_barrier_semaphore()

        def greet(peer):
            pl.semaphore_signal(sem, inc=1, device_id=peer, device_id_type=MESH)

        peers = [self.partner, self.x, self.y] + list(more)
        peers += [self.line((self.z + step) % LINE) for step in range(1, LINE)]
        for peer in peers:
            greet(peer)
        count = len(peers)
        for here, peer in senders:
            pl.when(here)(lambda peer=peer: greet(peer))
            count = count + here.astype(jnp.int32)
        pl.semaphore_wait(sem, count)


class Gather:
    def __init__(self, place, buf, z_send, z_recv, c_send, c_recv):
        self.pl, self.buf = place, buf
        self.sems = z_send, z_recv, c_send, c_recv

    def to_line(self, c, target, way):
        z_send, z_recv, _, _ = self.sems
        part = self.buf.at[c, self.pl.k]
        return remote(part, part, z_send.at[way, c], z_recv.at[c], self.pl.line(target))

    def to_core(self, c):
        _, _, c_send, c_recv = self.sems
        part = self.buf.at[c, self.pl.k]
        return remote(part, part, c_send.at[c], c_recv.at[c], self.pl.partner)

    def from_core(self, c):
        _, _, c_send, c_recv = self.sems
        part = self.buf.at[c, 1 - self.pl.k]
        return remote(part, part, c_send.at[c], c_recv.at[c], self.pl.partner)

    def start(self):
        z = self.pl.z
        pl.when(z < LINE - 1)(lambda: self.to_line(z, z + 1, 0).start())
        pl.when(z > 0)(lambda: self.to_line(z, z - 1, 1).start())
        self.to_core(z).start()

    def arrive(self, c):
        z = self.pl.z
        self.to_line(c, z, 0).wait_recv()
        pl.when(jnp.logical_and(c < z, z < LINE - 1))(lambda: self.to_line(c, z + 1, 0).start())
        pl.when(jnp.logical_and(c > z, z > 0))(lambda: self.to_line(c, z - 1, 1).start())
        self.to_core(c).start()

    def arrive_first(self):
        self.arrive(self.pl.order(1))
        pl.when(self.pl.ends == 0)(lambda: self.arrive(self.pl.order(2)))

    def arrive_second(self):
        self.arrive(self.pl.order(3 - self.pl.ends))

    def arrive_third(self):
        pl.when(self.pl.ends == 1)(lambda: self.arrive(self.pl.order(3)))

    def ready(self, c):
        self.from_core(c).wait_recv()

    def finish(self):
        z = self.pl.z

        def body(c, carry):
            pl.when(jnp.logical_and(c <= z, z < LINE - 1))(
                lambda: self.to_line(c, z, 0).wait_send()
            )
            pl.when(jnp.logical_and(c >= z, z > 0))(lambda: self.to_line(c, z, 1).wait_send())
            self.to_core(c).wait_send()
            return carry

        lax.fori_loop(0, LINE, body, 0)


class RowSum:
    def __init__(self, place, h, buffers, sems):
        self.pl, self.h = place, h
        self.term, self.pair_out, self.pair_in, self.keep, self.mine, self.line_out, self.line_in = buffers
        self.p_send, self.p_recv, self.l_send, self.l_recv = sems

    def pair(self, c):
        h = self.h
        return remote(
            self.pair_out.at[h, c], self.pair_in.at[h, c], self.p_send.at[h, c], self.p_recv.at[h, c],
            self.pl.partner,
        )

    def line(self, c, slot, target):
        h = self.h
        return remote(
            self.line_out.at[h, c], self.line_in.at[h, slot], self.l_send.at[h, c],
            self.l_recv.at[h, slot], self.pl.line(target),
        )

    def mate(self):
        return self.pl.z + 1 - 2 * (self.pl.z % 2)

    def give(self, c, s):
        h, k = self.h, self.pl.k
        self.pair_out[h, c] = self.term[1 - k].astype(BF16)
        self.pair(c).start()
        self.keep[h, s % 2] = self.term[k]

    def pass_on(self, c, s):
        h, z = self.h, self.pl.z
        near = c // 2 == z // 2
        end = self.pl.ends == 1
        self.pair(c).wait_recv()

        @pl.when(c == z)
        def _():
            self.mine[h] = self.keep[h, s % 2] + self.pair_in[h, c].astype(F32)

        @pl.when(c != z)
        def _():
            self.line_out[h, c] = (self.keep[h, s % 2] + self.pair_in[h, c].astype(F32)).astype(BF16)

        pl.when(jnp.logical_and(c != z, near))(lambda: self.line(c, z, c).start())
        pl.when(jnp.logical_and(jnp.logical_not(near), end))(
            lambda: self.line(c, 2 * c - 3 * (1 - z // 2), self.mate()).start()
        )

    def relay(self, far):
        h, z = self.h, self.pl.z

        @pl.when(self.pl.ends == 0)
        def _():
            c = 3 * (2 - z) if far else 3 - z
            slot = 2 * c - 3 * (2 - z)
            self.line(c, slot, z).wait_recv()
            self.line_out[h, c] = (
                self.line_out[h, c].astype(F32) + self.line_in[h, slot].astype(F32)
            ).astype(BF16)
            self.line(c, z, c).start()

    def total(self):
        h, z = self.h, self.pl.z
        result = self.mine[h]
        for source in (self.mate(), 2 - z // 2):
            self.line(source, source, source).wait_recv()
            result = result + self.line_in[h, source].astype(F32)
        return result

    def finish(self):
        z = self.pl.z

        def body(c, carry):
            self.pair(c).wait_send()
            pl.when(c != z)(lambda: self.line(c, z, c).wait_send())
            return carry

        lax.fori_loop(0, LINE, body, 0)


class Ring:
    def __init__(self, place, buf, rows, send, recv):
        self.pl, self.buf, self.rows = place, buf, rows
        self.send, self.recv = send, recv

    def block(self, p):
        return self.buf.at[at128(p * self.rows, self.rows)]

    def half(self, p, i):
        size = self.rows // 2
        return self.buf.at[at128(p * self.rows + i * size, size)]

    def own(self, way):
        part = self.block(self.pl.p)
        return remote(part, part, self.send.at[way], self.recv.at[way], (self.pl.x, self.pl.y)[way])

    def far(self, i):
        part = self.half((self.pl.p_x, self.pl.p_y)[i], i)
        return remote(part, part, self.send.at[2 + i], self.recv.at[2 + i], (self.pl.y, self.pl.x)[i])

    def start(self):
        self.own(0).start()
        self.own(1).start()

    def forward(self):
        for i in range(2):
            part = self.block((self.pl.p_x, self.pl.p_y)[i])
            remote(part, part, self.send.at[i], self.recv.at[i], (self.pl.x, self.pl.y)[i]).wait_recv()
            self.far(i).start()

    def ready(self):
        for i in range(2):
            part = self.half(self.pl.p_d, i)
            remote(part, part, self.send.at[2 + i], self.recv.at[2 + i], self.pl.x).wait_recv()

    def finish(self):
        for i in range(2):
            self.own(i).wait_send()
            self.far(i).wait_send()


def scale_columns(totals, rows, which):
    pick = (lax.broadcasted_iota(jnp.int32, (8, 128), 0) == which).astype(F32)
    return exact(totals[:, rows], pick, ((0,), (0,)))


def forward_kernel(
    pairs, gain_query, gain_key, gain_attn, gain_mlp, tokens, cotangent,
    w_query, w_key, w_value, w_out, w_gate, w_up, w_down,
    o_out, o_dmlp, o_gm, o_branch, o_tot,
    o_qkv, o_wo, o_g, o_u, o_dn, o_x, o_m, o_ga, o_ua, o_hid, o_raw, o_heads, o_probs, o_att, o_tab,
    qkv, wo, wg, wu, wd, xs, ms, ga, ua, hid, raw, heads, probs, att, tab, posr, posc,
    term, pair_out, pair_in, keep, mine, line_out, line_in,
    sq_own, sq_pair, sq_both, sq_line, mid, gains_qk, branch_kept,
    loc_sem, swap_send, swap_recv, ring_send, ring_recv, wo_send, wo_recv,
    zs, zr, cs, cr, ps, pr, ls, lr, ts, tr, as_, ar, out_sem,
):
    place = Place()
    z, f, p, k = place.z, place.f, place.p, place.k
    rows = 128
    width = 2048
    cols = 256
    seq = 512
    place.barrier()

    for i, ref in enumerate((gain_query, gain_key)):
        gains_qk[i : i + 1, :] = ref[:, at128(256 * (2 * z + k), 256)]

    def own_rows(n):
        return at128(n * (2 * p + k), n)

    def strips(core):
        return [1024 * (2 * q + core) + 256 * z for q in range(PLANE)]

    local, swap = {}, {}

    def split(name, w, buf, sources, first):
        local[name], swap[name] = [], []
        for i, (mine, theirs) in enumerate(sources):
            dst = buf.at[own_rows(256), pl.ds(256 * i + first[1], 256)]
            local[name].append(
                pltpu.make_async_copy(w.at[:, at128(mine, 256)], dst, loc_sem.at[first[0] + i])
            )
            swap[name].append(
                remote(
                    w.at[:, at128(theirs, 256)], dst, swap_send.at[first[0] + i],
                    swap_recv.at[first[0] + i], place.partner,
                )
            )

    head_cols = [(256 * (2 * z + k), 256 * (2 * z + 1 - k))]
    hid_cols = list(zip(strips(k), strips(1 - k)))
    split("q", w_query, qkv, head_cols, (0, 0))
    split("k", w_key, qkv, head_cols, (1, 256))
    split("v", w_value, qkv, head_cols, (2, 512))
    split("g", w_gate, wg, hid_cols, (3, 0))
    split("u", w_up, wu, hid_cols, (7, 0))

    def begin(*names):
        for name in names:
            for a, b in zip(local[name], swap[name]):
                b.start()
                a.start()

    def settle(*names):
        for name in names:
            for a, b in zip(local[name], swap[name]):
                a.wait()
                b.wait_recv()

    dx, dy = (p % 2 + z % 2) % 2, (p // 2 + z // 2) % 2
    top, low = wo.at[pl.ds(0, 128)], wo.at[pl.ds(128, 128)]
    wo_copy = pltpu.make_async_copy(w_out, wo, loc_sem.at[12])

    def wo_first(i, device):
        rows_i = pl.ds(128 * i, 128)
        return remote(w_out.at[rows_i], wo.at[rows_i], wo_send.at[i], wo_recv.at[i], device)

    def wo_send_to(i, part, device):
        return remote(part, part, wo_send.at[i], wo_recv.at[i], device)

    is_source = jnp.logical_and(dx == 0, dy == 0)
    is_x = jnp.logical_and(dx == 1, dy == 0)
    is_y = jnp.logical_and(dx == 0, dy == 1)
    is_d = jnp.logical_and(dx == 1, dy == 1)

    @pl.when(is_source)
    def _():
        wo_copy.start()
        wo_first(0, place.x).start()
        wo_first(1, place.y).start()

    begin("q", "k", "v")
    xs[z, k] = tokens[...]
    gather_x = Gather(place, xs, zs.at[0], zr.at[0], cs.at[0], cr.at[0])
    gather_x.start()
    down_copies = [
        pltpu.make_async_copy(
            w_down.at[at128(256 * z, 256), pl.ds(1024 * h, 1024)], wd.at[h, at128(256 * p, 256)],
            loc_sem.at[(11, 13)[h]],
        )
        for h in range(2)
    ]
    for copy in down_copies:
        copy.start()
    begin("g", "u")
    ring_qkv = Ring(place, qkv, 512, ring_send.at[0], ring_recv.at[0])
    ring_g = Ring(place, wg, 512, ring_send.at[1], ring_recv.at[1])
    ring_u = Ring(place, wu, 512, ring_send.at[2], ring_recv.at[2])
    ring_d = [Ring(place, wd.at[h], 256, ring_send.at[3 + h], ring_recv.at[3 + h]) for h in range(2)]
    settle("q", "k", "v")
    ring_qkv.start()

    def positions(shape, axis):
        i = lax.broadcasted_iota(jnp.int32, shape, axis)
        block = i // 64
        pos = jnp.zeros(shape, jnp.int32)
        for r in range(LINE):
            b = pairs[0, r]
            pos = pos + jnp.where(block == 2 * r, b * 64, 0)
            pos = pos + jnp.where(block == 2 * r + 1, (2 * LINE - 1 - b) * 64, 0)
        return (pos + i % 64).astype(F32)

    posr[k] = positions((8, seq), 1)
    col = positions((seq, 128), 0)
    posc[k] = col
    lane = lax.broadcasted_iota(jnp.int32, (seq, 128), 1)
    freq = jnp.exp((lane % 64).astype(F32) * (-2.0 / HD * math.log(ROPE_BASE)))
    angle = col * freq
    tab[0, k] = jnp.cos(angle)
    sine = jnp.sin(angle)
    tab[1, k] = jnp.where(lane < 64, -sine, sine)
    tables = [
        remote(r, r, ts.at[i], tr.at[i], place.partner)
        for i, r in enumerate([posr.at[k], posc.at[k], tab.at[0, k], tab.at[1, k]])
    ]
    for t in tables:
        t.start()

    gather_x.arrive_first()
    pl.when(is_x)(lambda: wo_send_to(0, top, place.x).wait_recv())
    pl.when(is_x)(lambda: wo_send_to(0, top, place.y).start())
    pl.when(is_y)(lambda: wo_send_to(1, low, place.x).wait_recv())
    pl.when(is_y)(lambda: wo_send_to(1, low, place.x).start())
    ring_qkv.forward()
    settle("g", "u")
    gather_x.arrive_second()

    @pl.when(is_d)
    def _():
        wo_send_to(0, top, place.x).wait_recv()
        wo_send_to(0, top, place.x).start()
        wo_send_to(1, low, place.x).wait_recv()
        wo_send_to(1, low, place.y).start()

    ring_g.start()
    ring_qkv.ready()

    def project(c):
        gather_x.ready(c)
        chunk = xs[c].reshape(2 * rows, width)
        there = at128(c * rows)
        sums = jnp.zeros((8, 2 * rows), F32)
        pick = lax.broadcasted_iota(jnp.int32, (8, cols), 0)
        for i in range(2):
            part = dot(chunk, qkv[:, i * cols : (i + 1) * cols])
            raw[i, :, there] = part.reshape(2, rows, cols)
            sums = sums + exact((pick == i).astype(F32), part * part, ((1,), (1,)))
        part = dot(chunk, qkv[:, 2 * cols :])
        heads[2, :, there] = part.astype(BF16).reshape(2, rows, cols)
        sq_own[c] = sums

    def project_step(s, carry):
        project(place.order(s))
        return carry

    lax.fori_loop(0, 3, project_step, 0)
    gather_x.arrive_third()
    lax.fori_loop(3, 4, project_step, 0)

    pair_sq = remote(sq_own, sq_pair, as_.at[0], ar.at[0], place.partner)
    pair_sq.start()
    ring_u.start()
    pair_sq.wait_recv()
    sq_both[...] = sq_own[...] + sq_pair[...]

    def line_sq(step, source):
        return remote(
            sq_both, sq_line.at[source], as_.at[step], ar.at[1 + source],
            place.line((z + step) % LINE),
        )

    for step in range(1, LINE):
        line_sq(step, z).start()
    for t in tables:
        t.wait_recv()
    for step in range(1, LINE):
        line_sq(step, (z + step) % LINE).wait_recv()
    sq_line[z] = sq_both[...]
    total = (sq_line[0] + sq_line[1]) + (sq_line[2] + sq_line[3])
    scales = lax.rsqrt(total / width + EPSILON)
    o_tot[...] = scales

    def rotate(c, carry):
        there = at128(c * rows)
        now = o_tot[c]
        for i in range(2):
            pick = (lax.broadcasted_iota(jnp.int32, (8, 128), 0) == i).astype(F32)
            column = exact(now, pick, ((0,), (0,)))
            for s in range(2):
                for h in range(2):
                    lanes = slice(128 * h, 128 * h + 128)
                    v = raw[i, s, there, lanes] * column[128 * s : 128 * s + 128]
                    v = v * gains_qk[i : i + 1, lanes]
                    v = v * tab[0, s, there] + pltpu.roll(v, 64, 1) * tab[1, s, there]
                    heads[i, s, there, lanes] = v.astype(BF16)
        return carry

    lax.fori_loop(0, LINE, rotate, 0)

    def attend(s, carry):
        mask = posr[s, 0:1, :] <= posc[s][:, 0:1]
        for h in range(2):
            lanes = slice(128 * h, 128 * h + 128)
            scores = dot_rt(heads[0, s, :, lanes], heads[1, s, :, lanes]) * (HD ** -0.5)
            scores = jnp.where(mask, scores, NEGATIVE)
            e = jnp.exp(scores - jnp.max(scores, axis=1, keepdims=True))
            low_p = (e / jnp.sum(e, axis=1, keepdims=True)).astype(BF16)
            probs[s, h] = low_p
            att[s, :, lanes] = dot(low_p, heads[2, s, :, lanes]).astype(BF16)
        return carry

    lax.fori_loop(0, 2, attend, 0)

    pl.when(is_source)(lambda: wo_copy.wait())
    pl.when(is_x)(lambda: wo_send_to(1, low, place.x).wait_recv())
    pl.when(is_y)(lambda: wo_send_to(0, top, place.x).wait_recv())

    ring_g.forward()
    buffers = (term, pair_out, pair_in, keep, mine, line_out, line_in)
    sums = [RowSum(place, h, buffers, (ps, pr, ls, lr)) for h in range(2)]

    def branch_step(s, carry):
        c = place.order(3 - s)
        left = att[:, at128(c * rows)].reshape(2 * rows, cols)
        for h in range(2):
            term[...] = dot(left, wo[:, 1024 * h : 1024 * h + 1024]).reshape(2, rows, 1024)
            sums[h].give(c, s)
        for h in range(2):
            pl.when(s > 0)(lambda h=h: sums[h].pass_on(place.order(4 - s), s + 1))
        return carry

    lax.fori_loop(0, 4, branch_step, 0)
    for h in range(2):
        sums[h].pass_on(z, 3)
    copies = []

    def save(*pairs):
        for a, b in pairs:
            copies.append(pltpu.make_async_copy(a, b, out_sem.at[len(copies)]))
            copies[-1].start()

    save((qkv, o_qkv), (wo, o_wo), (xs, o_x), (raw, o_raw), (heads, o_heads), (probs, o_probs), (att, o_att))
    save((tab, o_tab))
    for h in range(2):
        sums[h].relay(True)
    ring_u.forward()
    for h in range(2):
        sums[h].relay(False)
    for copy in down_copies:
        copy.wait()
    ring_d[0].start()
    branch = jnp.concatenate([sums[h].total() for h in range(2)], axis=1)
    for h in range(2):
        sums[h].finish()
    branch_kept[...] = branch

    def mean_sq(v):
        return jnp.sum(v * v, axis=1, keepdims=True) / width

    mid[...] = tokens[...].astype(F32) + branch * lax.rsqrt(mean_sq(branch) + EPSILON) * gain_attn[...]
    ms[z, k] = mid[...].astype(BF16)
    gather_m = Gather(place, ms, zs.at[1], zr.at[1], cs.at[1], cr.at[1])
    gather_m.start()

    ring_d[0].forward()
    ring_d[1].start()
    ring_g.ready()
    ring_u.ready()

    def expand(s, carry):
        c = place.order(s)
        gather_m.ready(c)
        chunk = ms[c].reshape(2 * rows, width)

        def body(t, inner):
            lanes = at128(t * 256, 256)
            g = dot(chunk, wg[:, lanes])
            u = dot(chunk, wu[:, lanes])
            ga[c, :, lanes] = g.astype(BF16)
            ua[c, :, lanes] = u.astype(BF16)
            hid[c, :, lanes] = (g / (1.0 + jnp.exp(-g)) * u).astype(BF16)
            return inner

        lax.fori_loop(0, 4, body, 0)
        return carry

    def contract(h, first, last):
        def step(s, carry):
            c = place.order(s)
            term[...] = dot(hid[c], wd[h]).reshape(2, rows, 1024)
            sums[h].give(c, s)
            pl.when(s > first)(lambda: sums[h].pass_on(place.order(s - 1), s + 1))
            return carry

        lax.fori_loop(first, last, step, 0)

    def flush(h, last):
        sums[h].pass_on(place.order(last - 1), last - 1)

    save((branch_kept, o_branch), (wg, o_g), (wu, o_u))
    lax.fori_loop(0, 1, expand, 0)
    gather_m.arrive_first()
    lax.fori_loop(1, 2, expand, 0)
    ring_d[0].ready()
    contract(0, 0, 2)
    gather_m.arrive_second()
    flush(0, 2)
    ring_d[1].forward()
    lax.fori_loop(2, 3, expand, 0)
    contract(0, 2, 3)
    ring_d[1].ready()
    flush(0, 3)
    contract(1, 0, 3)
    gather_m.arrive_third()
    flush(1, 3)
    lax.fori_loop(3, 4, expand, 0)
    contract(0, 3, 4)
    contract(1, 3, 4)
    for h in range(2):
        flush(h, 4)
    for h in range(2):
        sums[h].relay(False)
    for h in range(2):
        sums[h].relay(True)

    save((wd.at[0], o_dn.at[:, pl.ds(0, 1024)]), (wd.at[1], o_dn.at[:, pl.ds(1024, 1024)]), (ms, o_m), (ga, o_ga))
    save((ua, o_ua), (hid, o_hid))

    mlp = jnp.concatenate([sums[h].total() for h in range(2)], axis=1)
    for h in range(2):
        sums[h].finish()
    c_m = lax.rsqrt(mean_sq(mlp) + EPSILON)
    gain = gain_mlp[...]
    o_out[...] = (mid[...] + mlp * c_m * gain).astype(BF16)
    dy = cotangent[...].astype(F32)
    gdy = gain * dy
    inner = jnp.sum(mlp * gdy, axis=1, keepdims=True) / width
    o_dmlp[...] = (c_m * gdy - mlp * (c_m * c_m * c_m * inner)).astype(BF16)
    o_gm[...] = jnp.sum(dy * mlp * c_m, axis=0, keepdims=True)

    gather_x.finish()
    gather_m.finish()
    for ring in (ring_qkv, ring_g, ring_u, *ring_d):
        ring.finish()
    for group in swap.values():
        for copy in group:
            copy.wait_send()
    for t in tables:
        t.wait_send()
    pair_sq.wait_send()
    for step in range(1, LINE):
        line_sq(step, z).wait_send()

    @pl.when(is_source)
    def _():
        wo_first(0, place.x).wait_send()
        wo_first(1, place.y).wait_send()

    pl.when(is_x)(lambda: wo_send_to(0, top, place.y).wait_send())
    pl.when(is_y)(lambda: wo_send_to(1, low, place.x).wait_send())

    @pl.when(is_d)
    def _():
        wo_send_to(0, top, place.x).wait_send()
        wo_send_to(1, low, place.y).wait_send()

    for copy in copies:
        copy.wait()


def any_spec():
    return pl.BlockSpec(memory_space=pl.ANY)


def vmem_spec():
    return pl.BlockSpec(memory_space=pltpu.VMEM)


def run_forward(pairs, gain_query, gain_key, gain_attn, gain_mlp, tokens, cotangent, weights):
    shape = jax.ShapeDtypeStruct
    dma = pltpu.SemaphoreType.DMA
    kept = [
        shape((2048, 768), BF16),
        shape((256, 2048), BF16),
        shape((2048, 1024), BF16),
        shape((2048, 1024), BF16),
        shape((1024, 2048), BF16),
        shape((4, 2, 128, 2048), BF16),
        shape((4, 2, 128, 2048), BF16),
        shape((4, 256, 1024), BF16),
        shape((4, 256, 1024), BF16),
        shape((4, 256, 1024), BF16),
        shape((2, 2, 512, 256), F32),
        shape((3, 2, 512, 256), BF16),
        shape((2, 2, 512, 512), BF16),
        shape((2, 512, 256), BF16),
        shape((2, 2, 512, 128), F32),
    ]
    return pl.pallas_call(
        forward_kernel,
        name="forward",
        out_shape=[
            shape((128, 2048), BF16),
            shape((128, 2048), BF16),
            shape((1, 2048), F32),
            shape((128, 2048), F32),
            shape((4, 8, 256), F32),
        ]
        + kept,
        in_specs=[pl.BlockSpec(memory_space=pltpu.SMEM)] + [vmem_spec()] * 6 + [any_spec()] * 7,
        out_specs=[vmem_spec()] * 3 + [any_spec(), vmem_spec()] + [any_spec()] * len(kept),
        scratch_shapes=[pltpu.VMEM((2, 1024, 1024) if i == 4 else k.shape, k.dtype) for i, k in enumerate(kept)]
        + [
            pltpu.VMEM((2, 8, 512), F32),
            pltpu.VMEM((2, 512, 128), F32),
            pltpu.VMEM((2, 128, 1024), F32),
            pltpu.VMEM((2, 4, 128, 1024), BF16),
            pltpu.VMEM((2, 4, 128, 1024), BF16),
            pltpu.VMEM((2, 2, 128, 1024), F32),
            pltpu.VMEM((2, 128, 1024), F32),
            pltpu.VMEM((2, 4, 128, 1024), BF16),
            pltpu.VMEM((2, 4, 128, 1024), BF16),
            pltpu.VMEM((4, 8, 256), F32),
            pltpu.VMEM((4, 8, 256), F32),
            pltpu.VMEM((4, 8, 256), F32),
            pltpu.VMEM((4, 4, 8, 256), F32),
            pltpu.VMEM((128, 2048), F32),
            pltpu.VMEM((2, 256), F32),
            pltpu.VMEM((128, 2048), F32),
            dma((14,)),
            dma((11,)),
            dma((11,)),
            dma((5, 4)),
            dma((5, 4)),
            dma((2,)),
            dma((2,)),
            dma((2, 2, 4)),
            dma((2, 4)),
            dma((2, 4)),
            dma((2, 4)),
            dma((2, 4)),
            dma((2, 4)),
            dma((2, 4)),
            dma((2, 4)),
            dma((4,)),
            dma((4,)),
            dma((4,)),
            dma((5,)),
            dma((len(kept) + 2,)),
        ],
        compiler_params=pltpu.CompilerParams(
            collective_id=0, has_side_effects=True, vmem_limit_bytes=64 * 1024 * 1024
        ),
    )(pairs, gain_query, gain_key, gain_attn, gain_mlp, tokens, cotangent, *weights)


def backward_kernel(
    gain_query, gain_key, gain_attn, d_mlp, h_cot, h_branch, scales, gm_part,
    h_qkv, h_wo, h_g, h_u, h_dn, h_x, h_m, h_ga, h_ua, h_hid, h_raw, h_heads, h_probs, h_att, h_tab,
    o_tok, o_down, o_out, o_gu, o_qkv,
    st_g, rc_g, st_u, rc_u, st_dn, rc_dn, st_qkv, rc_qkv, st_out, rc_out,
    wd, wg, wu, ga, ua, hid, dm, dg, du, ms, db, raw, tab, datt, dy,
    term, pair_out, pair_in, keep, mine, line_out, line_in,
    sq_own, sq_pair, sq_both, sq_line, gn_own, d_mid, stage, stage_d, far_in, gains_qk, cotangent, branch,
    ld, far_sem, zs, zr, cs, cr, ps, pr, ls, lr, as_, ar, in_send, in_recv, st_sem, sum_sem,
    fin_send, fin_recv, fin_loc, al_send, al_recv, al_loc,
):
    place = Place()
    z, f, p, k = place.z, place.f, place.p, place.k
    rows, width, cols = 128, 2048, 256

    def strip_of(chip, plane):
        return (chip % 2 + plane // 2) % 2 + 2 * ((chip // 2 + plane % 2) % 2)

    down_to = (strip_of(p, z), 4 * k + z)
    down_from = (f % 4, 2 * strip_of(z, f % 4) + f // 4)
    down_moves = jnp.logical_or(down_to[0] != z, down_to[1] != f)
    out_to = (z, 4 * k + p)
    out_from = (z, 2 * (f % 4) + f // 4)
    out_moves = out_to[1] != f
    place.barrier(
        [place.d] + [place.cross((z + step) % LINE) for step in range(1, LINE)],
        [(down_moves, down_from), (out_moves, out_from)],
    )

    for i, ref in enumerate((gain_query, gain_key)):
        gains_qk[i : i + 1, :] = ref[:, at128(256 * (2 * z + k), 256)]
    loads = {}

    def load(name, src, dst):
        loads[name] = pltpu.make_async_copy(src, dst, ld.at[len(loads)])
        loads[name].start()

    dm[at128(z * 256 + k * rows)] = d_mlp[...]

    class Rows:
        def __init__(self, ref):
            self.ref = ref

        @property
        def at(self):
            ref = self.ref

            class At:
                def __getitem__(self, key):
                    c, core = key
                    return ref.at[at128(c * 256 + core * rows)]

            return At()

    gather_d = Gather(place, Rows(dm), zs.at[0], zr.at[0], cs.at[0], cr.at[0])
    gather_d.start()
    load("wd", h_dn, wd)
    load("ga", h_ga, ga)
    load("ua", h_ua, ua)
    load("wg", h_g, wg)
    load("wu", h_u, wu)
    load("hid", h_hid, hid)
    load("ms", h_m, ms)
    load("cot", h_cot, cotangent)
    load("branch", h_branch, branch)
    load("raw", h_raw, raw)
    load("tab", h_tab, tab)

    buffers = (term, pair_out, pair_in, keep, mine, line_out, line_in)
    sums = [RowSum(place, h, buffers, (ps, pr, ls, lr)) for h in range(2)]

    def chunk_rows(c):
        return at128(c * 256, 256)

    def expand(s, carry):
        c = place.order(s)
        gather_d.ready(c)
        here = chunk_rows(c)
        grad = dm[here]

        def act(t, inner):
            lanes = at128(t * 256, 256)
            dh = dot_rt(grad, wd[lanes])
            g = ga[here, lanes].astype(F32)
            u = ua[here, lanes].astype(F32)
            sig = 1.0 / (1.0 + jnp.exp(-g))
            dg[here, lanes] = (dh * u * sig * (1.0 + g * (1.0 - sig))).astype(BF16)
            du[here, lanes] = (dh * g * sig).astype(BF16)
            return inner

        lax.fori_loop(0, 4, act, 0)
        return carry

    def contract(s, carry):
        c = place.order(s)
        here = chunk_rows(c)
        left_g, left_u = dg[here], du[here]
        for h in range(2):
            out = slice(1024 * h, 1024 * h + 1024)
            term[...] = (dot_rt(left_g, wg[out]) + dot_rt(left_u, wu[out])).reshape(2, rows, 1024)
            sums[h].give(c, s)
        for h in range(2):
            pl.when(s > 0)(lambda h=h: sums[h].pass_on(place.order(s - 1), s + 1))
        return carry

    for name in ("wd", "ga", "ua"):
        loads[name].wait()
    lax.fori_loop(0, 1, expand, 0)
    for name in ("wg", "wu"):
        loads[name].wait()
    gather_d.arrive_first()
    lax.fori_loop(0, 1, contract, 0)
    for s in (1, 2):
        if s == 2:
            gather_d.arrive_second()
        lax.fori_loop(s, s + 1, expand, 0)
        lax.fori_loop(s, s + 1, contract, 0)
    gather_d.arrive_third()
    lax.fori_loop(3, 4, expand, 0)
    lax.fori_loop(3, 4, contract, 0)
    for h in range(2):
        sums[h].pass_on(place.order(3), 3)
    load("x", h_x, wd)
    load("qkv", h_qkv, wg.at[:, pl.ds(0, 768)])
    load("probs", h_probs, wu.at[:, pl.ds(0, 512)])
    load("qk", h_heads.at[pl.ds(0, 2048)], wu.at[:, pl.ds(512, 256)])
    load("v", h_heads.at[pl.ds(2048, 1024)], wu.at[pl.ds(0, 1024), pl.ds(768, 256)])
    load("att", h_att, wu.at[pl.ds(1024, 1024), pl.ds(768, 256)])

    chips = [place.p_x, place.p_y, place.p_d, p]
    near = [place.x, place.y, place.d]
    GATE, UP, DOWN, QKV, OUT = range(5)
    kinds = {GATE: (st_g, rc_g), UP: (st_u, rc_u), DOWN: (st_dn, rc_dn), QKV: (st_qkv, rc_qkv)}

    def half_of(kind, ref, i, half):
        if kind == DOWN:
            return ref.at[i, :, pl.ds(1024 * half, 1024)]
        return ref.at[i, pl.ds(256 * half, 256)]

    def far_part(kind, half):
        st, rc = kinds[kind]
        return remote(
            half_of(kind, st, 2, half), half_of(kind, rc, 2, half), in_send.at[kind, 2 + half],
            in_recv.at[kind, 2 + half], near[half],
        )

    def near_part(kind, i):
        st, rc = kinds[kind]
        return remote(st.at[i], rc.at[i], in_send.at[kind, i], in_recv.at[kind, i], near[i])

    def put(kind, i, buf, sem):
        wide = 896 if kind == QKV else 1024
        if i < 2:
            half = 1 - i
            far_part(kind, half).wait_recv()
            got = far_in.at[:, pl.ds(0, wide)]
            copy = pltpu.make_async_copy(half_of(kind, kinds[kind][1], 2, half), got, far_sem)
            copy.start()
            copy.wait()
            if kind == DOWN:
                now = (slice(None), slice(1024 * half, 1024 * half + 1024))
            else:
                now = (slice(256 * half, 256 * half + 256), slice(0, wide))
            buf[now] = (buf[now].astype(F32) + far_in[:, 0:wide].astype(F32)).astype(BF16)
        src = buf.at[:, pl.ds(0, 896)] if kind == QKV else buf
        copy = pltpu.make_async_copy(src, kinds[kind][0].at[i], st_sem.at[sem])
        copy.start()
        copy.wait()
        if i == 2:
            far_part(kind, 0).start()
            far_part(kind, 1).start()
        elif i < 2:
            near_part(kind, i).start()

    def feature_rows(ref, chip):
        return jnp.concatenate([ref[:, at128(512 * c + 128 * chip)] for c in range(LINE)], axis=1).T

    def gate_up_part(i):
        left = feature_rows(ms, chips[i])
        for m, right in enumerate((dg, du)):
            for t in range(2):
                lanes = slice(512 * t, 512 * t + 512)
                stage[m, :, lanes] = dot(left, right[:, lanes]).astype(BF16)
            put(m, i, stage.at[m], m)

    def down_part(i):
        left = hid[:, at128(strip_of(chips[i], z) * 256, 256)].T
        for t in range(4):
            lanes = slice(512 * t, 512 * t + 512)
            stage_d[:, lanes] = dot(left, dm[:, lanes]).astype(BF16)
        put(DOWN, i, stage_d, 2)

    loads["ms"].wait()
    loads["hid"].wait()
    gate_up_part(2)
    for h in range(2):
        sums[h].relay(False)
    down_part(2)
    gate_up_part(3)
    for h in range(2):
        sums[h].relay(True)
    gate_up_part(0)
    gate_up_part(1)
    gather_d.finish()

    def mean_of(v):
        return jnp.sum(v, axis=1, keepdims=True) / width

    loads["cot"].wait()
    loads["branch"].wait()
    d_mid[...] = cotangent[...].astype(F32) + jnp.concatenate([sums[h].total() for h in range(2)], axis=1)
    for h in range(2):
        sums[h].finish()
    b = branch[...]
    c_b = lax.rsqrt(mean_of(b * b) + EPSILON)
    gdy = gain_attn[...] * d_mid[...]
    db[at128(z * 256 + k * rows)] = (
        c_b * gdy - b * (c_b * c_b * c_b * mean_of(b * gdy))
    ).astype(BF16)
    gather_b = Gather(place, Rows(db), zs.at[1], zr.at[1], cs.at[1], cr.at[1])
    gather_b.start()
    gn_own[...] = jnp.zeros((8, width), F32)
    gn_own[2:3, :] = jnp.sum(d_mid[...] * b * c_b, axis=0, keepdims=True)
    gn_own[3:4, :] = gm_part[...]

    down_part(3)
    down_part(0)
    down_part(1)
    load("wo", h_wo, stage_d)

    for name in ("wo", "raw", "tab", "x", "qkv", "probs", "qk", "v", "att"):
        loads[name].wait()

    def attended_step(s, carry):
        c = place.order(s)
        gather_b.ready(c)
        part = dot_rt(db[chunk_rows(c)], stage_d[...]).astype(BF16)
        datt[:, at128(c * rows)] = part.reshape(2, rows, cols)
        return carry

    gather_b.arrive_first()
    lax.fori_loop(0, 2, attended_step, 0)
    gather_b.arrive_second()
    lax.fori_loop(2, 3, attended_step, 0)

    def fetch(kind, parts, first):
        copies = [
            pltpu.make_async_copy(src, dst, sum_sem.at[first + n]) for n, (src, dst) in enumerate(parts)
        ]
        for copy in copies:
            copy.start()
        for copy in copies:
            copy.wait()

    def to_owner(kind, src, dst):
        def go(c, core, device):
            return remote(
                src(c, core), dst.at[z, k], al_send.at[kind, c, core], al_recv.at[kind, z, k], device
            )

        def each(action):
            for step in range(1, LINE):
                c = (z + step) % LINE
                action(go(c, k, place.line(c)))
                action(go(c, 1 - k, place.cross(c)))
            action(go(z, 1 - k, place.partner))

        here = pltpu.make_async_copy(src(z, k), dst.at[z, k], al_loc.at[kind])
        each(lambda copy: copy.start())
        here.start()

        def wait():
            here.wait()
            each(lambda copy: copy.wait_send())
            for step in range(LINE):
                c = (z + step) % LINE
                for core in (0, 1):
                    got = remote(
                        src(c, k), dst.at[c, core], al_send.at[kind, c, core], al_recv.at[kind, c, core],
                        place.partner,
                    )
                    if step == 0:
                        pl.when(k != core)(lambda got=got: got.wait_recv())
                    else:
                        got.wait_recv()

        return wait

    waits = []

    def square_sum(kind, buf, other, lanes, dst):
        st, rc = kinds[kind]
        cut = pl.ds(0, lanes)
        near_part(kind, 0).wait_recv()
        near_part(kind, 1).wait_recv()
        fetch(
            kind,
            [
                (st.at[3], buf.at[pl.ds(0, 512), cut]),
                (rc.at[0], buf.at[pl.ds(512, 512), cut]),
                (rc.at[1], other.at[pl.ds(0, 512), cut]),
            ],
            3 * kind,
        )

        def add_up(t, carry):
            there = at128(t * 128)
            acc = buf[there, 0:lanes].astype(F32) + buf[at128(512 + t * 128), 0:lanes].astype(F32)
            buf[there, 0:lanes] = (acc + other[there, 0:lanes].astype(F32)).astype(BF16)
            return carry

        lax.fori_loop(0, 4, add_up, 0)
        waits.append(
            to_owner(
                min(kind, 2), lambda c, core: buf.at[at128(c * 128 + core * 64, 64), cut], dst
            )
        )

    square_sum(GATE, hid, ua, 1024, o_gu.at[0])
    gather_b.arrive_third()
    lax.fori_loop(3, 4, attended_step, 0)

    def attend(s, carry):
        there = at128(s * 512, 512)
        for h in range(2):
            lanes = slice(128 * h, 128 * h + 128)
            more = slice(512 + 128 * h, 640 + 128 * h)
            vals = slice(768 + 128 * h, 896 + 128 * h)
            low_p = wu[at128((2 * s + h) * 512, 512), 0:512]
            grad = datt[s, :, lanes]
            q = wu[there, more]
            key = wu[at128(1024 + s * 512, 512), more]
            value = wu[there, vals]
            d_value = dot_lt(low_p, grad).astype(BF16)
            d_probs = dot_rt(grad, value)
            pr32 = low_p.astype(F32)
            delta = jnp.sum(pr32 * d_probs, axis=1, keepdims=True)
            d_scores = (pr32 * (d_probs - delta)).astype(BF16)
            d_q = dot(d_scores, key) * (HD ** -0.5)
            d_k = dot_lt(d_scores, q) * (HD ** -0.5)
            for i, d in enumerate((d_q, d_k)):
                dy[i, s, :, lanes] = d * tab[0, s] - pltpu.roll(d, 64, 1) * tab[1, s]
            for c in range(LINE):
                ga[c * 256 + s * rows : c * 256 + s * rows + rows, vals.start - 256 : vals.stop - 256] = (
                    d_value[c * rows : c * rows + rows]
                )
        return carry

    for s in range(2):
        attend(s, 0)

    def dots_step(c, carry):
        there = at128(c * rows)
        pick = lax.broadcasted_iota(jnp.int32, (8, cols), 0)
        acc = jnp.zeros((8, 2 * rows), F32)
        for i in range(2):
            part = (raw[i, :, there] * dy[i, :, there]).reshape(2 * rows, cols) * gains_qk[i : i + 1]
            acc = acc + exact((pick == i).astype(F32), part, ((1,), (1,)))
        sq_own[c] = acc
        return carry

    lax.fori_loop(0, LINE, dots_step, 0)
    pair_sq = remote(sq_own, sq_pair, as_.at[0], ar.at[0], place.partner)
    pair_sq.start()
    pair_sq.wait_recv()
    sq_both[...] = sq_own[...] + sq_pair[...]

    def line_sq(step, source):
        return remote(
            sq_both, sq_line.at[source], as_.at[step], ar.at[1 + source], place.line((z + step) % LINE)
        )

    for step in range(1, LINE):
        line_sq(step, z).start()
    square_sum(UP, dg, du, 1024, o_gu.at[1])
    for step in range(1, LINE):
        line_sq(step, (z + step) % LINE).wait_recv()
    sq_line[z] = sq_both[...]

    def normalise(c, gains):
        there = at128(c * rows)
        means = ((sq_line[0, c] + sq_line[1, c]) + (sq_line[2, c] + sq_line[3, c])) / width
        now = scales[c]
        result = []
        for i in range(2):
            pick = (lax.broadcasted_iota(jnp.int32, (8, 128), 0) == i).astype(F32)
            scale = exact(now, pick, ((0,), (0,)))
            mean = exact(means, pick, ((0,), (0,)))
            gain_sum = []
            for h in range(2):
                lanes = slice(128 * h, 128 * h + 128)
                v = raw[i, :, there, lanes].reshape(2 * rows, 128)
                d = dy[i, :, there, lanes].reshape(2 * rows, 128)
                gain_sum.append(jnp.sum(d * v * scale, axis=0, keepdims=True))
                d = scale * gains_qk[i : i + 1, lanes] * d - v * (scale * scale * scale * mean)
                ga[chunk_rows(c), 256 * i + 128 * h : 256 * i + 128 * h + 128] = d.astype(BF16)
            result.append(gains[i] + jnp.concatenate(gain_sum, axis=1))
        return tuple(result)

    start = (jnp.zeros((1, cols), F32), jnp.zeros((1, cols), F32))
    gain_q, gain_k = lax.fori_loop(0, LINE, normalise, start)
    own_cols = at128(cols * (2 * z + k), cols)
    gn_own[0:1, own_cols] = gain_q
    gn_own[1:2, own_cols] = gain_k

    def token_step(s, carry):
        c = place.order(3 - s)
        left = ga[chunk_rows(c), 0:768]
        for h in range(2):
            term[...] = dot_rt(left, wg[1024 * h : 1024 * h + 1024, 0:768]).reshape(2, rows, 1024)
            sums[h].give(c, s)
        for h in range(2):
            pl.when(s > 0)(lambda h=h: sums[h].pass_on(place.order(4 - s), s + 1))
        return carry

    lax.fori_loop(0, 4, token_step, 0)
    for h in range(2):
        sums[h].pass_on(z, 3)

    def qkv_part(i):
        stage[0, :, 0:768] = dot(feature_rows(wd, chips[i]), ga[:, 0:768]).astype(BF16)
        sides = jnp.concatenate([gn_own[:, at128(512 * c + 128 * chips[i])] for c in range(LINE)], axis=1)
        lane = lax.broadcasted_iota(jnp.int32, (8, 128), 1)
        column = (lax.broadcasted_iota(jnp.int32, (8, 128), 0) == lane).astype(F32)
        stage[0, :, 768:896] = exact(sides, column, ((0,), (0,))).astype(BF16)
        put(QKV, i, stage.at[0], 3)

    qkv_part(2)
    for h in range(2):
        sums[h].relay(True)
    qkv_part(3)
    for s in range(2):
        for c in range(LINE):
            ua[c * 256 + s * rows : c * 256 + s * rows + rows, 0:256] = (
                wu[1024 + s * 512 + c * rows : 1024 + s * 512 + c * rows + rows, 768:1024]
            )

    def outer(t, carry):
        lanes = at128(t * 512, 512)
        stage_d[:, lanes] = dot_lt(ua[:, 0:256], db[:, lanes]).astype(BF16)
        return carry

    lax.fori_loop(0, 4, outer, 0)
    copy = pltpu.make_async_copy(stage_d, st_out, st_sem.at[0])
    copy.start()
    copy.wait()

    def out_part(i):
        return remote(
            st_out.at[at128(64 * chips[i], 64)], rc_out.at[i], in_send.at[OUT, i], in_recv.at[OUT, i], near[i]
        )

    qkv_part(0)
    qkv_part(1)
    for i in range(3):
        out_part(i).start()

    for h in range(2):
        sums[h].relay(False)

    near_part(DOWN, 0).wait_recv()
    near_part(DOWN, 1).wait_recv()
    fetch(
        DOWN,
        [
            (st_dn.at[3], ms.at[pl.ds(0, 256)]),
            (rc_dn.at[0], ms.at[pl.ds(256, 256)]),
            (rc_dn.at[1], ms.at[pl.ds(512, 256)]),
        ],
        3 * DOWN,
    )

    def add_down(t, carry):
        lanes = at128(t * 512, 512)
        acc = ms[0:256, lanes].astype(F32) + ms[256:512, lanes].astype(F32)
        dm[0:256, lanes] = (acc + ms[512:768, lanes].astype(F32)).astype(BF16)
        return carry

    lax.fori_loop(0, 4, add_down, 0)
    down_done = dm.at[pl.ds(0, 256)]
    fin_down = remote(down_done, o_down, fin_send.at[0], fin_recv.at[0], down_to)
    keep_down = pltpu.make_async_copy(down_done, o_down, fin_loc.at[0])
    pl.when(down_moves)(lambda: fin_down.start())
    pl.when(jnp.logical_not(down_moves))(lambda: keep_down.start())

    for h in range(2):
        out = slice(1024 * h, 1024 * h + 1024)
        o_tok[:, out] = (d_mid[:, out] + sums[h].total()).astype(BF16)
        sums[h].finish()

    square_sum(QKV, ua, du, 896, o_qkv)

    for i in range(3):
        out_part(i).wait_recv()
    sources = [rc_out.at[0], rc_out.at[1], rc_out.at[2], st_out.at[at128(64 * p, 64)]]
    copies = [
        pltpu.make_async_copy(src, ms.at[pl.ds(64 * i, 64)], sum_sem.at[16 + i])
        for i, src in enumerate(sources)
    ]
    for copy in copies:
        copy.start()
    for copy in copies:
        copy.wait()
    acc = ms[0:64].astype(F32) + ms[64:128].astype(F32)
    acc = acc + ms[128:192].astype(F32) + ms[192:256].astype(F32)
    ms[256:320] = acc.astype(BF16)
    out_done = ms.at[pl.ds(256, 64)]
    fin_out = remote(out_done, o_out, fin_send.at[1], fin_recv.at[1], out_to)
    keep_out = pltpu.make_async_copy(out_done, o_out, fin_loc.at[1])
    pl.when(out_moves)(lambda: fin_out.start())
    pl.when(jnp.logical_not(out_moves))(lambda: keep_out.start())

    gather_b.finish()
    pair_sq.wait_send()
    for step in range(1, LINE):
        line_sq(step, z).wait_send()
    for i in range(3):
        out_part(i).wait_send()
    for kind in kinds:
        for i in range(2):
            near_part(kind, i).wait_send()
            far_part(kind, i).wait_send()
    for wait in waits:
        wait()
    pl.when(down_moves)(lambda: fin_down.wait())
    pl.when(jnp.logical_not(down_moves))(lambda: keep_down.wait())
    pl.when(out_moves)(lambda: fin_out.wait())
    pl.when(jnp.logical_not(out_moves))(lambda: keep_out.wait())


def run_backward(gain_query, gain_key, gain_attn, d_mlp, cotangent, branch, scales, gm_part, kept):
    shape = jax.ShapeDtypeStruct
    dma = pltpu.SemaphoreType.DMA
    flat = [(2048, 768), (256, 2048), (2048, 1024), (2048, 1024), (1024, 2048), (1024, 2048), (1024, 2048),
            (1024, 1024), (1024, 1024), (1024, 1024), None, (3072, 256), (2048, 512), (1024, 256), None]
    kept = [a if s is None else a.reshape(s) for a, s in zip(kept, flat)]
    results = [
        shape((256, 2048), BF16),
        shape((64, 2048), BF16),
        shape((2, 4, 2, 64, 1024), BF16),
        shape((4, 2, 64, 896), BF16),
    ]
    transit = [
        shape((4, 512, 1024), BF16),
        shape((3, 512, 1024), BF16),
        shape((4, 512, 1024), BF16),
        shape((3, 512, 1024), BF16),
        shape((4, 256, 2048), BF16),
        shape((3, 256, 2048), BF16),
        shape((4, 512, 896), BF16),
        shape((3, 512, 896), BF16),
        shape((256, 2048), BF16),
        shape((3, 64, 2048), BF16),
    ]
    wide, square = pltpu.VMEM((1024, 2048), BF16), pltpu.VMEM((1024, 1024), BF16)
    tall = pltpu.VMEM((2048, 1024), BF16)
    rows = pltpu.VMEM((2, 4, 128, 1024), BF16)
    small = pltpu.VMEM((4, 8, 256), F32)
    return pl.pallas_call(
        backward_kernel,
        name="backward",
        out_shape=[shape((128, 2048), BF16)] + results + transit,
        in_specs=[vmem_spec()] * 4 + [any_spec()] * 2 + [vmem_spec()] * 2 + [any_spec()] * len(kept),
        out_specs=[vmem_spec()] + [any_spec()] * (len(results) + len(transit)),
        scratch_shapes=[
            wide, tall, tall, square, square, square, wide, square, square, wide, wide,
            pltpu.VMEM((2, 2, 512, 256), F32),
            pltpu.VMEM((2, 2, 512, 128), F32),
            pltpu.VMEM((2, 512, 256), BF16),
            pltpu.VMEM((2, 2, 512, 256), F32),
            pltpu.VMEM((2, 128, 1024), F32),
            rows,
            rows,
            pltpu.VMEM((2, 2, 128, 1024), F32),
            pltpu.VMEM((2, 128, 1024), F32),
            rows,
            rows,
            small,
            small,
            small,
            pltpu.VMEM((4, 4, 8, 256), F32),
            pltpu.VMEM((8, 2048), F32),
            pltpu.VMEM((128, 2048), F32),
            pltpu.VMEM((2, 512, 1024), BF16),
            pltpu.VMEM((256, 2048), BF16),
            pltpu.VMEM((256, 1024), BF16),
            pltpu.VMEM((2, 256), F32),
            pltpu.VMEM((128, 2048), BF16),
            pltpu.VMEM((128, 2048), F32),
            dma((18,)),
            dma(()),
            dma((2, 2, 4)), dma((2, 4)), dma((2, 4)), dma((2, 4)),
            dma((2, 4)), dma((2, 4)), dma((2, 4)), dma((2, 4)),
            dma((4,)), dma((5,)),
            dma((5, 4)), dma((5, 4)),
            dma((4,)), dma((20,)),
            dma((2,)), dma((2,)), dma((2,)),
            dma((3, 4, 2)), dma((3, 4, 2)), dma((3,)),
        ],
        compiler_params=pltpu.CompilerParams(
            collective_id=1, has_side_effects=True, vmem_limit_bytes=64 * 1024 * 1024
        ),
    )(gain_query, gain_key, gain_attn, d_mlp, cotangent, branch, scales, gm_part, *kept)[:5]


def arrange_kernel(
    gate_up, qkv, out_rows, down, result, d_tokens,
    o_result, o_tokens, o_q, o_k, o_v, o_out, o_gate, o_up, o_down, g_q, g_k, g_attn, g_mlp,
    v_gu, v_qkv, v_out, v_down, v_result, v_tokens, w_gu, w_qkv, w_out, w_down, in_sem, out_sem,
):
    reads = [
        pltpu.make_async_copy(src, dst, in_sem.at[i])
        for i, (src, dst) in enumerate([
            (gate_up, v_gu), (down, v_down), (qkv, v_qkv), (out_rows, v_out), (result, v_result),
            (d_tokens, v_tokens),
        ])
    ]
    for copy in reads:
        copy.start()
    writes = []

    def write(src, dst):
        copy = pltpu.make_async_copy(src, dst, out_sem.at[len(writes)])
        copy.start()
        writes.append(copy)

    reads[0].wait()
    for m, dst in enumerate((o_gate, o_up)):
        for z in range(LINE):
            for k in range(2):
                for q in range(PLANE):
                    at = 1024 * (2 * q + k) + 256 * z
                    w_gu[m, :, at : at + 256] = v_gu[m, z, k, :, 256 * q : 256 * q + 256].astype(F32)
        write(w_gu.at[m], dst)
    reads[1].wait()
    w_down[...] = v_down[...].astype(F32)
    write(w_down, o_down)
    reads[2].wait()
    total = jnp.zeros((64, 128), F32)
    for z in range(LINE):
        for k in range(2):
            at = 256 * (2 * z + k)
            for m in range(3):
                w_qkv[m, :, at : at + 256] = v_qkv[z, k, :, 256 * m : 256 * m + 256].astype(F32)
            total = total + v_qkv[z, k, :, 768:896].astype(F32)
    for m, dst in enumerate((o_q, o_k, o_v)):
        write(w_qkv.at[m], dst)
    lane = lax.broadcasted_iota(jnp.int32, (8, 128), 1)
    pick = (lax.broadcasted_iota(jnp.int32, (8, 128), 0) == lane).astype(F32)
    gains = exact(pick, total, ((1,), (1,)))
    for i, ref in enumerate((g_q, g_k, g_attn, g_mlp)):
        ref[...] = gains[i : i + 1]
    reads[3].wait()
    w_out[...] = v_out[...].astype(F32)
    write(w_out, o_out)
    reads[4].wait()
    write(v_result, o_result)
    reads[5].wait()
    write(v_tokens, o_tokens)
    for copy in writes:
        copy.wait()


def run_arrange(*arrays):
    shape = jax.ShapeDtypeStruct
    square = shape((64, 2048), F32)
    return pl.pallas_call(
        arrange_kernel,
        name="arrange",
        out_shape=[shape((128, 2048), BF16)] * 2 + [square] * 4 + [shape((64, 8192), F32)] * 2 + [shape((256, 2048), F32)]
        + [shape((1, 64), F32)] * 4,
        in_specs=[any_spec()] * 6,
        out_specs=[any_spec()] * 9 + [vmem_spec()] * 4,
        scratch_shapes=[pltpu.VMEM(a.shape, a.dtype) for a in arrays]
        + [
            pltpu.VMEM((2, 64, 8192), F32),
            pltpu.VMEM((3, 64, 2048), F32),
            pltpu.VMEM((64, 2048), F32),
            pltpu.VMEM((256, 2048), F32),
            pltpu.SemaphoreType.DMA((6,)),
            pltpu.SemaphoreType.DMA((9,)),
        ],
        compiler_params=pltpu.CompilerParams(vmem_limit_bytes=64 * 1024 * 1024),
    )(*arrays)


def shards_kernels(tokens, block_pairs, w_query, w_key, w_value, w_out, w_gate, w_up, w_down,
                   gain_query, gain_key, gain_attn, gain_mlp, cotangent):
    gains = [gain_query[None], gain_key[None], gain_attn[None]]
    out, d_mlp, gm_part, branch, scales, *kept = run_forward(
        block_pairs, *gains, gain_mlp[None], tokens[0], cotangent[0],
        (w_query, w_key, w_value, w_out, w_gate, w_up, w_down),
    )
    d_tokens, down, out_rows, gate_up, qkv = run_backward(
        *gains, d_mlp, cotangent[0], branch, scales, gm_part, kept
    )
    out, d_tokens, *grads = run_arrange(gate_up, qkv, out_rows, down, out, d_tokens)
    return (out[None], d_tokens[None], *grads[:7], *[g[0] for g in grads[7:]])


def shards(*arrays):
    tokens, w_query, w_down = arrays[0], arrays[2], arrays[8]
    here = (lax.axis_size("ctx"), lax.axis_size("fsdp"), tokens.shape, w_query.shape, w_down.shape)
    if here == (LINE, 2 * PLANE, (1, 128, 2048), (256, 2048), (1024, 2048)):
        return shards_kernels(*arrays)
    return shards_general(*arrays)


def solution(mesh):
    in_specs = (
        P("fsdp", "ctx", None),
        P("fsdp", None),
        P("fsdp", None),
        P("fsdp", None),
        P("fsdp", None),
        P("fsdp", None),
        P("fsdp", None),
        P("fsdp", None),
        P("fsdp", None),
        P(),
        P(),
        P(),
        P(),
        P("fsdp", "ctx", None),
    )
    out_specs = (
        P("fsdp", "ctx", None),
        P("fsdp", "ctx", None),
        P(("ctx", "fsdp"), None),
        P(("ctx", "fsdp"), None),
        P(("ctx", "fsdp"), None),
        P(("ctx", "fsdp"), None),
        P(("ctx", "fsdp"), None),
        P(("ctx", "fsdp"), None),
        P(("ctx", "fsdp"), None),
        P(("ctx", "fsdp")),
        P(("ctx", "fsdp")),
        P(("ctx", "fsdp")),
        P(("ctx", "fsdp")),
    )
    return jax.shard_map(shards, mesh=mesh, in_specs=in_specs, out_specs=out_specs, check_vma=False)
```

```python
import math

import jax
import jax.numpy as jnp
from jax import lax
from jax.experimental import pallas as pl
from jax.experimental.pallas import tpu as pltpu
from jax.sharding import PartitionSpec as P

HD = 128


EPSILON = 1e-06
ROPE_BASE = 500000.0
NEGATIVE = -1e30


def norm_scale(values, gain_vec):
    return (
        values * lax.rsqrt(jnp.mean(values * values, axis=-1, keepdims=True) + EPSILON) * gain_vec
    )


def turn_half(values, cosine, sine):
    half_size = values.shape[-1] // 2
    turned = jnp.concatenate([-values[..., half_size:], values[..., :half_size]], axis=-1)
    return values * cosine + turned * sine


def angle_tables(positions, head_size):
    half_size = head_size // 2
    frequency = jnp.power(ROPE_BASE, -(jnp.arange(half_size).astype(jnp.float32) * 2.0 / head_size))
    angles = positions.astype(jnp.float32)[:, None] * frequency[None, :]
    angles = jnp.concatenate([angles, angles], axis=-1)
    return (jnp.cos(angles)[:, None, :], jnp.sin(angles)[:, None, :])


def row_positions(row_ids, pair_row, block_rows, ctx_count):
    rank_of = row_ids // (2 * block_rows)
    second = row_ids // block_rows % 2
    offset = row_ids % block_rows
    rank_match = (rank_of[:, None] == jnp.arange(ctx_count, dtype=jnp.int32)[None, :]).astype(
        jnp.int32
    )
    chosen = jnp.sum(rank_match * pair_row[None, :], axis=1)
    block_index = jnp.where(second == 0, chosen, 2 * ctx_count - 1 - chosen)
    return block_index * block_rows + offset


def times_transpose(left, right):
    return lax.dot_general(
        left, right, (((1,), (1,)), ((), ())), preferred_element_type=jnp.float32
    )


def transpose_times(left, right):
    return lax.dot_general(
        left, right, (((0,), (0,)), ((), ())), preferred_element_type=jnp.float32
    )


def activate(gate_in, up_in):
    return jax.nn.silu(gate_in) * up_in


def spread_rows(values, outer, inner):
    rows, width = values.shape
    return (
        values.reshape(outer, inner, rows // (outer * inner), width)
        .transpose(1, 0, 2, 3)
        .reshape(rows, width)
    )


def shards_general(
    tokens,
    block_pairs,
    w_query,
    w_key,
    w_value,
    w_out,
    w_gate,
    w_up,
    w_down,
    gain_query,
    gain_key,
    gain_attn,
    gain_mlp,
    cotangent,
):
    bf16 = jnp.bfloat16
    f32 = jnp.float32
    local_rows = tokens.shape[1]
    block_rows = local_rows // 2
    width = w_query.shape[1]
    hidden_width = w_gate.shape[1]
    ctx_count = lax.axis_size("ctx")
    fsdp_count = lax.axis_size("fsdp")
    ctx_index = lax.axis_index("ctx")
    seq = local_rows * ctx_count
    cols = width // ctx_count
    heads = cols // HD
    strip = hidden_width // (ctx_count * fsdp_count)
    hid = strip * fsdp_count
    scale = HD ** (-0.5)

    def ctx_cols(w):
        return lax.dynamic_slice_in_dim(w, ctx_index * cols, cols, 1)

    def ctx_strips(w):
        parts = w.reshape(w.shape[0], fsdp_count, ctx_count, strip)
        return lax.dynamic_index_in_dim(parts, ctx_index, 2, keepdims=False).reshape(w.shape[0], hid)

    token_rows = tokens[0]
    x_all = lax.all_gather(token_rows, "ctx", axis=0, tiled=True)
    qkv_w = lax.all_gather(
        jnp.concatenate([ctx_cols(w_query), ctx_cols(w_key), ctx_cols(w_value)], axis=1),
        "fsdp", axis=0, tiled=True,
    )
    out_w = lax.dynamic_slice_in_dim(
        lax.all_gather(w_out, "fsdp", axis=0, tiled=True), ctx_index * cols, cols, 0
    )
    gate_w = lax.all_gather(ctx_strips(w_gate), "fsdp", axis=0, tiled=True)
    up_w = lax.all_gather(ctx_strips(w_up), "fsdp", axis=0, tiled=True)
    down_w = lax.all_gather(
        lax.dynamic_slice_in_dim(w_down, ctx_index * strip, strip, 0), "fsdp", axis=0, tiled=True
    )

    pos = row_positions(jnp.arange(seq, dtype=jnp.int32), block_pairs[0], block_rows, ctx_count)
    cosine, sine = angle_tables(pos, HD)
    mask = pos[None, :] <= pos[:, None]
    gain_q = lax.dynamic_slice_in_dim(gain_query, ctx_index * cols, cols)
    gain_k = lax.dynamic_slice_in_dim(gain_key, ctx_index * cols, cols)

    qkv = jnp.dot(x_all, qkv_w, preferred_element_type=f32)
    q_raw, k_raw, v_raw = qkv[:, :cols], qkv[:, cols : 2 * cols], qkv[:, 2 * cols :]
    squares = jnp.stack([jnp.sum(q_raw * q_raw, axis=1), jnp.sum(k_raw * k_raw, axis=1)])
    squares = lax.psum(squares, "ctx")
    scales = lax.rsqrt(squares / width + EPSILON)
    c_q, c_k = scales[0][:, None], scales[1][:, None]

    def rope(v):
        return turn_half(v.reshape(seq, heads, HD), cosine, sine)

    def rope_back(w):
        w = w.reshape(seq, heads, HD)
        u = w * sine
        half = HD // 2
        turned = jnp.concatenate([u[..., half:], -u[..., :half]], axis=-1)
        return (w * cosine + turned).reshape(seq, cols)

    queries = rope(q_raw * c_q * gain_q).astype(bf16)
    keys = rope(k_raw * c_k * gain_k).astype(bf16)
    values = v_raw.astype(bf16).reshape(seq, heads, HD)
    scores = jnp.einsum("qhd,khd->hqk", queries, keys, preferred_element_type=f32) * scale
    scores = jnp.where(mask[None], scores, NEGATIVE)
    exponent = jnp.exp(scores - jnp.max(scores, axis=-1, keepdims=True))
    probs = exponent / jnp.sum(exponent, axis=-1, keepdims=True)
    prob_low = probs.astype(bf16)
    attended = (
        jnp.einsum("hqk,khd->qhd", prob_low, values, preferred_element_type=f32)
        .reshape(seq, cols)
        .astype(bf16)
    )
    branch = lax.psum_scatter(
        jnp.dot(attended, out_w, preferred_element_type=f32).astype(bf16),
        "ctx", scatter_dimension=0, tiled=True,
    ).astype(f32)
    mid = token_rows.astype(f32) + norm_scale(branch, gain_attn)
    mid_all = lax.all_gather(mid.astype(bf16), "ctx", axis=0, tiled=True)
    gate_act = jnp.dot(mid_all, gate_w, preferred_element_type=f32)
    up_act = jnp.dot(mid_all, up_w, preferred_element_type=f32)
    hidden = activate(gate_act, up_act).astype(bf16)
    mlp_out = lax.psum_scatter(
        jnp.dot(hidden, down_w, preferred_element_type=f32).astype(bf16),
        "ctx", scatter_dimension=0, tiled=True,
    ).astype(f32)
    output = (mid + norm_scale(mlp_out, gain_mlp)).astype(bf16)

    d_output = cotangent[0].astype(f32)
    unused_mlp, pull_mlp = jax.vjp(norm_scale, mlp_out, gain_mlp)
    d_mlp, grad_gm = pull_mlp(d_output)
    d_mlp_all = lax.all_gather(d_mlp.astype(bf16), "ctx", axis=0, tiled=True)
    d_hidden = times_transpose(d_mlp_all, down_w)
    unused_act, pull_act = jax.vjp(activate, gate_act, up_act)
    d_gate, d_up = pull_act(d_hidden)
    d_gate = d_gate.astype(bf16)
    d_up = d_up.astype(bf16)
    d_mid_part = times_transpose(d_gate, gate_w) + times_transpose(d_up, up_w)
    d_mid = d_output + lax.psum_scatter(
        d_mid_part.astype(bf16), "ctx", scatter_dimension=0, tiled=True
    ).astype(f32)

    down_sum = lax.psum_scatter(
        transpose_times(hidden, d_mlp_all).astype(bf16), "fsdp", scatter_dimension=0, tiled=True
    )
    moves = [
        (z * fsdp_count + f, f * ctx_count + z)
        for z in range(ctx_count)
        for f in range(fsdp_count)
    ]
    grad_down = lax.ppermute(down_sum, ("ctx", "fsdp"), moves).astype(f32)

    def column_grad(left, right):
        part = transpose_times(left, right).astype(bf16)
        mine = lax.psum_scatter(
            spread_rows(part, ctx_count, fsdp_count), "fsdp", scatter_dimension=0, tiled=True
        )
        mine = mine.reshape(ctx_count, mine.shape[0] // ctx_count, mine.shape[1])
        return lax.all_to_all(mine, "ctx", 0, 0, tiled=True)

    gate_up = column_grad(mid_all, jnp.concatenate([d_gate, d_up], axis=1))
    rows = gate_up.shape[1]

    def from_strips(part):
        return (
            part.reshape(ctx_count, rows, fsdp_count, strip)
            .transpose(1, 2, 0, 3)
            .reshape(rows, hidden_width)
            .astype(f32)
        )

    unused_branch, pull_branch = jax.vjp(norm_scale, branch, gain_attn)
    d_branch, grad_ga = pull_branch(d_mid)
    d_branch_all = lax.all_gather(d_branch.astype(bf16), "ctx", axis=0, tiled=True)
    d_attended = times_transpose(d_branch_all, out_w).astype(bf16).reshape(seq, heads, HD)
    grad_out = lax.psum_scatter(
        transpose_times(attended, d_branch_all).astype(bf16),
        "fsdp", scatter_dimension=0, tiled=True,
    ).astype(f32)

    d_values = jnp.einsum("hqk,qhd->khd", prob_low, d_attended, preferred_element_type=f32)
    d_values = d_values.astype(bf16).reshape(seq, cols)
    d_probs = jnp.einsum("qhd,khd->hqk", d_attended, values, preferred_element_type=f32)
    delta = jnp.sum(probs * d_probs, axis=-1, keepdims=True)
    d_scores = (probs * (d_probs - delta)).astype(bf16)
    d_queries = jnp.einsum("hqk,khd->qhd", d_scores, keys, preferred_element_type=f32) * scale
    d_keys = jnp.einsum("hqk,qhd->khd", d_scores, queries, preferred_element_type=f32) * scale
    dy_q = rope_back(d_queries)
    dy_k = rope_back(d_keys)
    dots = jnp.stack([
        jnp.sum(q_raw * gain_q * dy_q, axis=1), jnp.sum(k_raw * gain_k * dy_k, axis=1)
    ])
    dots = lax.psum(dots, "ctx") / width
    d_q = c_q * gain_q * dy_q - q_raw * (c_q * c_q * c_q * dots[0][:, None])
    d_k = c_k * gain_k * dy_k - k_raw * (c_k * c_k * c_k * dots[1][:, None])
    d_qkv = jnp.concatenate([d_q.astype(bf16), d_k.astype(bf16), d_values], axis=1)
    d_tokens = d_mid + lax.psum_scatter(
        times_transpose(d_qkv, qkv_w).astype(bf16), "ctx", scatter_dimension=0, tiled=True
    ).astype(f32)
    qkv_grad = column_grad(x_all, d_qkv).transpose(1, 0, 2)
    sum_gqk = lax.psum_scatter(
        jnp.stack([jnp.sum(dy_q * q_raw * c_q, axis=0), jnp.sum(dy_k * k_raw * c_k, axis=0)]),
        "fsdp", scatter_dimension=1, tiled=True,
    )
    sum_gam = lax.psum_scatter(
        jnp.stack([grad_ga, grad_gm]), ("ctx", "fsdp"), scatter_dimension=1, tiled=True
    )

    def whole(part):
        return part.reshape(part.shape[0], width).astype(f32)

    return (
        output[None],
        d_tokens.astype(bf16)[None],
        whole(qkv_grad[:, :, :cols]),
        whole(qkv_grad[:, :, cols : 2 * cols]),
        whole(qkv_grad[:, :, 2 * cols :]),
        grad_out,
        from_strips(gate_up[:, :, :hid]),
        from_strips(gate_up[:, :, hid:]),
        grad_down,
        sum_gqk[0],
        sum_gqk[1],
        sum_gam[0],
        sum_gam[1],
    )


MESH = pl.DeviceIdType.MESH
BF16 = jnp.bfloat16
F32 = jnp.float32
LINE = 4
PLANE = 4


def dot(left, right):
    return lax.dot_general(left, right, (((1,), (0,)), ((), ())), preferred_element_type=F32)


def dot_rt(left, right):
    return lax.dot_general(left, right, (((1,), (1,)), ((), ())), preferred_element_type=F32)


def dot_lt(left, right):
    return lax.dot_general(left, right, (((0,), (0,)), ((), ())), preferred_element_type=F32)


def exact(left, right, dims):
    return lax.dot_general(
        left, right, (dims, ((), ())), precision=lax.Precision.HIGHEST, preferred_element_type=F32
    )


def remote(src, dst, send, recv, device):
    return pltpu.make_async_remote_copy(
        src_ref=src, dst_ref=dst, send_sem=send, recv_sem=recv, device_id=device, device_id_type=MESH
    )


def at128(i, step=128):
    return pl.ds(i if isinstance(i, int) else pl.multiple_of(i, step), step)


class Place:
    def __init__(self):
        z = lax.axis_index("ctx")
        f = lax.axis_index("fsdp")
        self.z, self.f = z, f
        self.p, self.k = f // 2, f % 2
        self.p_x = self.p + 1 - 2 * (self.p % 2)
        self.p_y = (self.p + 2) % PLANE
        self.p_d = PLANE - 1 - self.p
        self.partner = (z, 2 * self.p + 1 - self.k)
        self.x = (z, 2 * self.p_x + self.k)
        self.y = (z, 2 * self.p_y + self.k)
        self.d = (z, 2 * self.p_d + self.k)
        self.ends = z // 3 + (3 - z) // 3

    def line(self, c):
        return (c, self.f)

    def order(self, s):
        z, e, t = self.z, self.ends, s // 3
        end = z + s * (1 - 2 * (z // 3))
        mid = (1 - t) * (z + (3 * s * s - 5 * s) // 2) + t * 3 * (2 - z)
        return e * end + (1 - e) * mid

    def cross(self, c):
        return (c, 2 * self.p + 1 - self.k)

    def barrier(self, more=(), senders=()):
        sem = pltpu.get_barrier_semaphore()

        def greet(peer):
            pl.semaphore_signal(sem, inc=1, device_id=peer, device_id_type=MESH)

        peers = [self.partner, self.x, self.y] + list(more)
        peers += [self.line((self.z + step) % LINE) for step in range(1, LINE)]
        for peer in peers:
            greet(peer)
        count = len(peers)
        for here, peer in senders:
            pl.when(here)(lambda peer=peer: greet(peer))
            count = count + here.astype(jnp.int32)
        pl.semaphore_wait(sem, count)


class Gather:
    def __init__(self, place, buf, z_send, z_recv, c_send, c_recv):
        self.pl, self.buf = place, buf
        self.sems = z_send, z_recv, c_send, c_recv

    def to_line(self, c, target, way):
        z_send, z_recv, _, _ = self.sems
        part = self.buf.at[c, self.pl.k]
        return remote(part, part, z_send.at[way, c], z_recv.at[c], self.pl.line(target))

    def to_core(self, c):
        _, _, c_send, c_recv = self.sems
        part = self.buf.at[c, self.pl.k]
        return remote(part, part, c_send.at[c], c_recv.at[c], self.pl.partner)

    def from_core(self, c):
        _, _, c_send, c_recv = self.sems
        part = self.buf.at[c, 1 - self.pl.k]
        return remote(part, part, c_send.at[c], c_recv.at[c], self.pl.partner)

    def start(self):
        z = self.pl.z
        pl.when(z < LINE - 1)(lambda: self.to_line(z, z + 1, 0).start())
        pl.when(z > 0)(lambda: self.to_line(z, z - 1, 1).start())
        self.to_core(z).start()

    def arrive(self, c):
        z = self.pl.z
        self.to_line(c, z, 0).wait_recv()
        pl.when(jnp.logical_and(c < z, z < LINE - 1))(lambda: self.to_line(c, z + 1, 0).start())
        pl.when(jnp.logical_and(c > z, z > 0))(lambda: self.to_line(c, z - 1, 1).start())
        self.to_core(c).start()

    def arrive_first(self):
        self.arrive(self.pl.order(1))
        pl.when(self.pl.ends == 0)(lambda: self.arrive(self.pl.order(2)))

    def arrive_second(self):
        self.arrive(self.pl.order(3 - self.pl.ends))

    def arrive_third(self):
        pl.when(self.pl.ends == 1)(lambda: self.arrive(self.pl.order(3)))

    def ready(self, c):
        self.from_core(c).wait_recv()

    def finish(self):
        z = self.pl.z

        def body(c, carry):
            pl.when(jnp.logical_and(c <= z, z < LINE - 1))(
                lambda: self.to_line(c, z, 0).wait_send()
            )
            pl.when(jnp.logical_and(c >= z, z > 0))(lambda: self.to_line(c, z, 1).wait_send())
            self.to_core(c).wait_send()
            return carry

        lax.fori_loop(0, LINE, body, 0)


class RowSum:
    def __init__(self, place, h, buffers, sems):
        self.pl, self.h = place, h
        self.term, self.pair_out, self.pair_in, self.keep, self.mine, self.line_out, self.line_in = buffers
        self.p_send, self.p_recv, self.l_send, self.l_recv = sems

    def pair(self, c):
        h = self.h
        return remote(
            self.pair_out.at[h, c], self.pair_in.at[h, c], self.p_send.at[h, c], self.p_recv.at[h, c],
            self.pl.partner,
        )

    def line(self, c, slot, target):
        h = self.h
        return remote(
            self.line_out.at[h, c], self.line_in.at[h, slot], self.l_send.at[h, c],
            self.l_recv.at[h, slot], self.pl.line(target),
        )

    def mate(self):
        return self.pl.z + 1 - 2 * (self.pl.z % 2)

    def give(self, c, s):
        h, k = self.h, self.pl.k
        self.pair_out[h, c] = self.term[1 - k].astype(BF16)
        self.pair(c).start()
        self.keep[h, s % 2] = self.term[k]

    def pass_on(self, c, s):
        h, z = self.h, self.pl.z
        near = c // 2 == z // 2
        end = self.pl.ends == 1
        self.pair(c).wait_recv()

        @pl.when(c == z)
        def _():
            self.mine[h] = self.keep[h, s % 2] + self.pair_in[h, c].astype(F32)

        @pl.when(c != z)
        def _():
            self.line_out[h, c] = (self.keep[h, s % 2] + self.pair_in[h, c].astype(F32)).astype(BF16)

        pl.when(jnp.logical_and(c != z, near))(lambda: self.line(c, z, c).start())
        pl.when(jnp.logical_and(jnp.logical_not(near), end))(
            lambda: self.line(c, 2 * c - 3 * (1 - z // 2), self.mate()).start()
        )

    def relay(self, far):
        h, z = self.h, self.pl.z

        @pl.when(self.pl.ends == 0)
        def _():
            c = 3 * (2 - z) if far else 3 - z
            slot = 2 * c - 3 * (2 - z)
            self.line(c, slot, z).wait_recv()
            self.line_out[h, c] = (
                self.line_out[h, c].astype(F32) + self.line_in[h, slot].astype(F32)
            ).astype(BF16)
            self.line(c, z, c).start()

    def total(self):
        h, z = self.h, self.pl.z
        result = self.mine[h]
        for source in (self.mate(), 2 - z // 2):
            self.line(source, source, source).wait_recv()
            result = result + self.line_in[h, source].astype(F32)
        return result

    def finish(self):
        z = self.pl.z

        def body(c, carry):
            self.pair(c).wait_send()
            pl.when(c != z)(lambda: self.line(c, z, c).wait_send())
            return carry

        lax.fori_loop(0, LINE, body, 0)


class Ring:
    def __init__(self, place, buf, rows, send, recv):
        self.pl, self.buf, self.rows = place, buf, rows
        self.send, self.recv = send, recv

    def block(self, p):
        return self.buf.at[at128(p * self.rows, self.rows)]

    def half(self, p, i):
        size = self.rows // 2
        return self.buf.at[at128(p * self.rows + i * size, size)]

    def own(self, way):
        part = self.block(self.pl.p)
        return remote(part, part, self.send.at[way], self.recv.at[way], (self.pl.x, self.pl.y)[way])

    def far(self, i):
        part = self.half((self.pl.p_x, self.pl.p_y)[i], i)
        return remote(part, part, self.send.at[2 + i], self.recv.at[2 + i], (self.pl.y, self.pl.x)[i])

    def start(self):
        self.own(0).start()
        self.own(1).start()

    def forward(self):
        for i in range(2):
            part = self.block((self.pl.p_x, self.pl.p_y)[i])
            remote(part, part, self.send.at[i], self.recv.at[i], (self.pl.x, self.pl.y)[i]).wait_recv()
            self.far(i).start()

    def ready(self):
        for i in range(2):
            part = self.half(self.pl.p_d, i)
            remote(part, part, self.send.at[2 + i], self.recv.at[2 + i], self.pl.x).wait_recv()

    def finish(self):
        for i in range(2):
            self.own(i).wait_send()
            self.far(i).wait_send()


def scale_columns(totals, rows, which):
    pick = (lax.broadcasted_iota(jnp.int32, (8, 128), 0) == which).astype(F32)
    return exact(totals[:, rows], pick, ((0,), (0,)))


def forward_kernel(
    pairs, gain_query, gain_key, gain_attn, gain_mlp, tokens, cotangent,
    w_query, w_key, w_value, w_out, w_gate, w_up, w_down,
    o_out, o_dmlp, o_gm, o_branch, o_tot,
    o_qkv, o_wo, o_g, o_u, o_dn, o_x, o_m, o_ga, o_ua, o_hid, o_raw, o_heads, o_probs, o_att, o_tab,
    qkv, wo, wg, wu, wd, xs, ms, ga, ua, hid, raw, heads, probs, att, tab, posr, posc,
    term, pair_out, pair_in, keep, mine, line_out, line_in,
    sq_own, sq_pair, sq_both, sq_line, mid, gains_qk, branch_kept,
    loc_sem, swap_send, swap_recv, ring_send, ring_recv, wo_send, wo_recv,
    zs, zr, cs, cr, ps, pr, ls, lr, ts, tr, as_, ar, out_sem,
):
    place = Place()
    z, f, p, k = place.z, place.f, place.p, place.k
    rows = 128
    width = 2048
    cols = 256
    seq = 512
    place.barrier()

    for i, ref in enumerate((gain_query, gain_key)):
        gains_qk[i : i + 1, :] = ref[:, at128(256 * (2 * z + k), 256)]

    def own_rows(n):
        return at128(n * (2 * p + k), n)

    def strips(core):
        return [1024 * (2 * q + core) + 256 * z for q in range(PLANE)]

    local, swap = {}, {}

    def split(name, w, buf, sources, first):
        local[name], swap[name] = [], []
        for i, (mine, theirs) in enumerate(sources):
            dst = buf.at[own_rows(256), pl.ds(256 * i + first[1], 256)]
            local[name].append(
                pltpu.make_async_copy(w.at[:, at128(mine, 256)], dst, loc_sem.at[first[0] + i])
            )
            swap[name].append(
                remote(
                    w.at[:, at128(theirs, 256)], dst, swap_send.at[first[0] + i],
                    swap_recv.at[first[0] + i], place.partner,
                )
            )

    head_cols = [(256 * (2 * z + k), 256 * (2 * z + 1 - k))]
    hid_cols = list(zip(strips(k), strips(1 - k)))
    split("q", w_query, qkv, head_cols, (0, 0))
    split("k", w_key, qkv, head_cols, (1, 256))
    split("v", w_value, qkv, head_cols, (2, 512))
    split("g", w_gate, wg, hid_cols, (3, 0))
    split("u", w_up, wu, hid_cols, (7, 0))

    def begin(*names):
        for name in names:
            for a, b in zip(local[name], swap[name]):
                b.start()
                a.start()

    def settle(*names):
        for name in names:
            for a, b in zip(local[name], swap[name]):
                a.wait()
                b.wait_recv()

    dx, dy = (p % 2 + z % 2) % 2, (p // 2 + z // 2) % 2
    top, low = wo.at[pl.ds(0, 128)], wo.at[pl.ds(128, 128)]
    wo_copy = pltpu.make_async_copy(w_out, wo, loc_sem.at[12])

    def wo_first(i, device):
        rows_i = pl.ds(128 * i, 128)
        return remote(w_out.at[rows_i], wo.at[rows_i], wo_send.at[i], wo_recv.at[i], device)

    def wo_send_to(i, part, device):
        return remote(part, part, wo_send.at[i], wo_recv.at[i], device)

    is_source = jnp.logical_and(dx == 0, dy == 0)
    is_x = jnp.logical_and(dx == 1, dy == 0)
    is_y = jnp.logical_and(dx == 0, dy == 1)
    is_d = jnp.logical_and(dx == 1, dy == 1)

    @pl.when(is_source)
    def _():
        wo_copy.start()
        wo_first(0, place.x).start()
        wo_first(1, place.y).start()

    begin("q", "k", "v")
    xs[z, k] = tokens[...]
    gather_x = Gather(place, xs, zs.at[0], zr.at[0], cs.at[0], cr.at[0])
    gather_x.start()
    down_copies = [
        pltpu.make_async_copy(
            w_down.at[at128(256 * z, 256), pl.ds(1024 * h, 1024)], wd.at[h, at128(256 * p, 256)],
            loc_sem.at[(11, 13)[h]],
        )
        for h in range(2)
    ]
    for copy in down_copies:
        copy.start()
    begin("g", "u")
    ring_qkv = Ring(place, qkv, 512, ring_send.at[0], ring_recv.at[0])
    ring_g = Ring(place, wg, 512, ring_send.at[1], ring_recv.at[1])
    ring_u = Ring(place, wu, 512, ring_send.at[2], ring_recv.at[2])
    ring_d = [Ring(place, wd.at[h], 256, ring_send.at[3 + h], ring_recv.at[3 + h]) for h in range(2)]
    settle("q", "k", "v")
    ring_qkv.start()

    def positions(shape, axis):
        i = lax.broadcasted_iota(jnp.int32, shape, axis)
        block = i // 64
        pos = jnp.zeros(shape, jnp.int32)
        for r in range(LINE):
            b = pairs[0, r]
            pos = pos + jnp.where(block == 2 * r, b * 64, 0)
            pos = pos + jnp.where(block == 2 * r + 1, (2 * LINE - 1 - b) * 64, 0)
        return (pos + i % 64).astype(F32)

    posr[k] = positions((8, seq), 1)
    col = positions((seq, 128), 0)
    posc[k] = col
    lane = lax.broadcasted_iota(jnp.int32, (seq, 128), 1)
    freq = jnp.exp((lane % 64).astype(F32) * (-2.0 / HD * math.log(ROPE_BASE)))
    angle = col * freq
    tab[0, k] = jnp.cos(angle)
    sine = jnp.sin(angle)
    tab[1, k] = jnp.where(lane < 64, -sine, sine)
    tables = [
        remote(r, r, ts.at[i], tr.at[i], place.partner)
        for i, r in enumerate([posr.at[k], posc.at[k], tab.at[0, k], tab.at[1, k]])
    ]
    for t in tables:
        t.start()

    gather_x.arrive_first()
    pl.when(is_x)(lambda: wo_send_to(0, top, place.x).wait_recv())
    pl.when(is_x)(lambda: wo_send_to(0, top, place.y).start())
    pl.when(is_y)(lambda: wo_send_to(1, low, place.x).wait_recv())
    pl.when(is_y)(lambda: wo_send_to(1, low, place.x).start())
    ring_qkv.forward()
    settle("g", "u")
    gather_x.arrive_second()

    @pl.when(is_d)
    def _():
        wo_send_to(0, top, place.x).wait_recv()
        wo_send_to(0, top, place.x).start()
        wo_send_to(1, low, place.x).wait_recv()
        wo_send_to(1, low, place.y).start()

    ring_g.start()
    ring_qkv.ready()

    def project(c):
        gather_x.ready(c)
        chunk = xs[c].reshape(2 * rows, width)
        there = at128(c * rows)
        sums = jnp.zeros((8, 2 * rows), F32)
        pick = lax.broadcasted_iota(jnp.int32, (8, cols), 0)
        for i in range(2):
            part = dot(chunk, qkv[:, i * cols : (i + 1) * cols])
            raw[i, :, there] = part.reshape(2, rows, cols)
            sums = sums + exact((pick == i).astype(F32), part * part, ((1,), (1,)))
        part = dot(chunk, qkv[:, 2 * cols :])
        heads[2, :, there] = part.astype(BF16).reshape(2, rows, cols)
        sq_own[c] = sums

    def project_step(s, carry):
        project(place.order(s))
        return carry

    lax.fori_loop(0, 3, project_step, 0)
    gather_x.arrive_third()
    lax.fori_loop(3, 4, project_step, 0)

    pair_sq = remote(sq_own, sq_pair, as_.at[0], ar.at[0], place.partner)
    pair_sq.start()
    ring_u.start()
    pair_sq.wait_recv()
    sq_both[...] = sq_own[...] + sq_pair[...]

    def line_sq(step, source):
        return remote(
            sq_both, sq_line.at[source], as_.at[step], ar.at[1 + source],
            place.line((z + step) % LINE),
        )

    for step in range(1, LINE):
        line_sq(step, z).start()
    for t in tables:
        t.wait_recv()
    for step in range(1, LINE):
        line_sq(step, (z + step) % LINE).wait_recv()
    sq_line[z] = sq_both[...]
    total = (sq_line[0] + sq_line[1]) + (sq_line[2] + sq_line[3])
    scales = lax.rsqrt(total / width + EPSILON)
    o_tot[...] = scales

    def rotate(c, carry):
        there = at128(c * rows)
        now = o_tot[c]
        for i in range(2):
            pick = (lax.broadcasted_iota(jnp.int32, (8, 128), 0) == i).astype(F32)
            column = exact(now, pick, ((0,), (0,)))
            for s in range(2):
                for h in range(2):
                    lanes = slice(128 * h, 128 * h + 128)
                    v = raw[i, s, there, lanes] * column[128 * s : 128 * s + 128]
                    v = v * gains_qk[i : i + 1, lanes]
                    v = v * tab[0, s, there] + pltpu.roll(v, 64, 1) * tab[1, s, there]
                    heads[i, s, there, lanes] = v.astype(BF16)
        return carry

    lax.fori_loop(0, LINE, rotate, 0)

    def attend(s, carry):
        mask = posr[s, 0:1, :] <= posc[s][:, 0:1]
        for h in range(2):
            lanes = slice(128 * h, 128 * h + 128)
            scores = dot_rt(heads[0, s, :, lanes], heads[1, s, :, lanes]) * (HD ** -0.5)
            scores = jnp.where(mask, scores, NEGATIVE)
            e = jnp.exp(scores - jnp.max(scores, axis=1, keepdims=True))
            low_p = (e / jnp.sum(e, axis=1, keepdims=True)).astype(BF16)
            probs[s, h] = low_p
            att[s, :, lanes] = dot(low_p, heads[2, s, :, lanes]).astype(BF16)
        return carry

    lax.fori_loop(0, 2, attend, 0)

    pl.when(is_source)(lambda: wo_copy.wait())
    pl.when(is_x)(lambda: wo_send_to(1, low, place.x).wait_recv())
    pl.when(is_y)(lambda: wo_send_to(0, top, place.x).wait_recv())

    ring_g.forward()
    buffers = (term, pair_out, pair_in, keep, mine, line_out, line_in)
    sums = [RowSum(place, h, buffers, (ps, pr, ls, lr)) for h in range(2)]

    def branch_step(s, carry):
        c = place.order(3 - s)
        left = att[:, at128(c * rows)].reshape(2 * rows, cols)
        for h in range(2):
            term[...] = dot(left, wo[:, 1024 * h : 1024 * h + 1024]).reshape(2, rows, 1024)
            sums[h].give(c, s)
        for h in range(2):
            pl.when(s > 0)(lambda h=h: sums[h].pass_on(place.order(4 - s), s + 1))
        return carry

    lax.fori_loop(0, 4, branch_step, 0)
    for h in range(2):
        sums[h].pass_on(z, 3)
    copies = []

    def save(*pairs):
        for a, b in pairs:
            copies.append(pltpu.make_async_copy(a, b, out_sem.at[len(copies)]))
            copies[-1].start()

    save((qkv, o_qkv), (wo, o_wo), (xs, o_x), (raw, o_raw), (heads, o_heads), (probs, o_probs), (att, o_att))
    save((tab, o_tab))
    for h in range(2):
        sums[h].relay(True)
    ring_u.forward()
    for h in range(2):
        sums[h].relay(False)
    for copy in down_copies:
        copy.wait()
    ring_d[0].start()
    branch = jnp.concatenate([sums[h].total() for h in range(2)], axis=1)
    for h in range(2):
        sums[h].finish()
    branch_kept[...] = branch

    def mean_sq(v):
        return jnp.sum(v * v, axis=1, keepdims=True) / width

    mid[...] = tokens[...].astype(F32) + branch * lax.rsqrt(mean_sq(branch) + EPSILON) * gain_attn[...]
    ms[z, k] = mid[...].astype(BF16)
    gather_m = Gather(place, ms, zs.at[1], zr.at[1], cs.at[1], cr.at[1])
    gather_m.start()

    ring_d[0].forward()
    ring_d[1].start()
    ring_g.ready()
    ring_u.ready()

    def expand(s, carry):
        c = place.order(s)
        gather_m.ready(c)
        chunk = ms[c].reshape(2 * rows, width)

        def body(t, inner):
            lanes = at128(t * 256, 256)
            g = dot(chunk, wg[:, lanes])
            u = dot(chunk, wu[:, lanes])
            ga[c, :, lanes] = g.astype(BF16)
            ua[c, :, lanes] = u.astype(BF16)
            hid[c, :, lanes] = (g / (1.0 + jnp.exp(-g)) * u).astype(BF16)
            return inner

        lax.fori_loop(0, 4, body, 0)
        return carry

    def contract(h, first, last):
        def step(s, carry):
            c = place.order(s)
            term[...] = dot(hid[c], wd[h]).reshape(2, rows, 1024)
            sums[h].give(c, s)
            pl.when(s > first)(lambda: sums[h].pass_on(place.order(s - 1), s + 1))
            return carry

        lax.fori_loop(first, last, step, 0)

    def flush(h, last):
        sums[h].pass_on(place.order(last - 1), last - 1)

    save((branch_kept, o_branch), (wg, o_g), (wu, o_u))
    lax.fori_loop(0, 1, expand, 0)
    gather_m.arrive_first()
    lax.fori_loop(1, 2, expand, 0)
    ring_d[0].ready()
    save((wd.at[0], o_dn.at[:, pl.ds(0, 1024)]))
    contract(0, 0, 2)
    gather_m.arrive_second()
    flush(0, 2)
    ring_d[1].forward()
    lax.fori_loop(2, 3, expand, 0)
    contract(0, 2, 3)
    ring_d[1].ready()
    save((wd.at[1], o_dn.at[:, pl.ds(1024, 1024)]))
    flush(0, 3)
    contract(1, 0, 3)
    gather_m.arrive_third()
    flush(1, 3)
    lax.fori_loop(3, 4, expand, 0)
    save((ms, o_m), (ga, o_ga), (ua, o_ua), (hid, o_hid))
    contract(0, 3, 4)
    contract(1, 3, 4)
    for h in range(2):
        flush(h, 4)
    for h in range(2):
        sums[h].relay(False)
    for h in range(2):
        sums[h].relay(True)

    mlp = jnp.concatenate([sums[h].total() for h in range(2)], axis=1)
    for h in range(2):
        sums[h].finish()
    c_m = lax.rsqrt(mean_sq(mlp) + EPSILON)
    gain = gain_mlp[...]
    o_out[...] = (mid[...] + mlp * c_m * gain).astype(BF16)
    dy = cotangent[...].astype(F32)
    gdy = gain * dy
    inner = jnp.sum(mlp * gdy, axis=1, keepdims=True) / width
    o_dmlp[...] = (c_m * gdy - mlp * (c_m * c_m * c_m * inner)).astype(BF16)
    o_gm[...] = jnp.sum(dy * mlp * c_m, axis=0, keepdims=True)

    gather_x.finish()
    gather_m.finish()
    for ring in (ring_qkv, ring_g, ring_u, *ring_d):
        ring.finish()
    for group in swap.values():
        for copy in group:
            copy.wait_send()
    for t in tables:
        t.wait_send()
    pair_sq.wait_send()
    for step in range(1, LINE):
        line_sq(step, z).wait_send()

    @pl.when(is_source)
    def _():
        wo_first(0, place.x).wait_send()
        wo_first(1, place.y).wait_send()

    pl.when(is_x)(lambda: wo_send_to(0, top, place.y).wait_send())
    pl.when(is_y)(lambda: wo_send_to(1, low, place.x).wait_send())

    @pl.when(is_d)
    def _():
        wo_send_to(0, top, place.x).wait_send()
        wo_send_to(1, low, place.y).wait_send()

    for copy in copies:
        copy.wait()


def any_spec():
    return pl.BlockSpec(memory_space=pl.ANY)


def vmem_spec():
    return pl.BlockSpec(memory_space=pltpu.VMEM)


def run_forward(pairs, gain_query, gain_key, gain_attn, gain_mlp, tokens, cotangent, weights):
    shape = jax.ShapeDtypeStruct
    dma = pltpu.SemaphoreType.DMA
    kept = [
        shape((2048, 768), BF16),
        shape((256, 2048), BF16),
        shape((2048, 1024), BF16),
        shape((2048, 1024), BF16),
        shape((1024, 2048), BF16),
        shape((4, 2, 128, 2048), BF16),
        shape((4, 2, 128, 2048), BF16),
        shape((4, 256, 1024), BF16),
        shape((4, 256, 1024), BF16),
        shape((4, 256, 1024), BF16),
        shape((2, 2, 512, 256), F32),
        shape((3, 2, 512, 256), BF16),
        shape((2, 2, 512, 512), BF16),
        shape((2, 512, 256), BF16),
        shape((2, 2, 512, 128), F32),
    ]
    return pl.pallas_call(
        forward_kernel,
        name="forward",
        out_shape=[
            shape((128, 2048), BF16),
            shape((128, 2048), BF16),
            shape((1, 2048), F32),
            shape((128, 2048), F32),
            shape((4, 8, 256), F32),
        ]
        + kept,
        in_specs=[pl.BlockSpec(memory_space=pltpu.SMEM)] + [vmem_spec()] * 6 + [any_spec()] * 7,
        out_specs=[vmem_spec()] * 3 + [any_spec(), vmem_spec()] + [any_spec()] * len(kept),
        scratch_shapes=[pltpu.VMEM((2, 1024, 1024) if i == 4 else k.shape, k.dtype) for i, k in enumerate(kept)]
        + [
            pltpu.VMEM((2, 8, 512), F32),
            pltpu.VMEM((2, 512, 128), F32),
            pltpu.VMEM((2, 128, 1024), F32),
            pltpu.VMEM((2, 4, 128, 1024), BF16),
            pltpu.VMEM((2, 4, 128, 1024), BF16),
            pltpu.VMEM((2, 2, 128, 1024), F32),
            pltpu.VMEM((2, 128, 1024), F32),
            pltpu.VMEM((2, 4, 128, 1024), BF16),
            pltpu.VMEM((2, 4, 128, 1024), BF16),
            pltpu.VMEM((4, 8, 256), F32),
            pltpu.VMEM((4, 8, 256), F32),
            pltpu.VMEM((4, 8, 256), F32),
            pltpu.VMEM((4, 4, 8, 256), F32),
            pltpu.VMEM((128, 2048), F32),
            pltpu.VMEM((2, 256), F32),
            pltpu.VMEM((128, 2048), F32),
            dma((14,)),
            dma((11,)),
            dma((11,)),
            dma((5, 4)),
            dma((5, 4)),
            dma((2,)),
            dma((2,)),
            dma((2, 2, 4)),
            dma((2, 4)),
            dma((2, 4)),
            dma((2, 4)),
            dma((2, 4)),
            dma((2, 4)),
            dma((2, 4)),
            dma((2, 4)),
            dma((4,)),
            dma((4,)),
            dma((4,)),
            dma((5,)),
            dma((len(kept) + 2,)),
        ],
        compiler_params=pltpu.CompilerParams(
            collective_id=0, has_side_effects=True, vmem_limit_bytes=64 * 1024 * 1024
        ),
    )(pairs, gain_query, gain_key, gain_attn, gain_mlp, tokens, cotangent, *weights)


def backward_kernel(
    gain_query, gain_key, gain_attn, d_mlp, h_cot, h_branch, scales, gm_part,
    h_qkv, h_wo, h_g, h_u, h_dn, h_x, h_m, h_ga, h_ua, h_hid, h_raw, h_heads, h_probs, h_att, h_tab,
    o_tok, o_down, o_out, o_gu, o_qkv,
    st_g, rc_g, st_u, rc_u, st_dn, rc_dn, st_qkv, rc_qkv, st_out, rc_out,
    wd, wg, wu, ga, ua, hid, dm, dg, du, ms, db, raw, tab, datt, dy,
    term, pair_out, pair_in, keep, mine, line_out, line_in,
    sq_own, sq_pair, sq_both, sq_line, gn_own, d_mid, stage, stage_d, far_in, gains_qk, cotangent, branch,
    ld, far_sem, zs, zr, cs, cr, ps, pr, ls, lr, as_, ar, in_send, in_recv, st_sem, sum_sem,
    fin_send, fin_recv, fin_loc, al_send, al_recv, al_loc,
):
    place = Place()
    z, f, p, k = place.z, place.f, place.p, place.k
    rows, width, cols = 128, 2048, 256

    def strip_of(chip, plane):
        return (chip % 2 + plane // 2) % 2 + 2 * ((chip // 2 + plane % 2) % 2)

    down_to = (strip_of(p, z), 4 * k + z)
    down_from = (f % 4, 2 * strip_of(z, f % 4) + f // 4)
    down_moves = jnp.logical_or(down_to[0] != z, down_to[1] != f)
    out_to = (z, 4 * k + p)
    out_from = (z, 2 * (f % 4) + f // 4)
    out_moves = out_to[1] != f
    place.barrier(
        [place.d] + [place.cross((z + step) % LINE) for step in range(1, LINE)],
        [(down_moves, down_from), (out_moves, out_from)],
    )

    for i, ref in enumerate((gain_query, gain_key)):
        gains_qk[i : i + 1, :] = ref[:, at128(256 * (2 * z + k), 256)]
    loads = {}

    def load(name, src, dst):
        loads[name] = pltpu.make_async_copy(src, dst, ld.at[len(loads)])
        loads[name].start()

    dm[at128(z * 256 + k * rows)] = d_mlp[...]

    class Rows:
        def __init__(self, ref):
            self.ref = ref

        @property
        def at(self):
            ref = self.ref

            class At:
                def __getitem__(self, key):
                    c, core = key
                    return ref.at[at128(c * 256 + core * rows)]

            return At()

    gather_d = Gather(place, Rows(dm), zs.at[0], zr.at[0], cs.at[0], cr.at[0])
    gather_d.start()
    load("wd", h_dn, wd)
    load("ga", h_ga, ga)
    load("ua", h_ua, ua)
    load("wg", h_g, wg)
    load("wu", h_u, wu)
    load("hid", h_hid, hid)
    load("ms", h_m, ms)
    load("cot", h_cot, cotangent)
    load("branch", h_branch, branch)
    load("raw", h_raw, raw)
    load("tab", h_tab, tab)

    buffers = (term, pair_out, pair_in, keep, mine, line_out, line_in)
    sums = [RowSum(place, h, buffers, (ps, pr, ls, lr)) for h in range(2)]

    def chunk_rows(c):
        return at128(c * 256, 256)

    def expand(s, carry):
        c = place.order(s)
        gather_d.ready(c)
        here = chunk_rows(c)
        grad = dm[here]

        def act(t, inner):
            lanes = at128(t * 256, 256)
            dh = dot_rt(grad, wd[lanes])
            g = ga[here, lanes].astype(F32)
            u = ua[here, lanes].astype(F32)
            sig = 1.0 / (1.0 + jnp.exp(-g))
            dg[here, lanes] = (dh * u * sig * (1.0 + g * (1.0 - sig))).astype(BF16)
            du[here, lanes] = (dh * g * sig).astype(BF16)
            return inner

        lax.fori_loop(0, 4, act, 0)
        return carry

    def contract(s, carry):
        c = place.order(s)
        here = chunk_rows(c)
        left_g, left_u = dg[here], du[here]
        for h in range(2):
            out = slice(1024 * h, 1024 * h + 1024)
            term[...] = (dot_rt(left_g, wg[out]) + dot_rt(left_u, wu[out])).reshape(2, rows, 1024)
            sums[h].give(c, s)
        for h in range(2):
            pl.when(s > 0)(lambda h=h: sums[h].pass_on(place.order(s - 1), s + 1))
        return carry

    for name in ("wd", "ga", "ua"):
        loads[name].wait()
    lax.fori_loop(0, 1, expand, 0)
    for name in ("wg", "wu"):
        loads[name].wait()
    gather_d.arrive_first()
    lax.fori_loop(0, 1, contract, 0)
    for s in (1, 2):
        if s == 2:
            gather_d.arrive_second()
        lax.fori_loop(s, s + 1, expand, 0)
        lax.fori_loop(s, s + 1, contract, 0)
    gather_d.arrive_third()
    lax.fori_loop(3, 4, expand, 0)
    lax.fori_loop(3, 4, contract, 0)
    for h in range(2):
        sums[h].pass_on(place.order(3), 3)
    load("x", h_x, wd)
    load("qkv", h_qkv, wg.at[:, pl.ds(0, 768)])
    load("probs", h_probs, wu.at[:, pl.ds(0, 512)])
    load("qk", h_heads.at[pl.ds(0, 2048)], wu.at[:, pl.ds(512, 256)])
    load("v", h_heads.at[pl.ds(2048, 1024)], wu.at[pl.ds(0, 1024), pl.ds(768, 256)])
    load("att", h_att, wu.at[pl.ds(1024, 1024), pl.ds(768, 256)])

    chips = [place.p_x, place.p_y, place.p_d, p]
    near = [place.x, place.y, place.d]
    GATE, UP, DOWN, QKV, OUT = range(5)
    kinds = {GATE: (st_g, rc_g), UP: (st_u, rc_u), DOWN: (st_dn, rc_dn), QKV: (st_qkv, rc_qkv)}

    def half_of(kind, ref, i, half):
        if kind == DOWN:
            return ref.at[i, :, pl.ds(1024 * half, 1024)]
        return ref.at[i, pl.ds(256 * half, 256)]

    def far_part(kind, half):
        st, rc = kinds[kind]
        return remote(
            half_of(kind, st, 2, half), half_of(kind, rc, 2, half), in_send.at[kind, 2 + half],
            in_recv.at[kind, 2 + half], near[half],
        )

    def near_part(kind, i):
        st, rc = kinds[kind]
        return remote(st.at[i], rc.at[i], in_send.at[kind, i], in_recv.at[kind, i], near[i])

    def put(kind, i, buf, sem):
        wide = 896 if kind == QKV else 1024
        if i < 2:
            half = 1 - i
            far_part(kind, half).wait_recv()
            got = far_in.at[:, pl.ds(0, wide)]
            copy = pltpu.make_async_copy(half_of(kind, kinds[kind][1], 2, half), got, far_sem)
            copy.start()
            copy.wait()
            if kind == DOWN:
                now = (slice(None), slice(1024 * half, 1024 * half + 1024))
            else:
                now = (slice(256 * half, 256 * half + 256), slice(0, wide))
            buf[now] = (buf[now].astype(F32) + far_in[:, 0:wide].astype(F32)).astype(BF16)
        src = buf.at[:, pl.ds(0, 896)] if kind == QKV else buf
        copy = pltpu.make_async_copy(src, kinds[kind][0].at[i], st_sem.at[sem])
        copy.start()
        copy.wait()
        if i == 2:
            far_part(kind, 0).start()
            far_part(kind, 1).start()
        elif i < 2:
            near_part(kind, i).start()

    def feature_rows(ref, chip):
        return jnp.concatenate([ref[:, at128(512 * c + 128 * chip)] for c in range(LINE)], axis=1).T

    def gate_up_part(i):
        left = feature_rows(ms, chips[i])
        for m, right in enumerate((dg, du)):
            for t in range(2):
                lanes = slice(512 * t, 512 * t + 512)
                stage[m, :, lanes] = dot(left, right[:, lanes]).astype(BF16)
            put(m, i, stage.at[m], m)

    def down_part(i):
        left = hid[:, at128(strip_of(chips[i], z) * 256, 256)].T
        for t in range(4):
            lanes = slice(512 * t, 512 * t + 512)
            stage_d[:, lanes] = dot(left, dm[:, lanes]).astype(BF16)
        put(DOWN, i, stage_d, 2)

    loads["ms"].wait()
    loads["hid"].wait()
    gate_up_part(2)
    for h in range(2):
        sums[h].relay(False)
    down_part(2)
    gate_up_part(3)
    for h in range(2):
        sums[h].relay(True)
    gate_up_part(0)
    gate_up_part(1)
    gather_d.finish()

    def mean_of(v):
        return jnp.sum(v, axis=1, keepdims=True) / width

    loads["cot"].wait()
    loads["branch"].wait()
    d_mid[...] = cotangent[...].astype(F32) + jnp.concatenate([sums[h].total() for h in range(2)], axis=1)
    for h in range(2):
        sums[h].finish()
    b = branch[...]
    c_b = lax.rsqrt(mean_of(b * b) + EPSILON)
    gdy = gain_attn[...] * d_mid[...]
    db[at128(z * 256 + k * rows)] = (
        c_b * gdy - b * (c_b * c_b * c_b * mean_of(b * gdy))
    ).astype(BF16)
    gather_b = Gather(place, Rows(db), zs.at[1], zr.at[1], cs.at[1], cr.at[1])
    gather_b.start()
    gn_own[...] = jnp.zeros((8, width), F32)
    gn_own[2:3, :] = jnp.sum(d_mid[...] * b * c_b, axis=0, keepdims=True)
    gn_own[3:4, :] = gm_part[...]

    down_part(3)
    down_part(0)
    down_part(1)
    load("wo", h_wo, stage_d)

    for name in ("wo", "raw", "tab", "x", "qkv", "probs", "qk", "v", "att"):
        loads[name].wait()

    def attended_step(s, carry):
        c = place.order(s)
        gather_b.ready(c)
        part = dot_rt(db[chunk_rows(c)], stage_d[...]).astype(BF16)
        datt[:, at128(c * rows)] = part.reshape(2, rows, cols)
        return carry

    gather_b.arrive_first()
    lax.fori_loop(0, 2, attended_step, 0)
    gather_b.arrive_second()
    lax.fori_loop(2, 3, attended_step, 0)

    def fetch(kind, parts, first):
        copies = [
            pltpu.make_async_copy(src, dst, sum_sem.at[first + n]) for n, (src, dst) in enumerate(parts)
        ]
        for copy in copies:
            copy.start()
        for copy in copies:
            copy.wait()

    def to_owner(kind, src, dst):
        def go(c, core, device):
            return remote(
                src(c, core), dst.at[z, k], al_send.at[kind, c, core], al_recv.at[kind, z, k], device
            )

        def each(action):
            for step in range(1, LINE):
                c = (z + step) % LINE
                action(go(c, k, place.line(c)))
                action(go(c, 1 - k, place.cross(c)))
            action(go(z, 1 - k, place.partner))

        here = pltpu.make_async_copy(src(z, k), dst.at[z, k], al_loc.at[kind])
        each(lambda copy: copy.start())
        here.start()

        def wait():
            here.wait()
            each(lambda copy: copy.wait_send())
            for step in range(LINE):
                c = (z + step) % LINE
                for core in (0, 1):
                    got = remote(
                        src(c, k), dst.at[c, core], al_send.at[kind, c, core], al_recv.at[kind, c, core],
                        place.partner,
                    )
                    if step == 0:
                        pl.when(k != core)(lambda got=got: got.wait_recv())
                    else:
                        got.wait_recv()

        return wait

    waits = []

    def square_sum(kind, buf, other, lanes, dst):
        st, rc = kinds[kind]
        cut = pl.ds(0, lanes)
        near_part(kind, 0).wait_recv()
        near_part(kind, 1).wait_recv()
        fetch(
            kind,
            [
                (st.at[3], buf.at[pl.ds(0, 512), cut]),
                (rc.at[0], buf.at[pl.ds(512, 512), cut]),
                (rc.at[1], other.at[pl.ds(0, 512), cut]),
            ],
            3 * kind,
        )

        def add_up(t, carry):
            there = at128(t * 128)
            acc = buf[there, 0:lanes].astype(F32) + buf[at128(512 + t * 128), 0:lanes].astype(F32)
            buf[there, 0:lanes] = (acc + other[there, 0:lanes].astype(F32)).astype(BF16)
            return carry

        lax.fori_loop(0, 4, add_up, 0)
        waits.append(
            to_owner(
                min(kind, 2), lambda c, core: buf.at[at128(c * 128 + core * 64, 64), cut], dst
            )
        )

    square_sum(GATE, hid, ua, 1024, o_gu.at[0])
    gather_b.arrive_third()
    lax.fori_loop(3, 4, attended_step, 0)

    def attend(s, carry):
        there = at128(s * 512, 512)
        for h in range(2):
            lanes = slice(128 * h, 128 * h + 128)
            more = slice(512 + 128 * h, 640 + 128 * h)
            vals = slice(768 + 128 * h, 896 + 128 * h)
            low_p = wu[at128((2 * s + h) * 512, 512), 0:512]
            grad = datt[s, :, lanes]
            q = wu[there, more]
            key = wu[at128(1024 + s * 512, 512), more]
            value = wu[there, vals]
            d_value = dot_lt(low_p, grad).astype(BF16)
            d_probs = dot_rt(grad, value)
            pr32 = low_p.astype(F32)
            delta = jnp.sum(pr32 * d_probs, axis=1, keepdims=True)
            d_scores = (pr32 * (d_probs - delta)).astype(BF16)
            d_q = dot(d_scores, key) * (HD ** -0.5)
            d_k = dot_lt(d_scores, q) * (HD ** -0.5)
            for i, d in enumerate((d_q, d_k)):
                dy[i, s, :, lanes] = d * tab[0, s] - pltpu.roll(d, 64, 1) * tab[1, s]
            for c in range(LINE):
                ga[c * 256 + s * rows : c * 256 + s * rows + rows, vals.start - 256 : vals.stop - 256] = (
                    d_value[c * rows : c * rows + rows]
                )
        return carry

    for s in range(2):
        attend(s, 0)

    def dots_step(c, carry):
        there = at128(c * rows)
        pick = lax.broadcasted_iota(jnp.int32, (8, cols), 0)
        acc = jnp.zeros((8, 2 * rows), F32)
        for i in range(2):
            part = (raw[i, :, there] * dy[i, :, there]).reshape(2 * rows, cols) * gains_qk[i : i + 1]
            acc = acc + exact((pick == i).astype(F32), part, ((1,), (1,)))
        sq_own[c] = acc
        return carry

    lax.fori_loop(0, LINE, dots_step, 0)
    pair_sq = remote(sq_own, sq_pair, as_.at[0], ar.at[0], place.partner)
    pair_sq.start()
    pair_sq.wait_recv()
    sq_both[...] = sq_own[...] + sq_pair[...]

    def line_sq(step, source):
        return remote(
            sq_both, sq_line.at[source], as_.at[step], ar.at[1 + source], place.line((z + step) % LINE)
        )

    for step in range(1, LINE):
        line_sq(step, z).start()
    square_sum(UP, dg, du, 1024, o_gu.at[1])
    for step in range(1, LINE):
        line_sq(step, (z + step) % LINE).wait_recv()
    sq_line[z] = sq_both[...]

    def normalise(c, gains):
        there = at128(c * rows)
        means = ((sq_line[0, c] + sq_line[1, c]) + (sq_line[2, c] + sq_line[3, c])) / width
        now = scales[c]
        result = []
        for i in range(2):
            pick = (lax.broadcasted_iota(jnp.int32, (8, 128), 0) == i).astype(F32)
            scale = exact(now, pick, ((0,), (0,)))
            mean = exact(means, pick, ((0,), (0,)))
            gain_sum = []
            for h in range(2):
                lanes = slice(128 * h, 128 * h + 128)
                v = raw[i, :, there, lanes].reshape(2 * rows, 128)
                d = dy[i, :, there, lanes].reshape(2 * rows, 128)
                gain_sum.append(jnp.sum(d * v * scale, axis=0, keepdims=True))
                d = scale * gains_qk[i : i + 1, lanes] * d - v * (scale * scale * scale * mean)
                ga[chunk_rows(c), 256 * i + 128 * h : 256 * i + 128 * h + 128] = d.astype(BF16)
            result.append(gains[i] + jnp.concatenate(gain_sum, axis=1))
        return tuple(result)

    start = (jnp.zeros((1, cols), F32), jnp.zeros((1, cols), F32))
    gain_q, gain_k = lax.fori_loop(0, LINE, normalise, start)
    own_cols = at128(cols * (2 * z + k), cols)
    gn_own[0:1, own_cols] = gain_q
    gn_own[1:2, own_cols] = gain_k

    def token_step(s, carry):
        c = place.order(3 - s)
        left = ga[chunk_rows(c), 0:768]
        for h in range(2):
            term[...] = dot_rt(left, wg[1024 * h : 1024 * h + 1024, 0:768]).reshape(2, rows, 1024)
            sums[h].give(c, s)
        for h in range(2):
            pl.when(s > 0)(lambda h=h: sums[h].pass_on(place.order(4 - s), s + 1))
        return carry

    lax.fori_loop(0, 4, token_step, 0)
    for h in range(2):
        sums[h].pass_on(z, 3)

    def qkv_part(i):
        stage[0, :, 0:768] = dot(feature_rows(wd, chips[i]), ga[:, 0:768]).astype(BF16)
        sides = jnp.concatenate([gn_own[:, at128(512 * c + 128 * chips[i])] for c in range(LINE)], axis=1)
        lane = lax.broadcasted_iota(jnp.int32, (8, 128), 1)
        column = (lax.broadcasted_iota(jnp.int32, (8, 128), 0) == lane).astype(F32)
        stage[0, :, 768:896] = exact(sides, column, ((0,), (0,))).astype(BF16)
        put(QKV, i, stage.at[0], 3)

    qkv_part(2)
    for h in range(2):
        sums[h].relay(True)
    qkv_part(3)
    for s in range(2):
        for c in range(LINE):
            ua[c * 256 + s * rows : c * 256 + s * rows + rows, 0:256] = (
                wu[1024 + s * 512 + c * rows : 1024 + s * 512 + c * rows + rows, 768:1024]
            )

    def outer(t, carry):
        lanes = at128(t * 512, 512)
        stage_d[:, lanes] = dot_lt(ua[:, 0:256], db[:, lanes]).astype(BF16)
        return carry

    lax.fori_loop(0, 4, outer, 0)
    copy = pltpu.make_async_copy(stage_d, st_out, st_sem.at[0])
    copy.start()
    copy.wait()

    def out_part(i):
        return remote(
            st_out.at[at128(64 * chips[i], 64)], rc_out.at[i], in_send.at[OUT, i], in_recv.at[OUT, i], near[i]
        )

    qkv_part(0)
    qkv_part(1)
    for i in range(3):
        out_part(i).start()

    for h in range(2):
        sums[h].relay(False)

    near_part(DOWN, 0).wait_recv()
    near_part(DOWN, 1).wait_recv()
    fetch(
        DOWN,
        [
            (st_dn.at[3], ms.at[pl.ds(0, 256)]),
            (rc_dn.at[0], ms.at[pl.ds(256, 256)]),
            (rc_dn.at[1], ms.at[pl.ds(512, 256)]),
        ],
        3 * DOWN,
    )

    def add_down(t, carry):
        lanes = at128(t * 512, 512)
        acc = ms[0:256, lanes].astype(F32) + ms[256:512, lanes].astype(F32)
        dm[0:256, lanes] = (acc + ms[512:768, lanes].astype(F32)).astype(BF16)
        return carry

    lax.fori_loop(0, 4, add_down, 0)
    down_done = dm.at[pl.ds(0, 256)]
    fin_down = remote(down_done, o_down, fin_send.at[0], fin_recv.at[0], down_to)
    keep_down = pltpu.make_async_copy(down_done, o_down, fin_loc.at[0])
    pl.when(down_moves)(lambda: fin_down.start())
    pl.when(jnp.logical_not(down_moves))(lambda: keep_down.start())

    for h in range(2):
        out = slice(1024 * h, 1024 * h + 1024)
        o_tok[:, out] = (d_mid[:, out] + sums[h].total()).astype(BF16)
        sums[h].finish()

    square_sum(QKV, ua, du, 896, o_qkv)

    for i in range(3):
        out_part(i).wait_recv()
    sources = [rc_out.at[0], rc_out.at[1], rc_out.at[2], st_out.at[at128(64 * p, 64)]]
    copies = [
        pltpu.make_async_copy(src, ms.at[pl.ds(64 * i, 64)], sum_sem.at[16 + i])
        for i, src in enumerate(sources)
    ]
    for copy in copies:
        copy.start()
    for copy in copies:
        copy.wait()
    acc = ms[0:64].astype(F32) + ms[64:128].astype(F32)
    acc = acc + ms[128:192].astype(F32) + ms[192:256].astype(F32)
    ms[256:320] = acc.astype(BF16)
    out_done = ms.at[pl.ds(256, 64)]
    fin_out = remote(out_done, o_out, fin_send.at[1], fin_recv.at[1], out_to)
    keep_out = pltpu.make_async_copy(out_done, o_out, fin_loc.at[1])
    pl.when(out_moves)(lambda: fin_out.start())
    pl.when(jnp.logical_not(out_moves))(lambda: keep_out.start())

    gather_b.finish()
    pair_sq.wait_send()
    for step in range(1, LINE):
        line_sq(step, z).wait_send()
    for i in range(3):
        out_part(i).wait_send()
    for kind in kinds:
        for i in range(2):
            near_part(kind, i).wait_send()
            far_part(kind, i).wait_send()
    for wait in waits:
        wait()
    pl.when(down_moves)(lambda: fin_down.wait())
    pl.when(jnp.logical_not(down_moves))(lambda: keep_down.wait())
    pl.when(out_moves)(lambda: fin_out.wait())
    pl.when(jnp.logical_not(out_moves))(lambda: keep_out.wait())


def run_backward(gain_query, gain_key, gain_attn, d_mlp, cotangent, branch, scales, gm_part, kept):
    shape = jax.ShapeDtypeStruct
    dma = pltpu.SemaphoreType.DMA
    flat = [(2048, 768), (256, 2048), (2048, 1024), (2048, 1024), (1024, 2048), (1024, 2048), (1024, 2048),
            (1024, 1024), (1024, 1024), (1024, 1024), None, (3072, 256), (2048, 512), (1024, 256), None]
    kept = [a if s is None else a.reshape(s) for a, s in zip(kept, flat)]
    results = [
        shape((256, 2048), BF16),
        shape((64, 2048), BF16),
        shape((2, 4, 2, 64, 1024), BF16),
        shape((4, 2, 64, 896), BF16),
    ]
    transit = [
        shape((4, 512, 1024), BF16),
        shape((3, 512, 1024), BF16),
        shape((4, 512, 1024), BF16),
        shape((3, 512, 1024), BF16),
        shape((4, 256, 2048), BF16),
        shape((3, 256, 2048), BF16),
        shape((4, 512, 896), BF16),
        shape((3, 512, 896), BF16),
        shape((256, 2048), BF16),
        shape((3, 64, 2048), BF16),
    ]
    wide, square = pltpu.VMEM((1024, 2048), BF16), pltpu.VMEM((1024, 1024), BF16)
    tall = pltpu.VMEM((2048, 1024), BF16)
    rows = pltpu.VMEM((2, 4, 128, 1024), BF16)
    small = pltpu.VMEM((4, 8, 256), F32)
    return pl.pallas_call(
        backward_kernel,
        name="backward",
        out_shape=[shape((128, 2048), BF16)] + results + transit,
        in_specs=[vmem_spec()] * 4 + [any_spec()] * 2 + [vmem_spec()] * 2 + [any_spec()] * len(kept),
        out_specs=[vmem_spec()] + [any_spec()] * (len(results) + len(transit)),
        scratch_shapes=[
            wide, tall, tall, square, square, square, wide, square, square, wide, wide,
            pltpu.VMEM((2, 2, 512, 256), F32),
            pltpu.VMEM((2, 2, 512, 128), F32),
            pltpu.VMEM((2, 512, 256), BF16),
            pltpu.VMEM((2, 2, 512, 256), F32),
            pltpu.VMEM((2, 128, 1024), F32),
            rows,
            rows,
            pltpu.VMEM((2, 2, 128, 1024), F32),
            pltpu.VMEM((2, 128, 1024), F32),
            rows,
            rows,
            small,
            small,
            small,
            pltpu.VMEM((4, 4, 8, 256), F32),
            pltpu.VMEM((8, 2048), F32),
            pltpu.VMEM((128, 2048), F32),
            pltpu.VMEM((2, 512, 1024), BF16),
            pltpu.VMEM((256, 2048), BF16),
            pltpu.VMEM((256, 1024), BF16),
            pltpu.VMEM((2, 256), F32),
            pltpu.VMEM((128, 2048), BF16),
            pltpu.VMEM((128, 2048), F32),
            dma((18,)),
            dma(()),
            dma((2, 2, 4)), dma((2, 4)), dma((2, 4)), dma((2, 4)),
            dma((2, 4)), dma((2, 4)), dma((2, 4)), dma((2, 4)),
            dma((4,)), dma((5,)),
            dma((5, 4)), dma((5, 4)),
            dma((4,)), dma((20,)),
            dma((2,)), dma((2,)), dma((2,)),
            dma((3, 4, 2)), dma((3, 4, 2)), dma((3,)),
        ],
        compiler_params=pltpu.CompilerParams(
            collective_id=1, has_side_effects=True, vmem_limit_bytes=64 * 1024 * 1024
        ),
    )(gain_query, gain_key, gain_attn, d_mlp, cotangent, branch, scales, gm_part, *kept)[:5]


def arrange_kernel(
    gate_up, qkv, out_rows, down, result, d_tokens,
    o_result, o_tokens, o_q, o_k, o_v, o_out, o_gate, o_up, o_down, g_q, g_k, g_attn, g_mlp,
    v_gu, v_qkv, v_out, v_down, v_result, v_tokens, w_gu, w_qkv, w_out, w_down, in_sem, out_sem,
):
    reads = [
        pltpu.make_async_copy(src, dst, in_sem.at[i])
        for i, (src, dst) in enumerate([
            (gate_up, v_gu), (down, v_down), (qkv, v_qkv), (out_rows, v_out), (result, v_result),
            (d_tokens, v_tokens),
        ])
    ]
    for copy in reads:
        copy.start()
    writes = []

    def write(src, dst):
        copy = pltpu.make_async_copy(src, dst, out_sem.at[len(writes)])
        copy.start()
        writes.append(copy)

    reads[0].wait()
    for m, dst in enumerate((o_gate, o_up)):
        for z in range(LINE):
            for k in range(2):
                for q in range(PLANE):
                    at = 1024 * (2 * q + k) + 256 * z
                    w_gu[m, :, at : at + 256] = v_gu[m, z, k, :, 256 * q : 256 * q + 256].astype(F32)
        write(w_gu.at[m], dst)
    reads[1].wait()
    w_down[...] = v_down[...].astype(F32)
    write(w_down, o_down)
    reads[2].wait()
    total = jnp.zeros((64, 128), F32)
    for z in range(LINE):
        for k in range(2):
            at = 256 * (2 * z + k)
            for m in range(3):
                w_qkv[m, :, at : at + 256] = v_qkv[z, k, :, 256 * m : 256 * m + 256].astype(F32)
            total = total + v_qkv[z, k, :, 768:896].astype(F32)
    for m, dst in enumerate((o_q, o_k, o_v)):
        write(w_qkv.at[m], dst)
    lane = lax.broadcasted_iota(jnp.int32, (8, 128), 1)
    pick = (lax.broadcasted_iota(jnp.int32, (8, 128), 0) == lane).astype(F32)
    gains = exact(pick, total, ((1,), (1,)))
    for i, ref in enumerate((g_q, g_k, g_attn, g_mlp)):
        ref[...] = gains[i : i + 1]
    reads[3].wait()
    w_out[...] = v_out[...].astype(F32)
    write(w_out, o_out)
    reads[4].wait()
    write(v_result, o_result)
    reads[5].wait()
    write(v_tokens, o_tokens)
    for copy in writes:
        copy.wait()


def run_arrange(*arrays):
    shape = jax.ShapeDtypeStruct
    square = shape((64, 2048), F32)
    return pl.pallas_call(
        arrange_kernel,
        name="arrange",
        out_shape=[shape((128, 2048), BF16)] * 2 + [square] * 4 + [shape((64, 8192), F32)] * 2 + [shape((256, 2048), F32)]
        + [shape((1, 64), F32)] * 4,
        in_specs=[any_spec()] * 6,
        out_specs=[any_spec()] * 9 + [vmem_spec()] * 4,
        scratch_shapes=[pltpu.VMEM(a.shape, a.dtype) for a in arrays]
        + [
            pltpu.VMEM((2, 64, 8192), F32),
            pltpu.VMEM((3, 64, 2048), F32),
            pltpu.VMEM((64, 2048), F32),
            pltpu.VMEM((256, 2048), F32),
            pltpu.SemaphoreType.DMA((6,)),
            pltpu.SemaphoreType.DMA((9,)),
        ],
        compiler_params=pltpu.CompilerParams(vmem_limit_bytes=64 * 1024 * 1024),
    )(*arrays)


def shards_kernels(tokens, block_pairs, w_query, w_key, w_value, w_out, w_gate, w_up, w_down,
                   gain_query, gain_key, gain_attn, gain_mlp, cotangent):
    gains = [gain_query[None], gain_key[None], gain_attn[None]]
    out, d_mlp, gm_part, branch, scales, *kept = run_forward(
        block_pairs, *gains, gain_mlp[None], tokens[0], cotangent[0],
        (w_query, w_key, w_value, w_out, w_gate, w_up, w_down),
    )
    d_tokens, down, out_rows, gate_up, qkv = run_backward(
        *gains, d_mlp, cotangent[0], branch, scales, gm_part, kept
    )
    out, d_tokens, *grads = run_arrange(gate_up, qkv, out_rows, down, out, d_tokens)
    return (out[None], d_tokens[None], *grads[:7], *[g[0] for g in grads[7:]])


def shards(*arrays):
    tokens, w_query, w_down = arrays[0], arrays[2], arrays[8]
    here = (lax.axis_size("ctx"), lax.axis_size("fsdp"), tokens.shape, w_query.shape, w_down.shape)
    if here == (LINE, 2 * PLANE, (1, 128, 2048), (256, 2048), (1024, 2048)):
        return shards_kernels(*arrays)
    return shards_general(*arrays)


def solution(mesh):
    in_specs = (
        P("fsdp", "ctx", None),
        P("fsdp", None),
        P("fsdp", None),
        P("fsdp", None),
        P("fsdp", None),
        P("fsdp", None),
        P("fsdp", None),
        P("fsdp", None),
        P("fsdp", None),
        P(),
        P(),
        P(),
        P(),
        P("fsdp", "ctx", None),
    )
    out_specs = (
        P("fsdp", "ctx", None),
        P("fsdp", "ctx", None),
        P(("ctx", "fsdp"), None),
        P(("ctx", "fsdp"), None),
        P(("ctx", "fsdp"), None),
        P(("ctx", "fsdp"), None),
        P(("ctx", "fsdp"), None),
        P(("ctx", "fsdp"), None),
        P(("ctx", "fsdp"), None),
        P(("ctx", "fsdp")),
        P(("ctx", "fsdp")),
        P(("ctx", "fsdp")),
        P(("ctx", "fsdp")),
    )
    return jax.shard_map(shards, mesh=mesh, in_specs=in_specs, out_specs=out_specs, check_vma=False)
```
